32 devices in a mesh: seg: 8 (over z, x), tp: 4 (over y, core).
Axes of the slice: x: 2, y: 2, z: 4, core: 2. Of those that a mesh axis runs over, the one named last changes fastest.
Arguments:
- tokens: bfloat16 [2, 8, 240, 768], P(None, 'seg', 'tp'), may hold values from -6 to 6
- mem_tokens: bfloat16 [16, 768], P('tp'), may hold values from -6 to 6
- segno: int32 [2, 8], P(None, 'seg'), may hold values from 0 to 7, as said below
- gains: bfloat16 [2, 3, 768], replicated, may hold values from 0.5 to 1.5
- shifts: bfloat16 [2, 3, 768], replicated, may hold values from -1 to 1
- assoc: bfloat16 [2, 768, 768], replicated, may hold values from -0.4375 to 0.4375
- w_write: bfloat16 [2, 768, 768], P(None, None, 'tp'), may hold values from -0.875 to 0.875
- w_qkv: bfloat16 [2, 768, 2304], P(None, None, 'tp'), may hold values from -0.21875 to 0.21875
- b_query_value: bfloat16 [2, 1536], P(None, 'tp'), may hold values from -2 to 2
- w_out: bfloat16 [2, 768, 768], P(None, 'tp'), may hold values from -0.4375 to 0.4375
- out_bias: bfloat16 [2, 2, 768], replicated, may hold values from -1 to 1
- w_fc: bfloat16 [2, 768, 3072], P(None, None, 'tp'), may hold values from -0.21875 to 0.21875
- b_fc: bfloat16 [2, 3072], P(None, 'tp'), may hold values from -2 to 2
- w_proj: bfloat16 [2, 3072, 768], P(None, 'tp'), may hold values from -0.109375 to 0.109375
- cot_tokens: bfloat16 [2, 8, 240, 768], P(None, 'seg', 'tp'), may hold values from -6 to 6
- cot_memory: bfloat16 [2, 8, 16, 768], P(None, 'seg', 'tp'), may hold values from -6 to 6
Outputs:
- out_tokens: bfloat16 [2, 8, 240, 768], P(None, 'seg', 'tp')
- out_memory: bfloat16 [2, 8, 16, 768], P(None, 'seg', 'tp')
- grad_tokens: float32 [2, 8, 240, 768], P(None, 'seg', 'tp')
- grad_mem_tokens: float32 [16, 768], P(None, ('seg', 'tp'))
- grad_gains: float32 [2, 3, 768], P(None, None, ('seg', 'tp'))
- grad_shifts: float32 [2, 3, 768], P(None, None, ('seg', 'tp'))
- grad_assoc: float32 [2, 768, 768], P(None, None, ('seg', 'tp'))
- grad_write: float32 [2, 768, 768], P(None, 'seg', 'tp')
- grad_qkv: float32 [2, 768, 2304], P(None, 'seg', 'tp')
- grad_query_value: float32 [2, 1536], P(None, ('seg', 'tp'))
- grad_out: float32 [2, 768, 768], P(None, 'tp', 'seg')
- grad_out_bias: float32 [2, 2, 768], P(None, None, ('seg', 'tp'))
- grad_fc: float32 [2, 768, 3072], P(None, 'seg', 'tp')
- grad_b_fc: float32 [2, 3072], P(None, ('seg', 'tp'))
- grad_proj: float32 [2, 3072, 768], P(None, 'tp', 'seg')
The draws below stay inside these ranges and needn't reach their ends.
Inputs may be any that keep to these rules, and one draw needn't show every extreme that they name: `segno`: 0 at an item's first segment and one more at each later segment of the same micro-batch; in each draw one micro-batch holds a single item of all 8 segments.
All inputs are finite; a program needn't handle non-finite values.
Results may differ from the reference program's by a relative error of at most 0.02.
Values may be sent and summed in bfloat16 or wider, within the bound.
No kernel may reach another device: no remote copies, remote signals or barrier semaphores. Data moves between devices by JAX's collectives and lax.ppermute only.
A program may use at most 512 MiB of HBM per device.

```python
import jax
import jax.numpy as jnp
from jax import lax

D = 768
HEADS = 12
HD = 64
FF = 3072
KD = 384
NMEM = 16
LAYERS = 2
L = 240
MB = 2
PHI = 2304
SEGS = 8


def draw_segno(key, part):
    key = jax.random.fold_in(key, 7)
    first_key, second_key = jax.random.split(key)
    starts = jax.random.randint(first_key, (MB, SEGS), 0, 4) == 0
    longest = jax.random.randint(second_key, (), 0, MB)
    batch_index = jnp.arange(MB)[:, None]
    positions = jnp.arange(SEGS)[None, :]
    starts = jnp.where(batch_index == longest, False, starts) | (positions == 0)
    firsts = lax.cummax(jnp.where(starts, positions, 0), axis=1)
    return (positions - firsts).astype(jnp.int32)


def shard_levels(own_key, shape, shards, low, largest):
    def one(dim, blocks):
        draws = jax.random.uniform(jax.random.fold_in(jax.random.fold_in(own_key, 6), dim), (blocks,), jnp.float32, low / len(shards), largest / len(shards))
        return jnp.repeat(jnp.exp(draws), shape[dim] // blocks).reshape((-1,) + (1,) * (len(shape) - dim - 1))

    level = one(*shards[0])
    for cut in shards[1:]:
        level = level * one(*cut)
    return level


def noise(key, extent, width, most, shards=(), held_as=jnp.bfloat16):
    array = width * jax.random.normal(key, extent, jnp.float32)
    if shards:
        array = array * shard_levels(key, extent, shards, -0.22, 0.18)
    return jnp.clip(array, -most, most).astype(held_as)


def setup_inputs(seed: int = 0) -> dict:
    seeds = jax.random.split(jax.random.key(seed), 17)
    return {
        "tokens": noise(seeds[0], (MB, SEGS, L, D), 1.0, 6.0, ((1, 8), (2, 4))),
        "mem_tokens": noise(seeds[1], (NMEM, D), 1.0, 6.0, ((0, 4),)),
        "segno": draw_segno(jax.random.fold_in(seeds[16], 71), 0),
        "gains": jnp.clip(1.0 + 0.1 * jax.random.normal(seeds[3], (LAYERS, 3, D), jnp.float32), 0.5, 1.5).astype(jnp.bfloat16),
        "shifts": noise(seeds[4], (LAYERS, 3, D), 0.2, 1.0),
        "assoc": noise(seeds[5], (LAYERS, 2 * KD, D), (D // 4) ** -0.5, 0.4375),
        "w_write": noise(seeds[6], (LAYERS, D, D), (D // 16) ** -0.5, 0.875, ((2, 4),)),
        "w_qkv": noise(seeds[7], (LAYERS, D, 3 * D), D ** -0.5, 0.21875, ((2, 4),)),
        "b_query_value": noise(seeds[8], (LAYERS, 2 * D), 0.3, 2.0, ((1, 4),)),
        "w_out": noise(seeds[9], (LAYERS, D, D), (D // 4) ** -0.5, 0.4375, ((1, 4),)),
        "out_bias": noise(seeds[10], (LAYERS, 2, D), 0.2, 1.0),
        "w_fc": noise(seeds[11], (LAYERS, D, FF), D ** -0.5, 0.21875, ((2, 4),)),
        "b_fc": noise(seeds[12], (LAYERS, FF), 0.3, 2.0, ((1, 4),)),
        "w_proj": noise(seeds[13], (LAYERS, FF, D), FF ** -0.5, 0.109375, ((1, 4),)),
        "cot_tokens": noise(seeds[14], (MB, SEGS, L, D), 1.0, 6.0, ((1, 8), (2, 4))),
        "cot_memory": noise(seeds[15], (MB, SEGS, NMEM, D), 1.0, 6.0, ((1, 8), (2, 4))),
    }


@jax.custom_vjp
def low(v):
    return lax.optimization_barrier(v.astype(jnp.bfloat16)).astype(jnp.float32)

@jax.custom_vjp
def low_back(v):
    return v

def low_keep(v):
    return (low(v), None)

def low_pass(kept, grad):
    return (grad,)

def back_keep(v):
    return (v, None)

def back_low(kept, grad):
    return (low(grad),)
low.defvjp(low_keep, low_pass)
low_back.defvjp(back_keep, back_low)

def highdot(first_op, second_op):
    return jnp.dot(first_op, second_op, precision=lax.Precision.HIGHEST)

def norm_rows(stream, gain, shift):
    average = lax.optimization_barrier(jnp.mean(stream, axis=-1, keepdims=True))
    centred = stream - average
    variance = lax.optimization_barrier(jnp.mean(centred * centred, axis=-1, keepdims=True))
    return centred * lax.rsqrt(variance + 1e-05) * gain + shift

def features(keys_in):
    paired = jnp.concatenate([jax.nn.softplus(keys_in), jax.nn.softplus(-keys_in)], axis=-1)
    return jnp.concatenate([paired * jnp.roll(paired, -offset, axis=-1) for offset in (1, 2, 3)], axis=-1)

def qv_bias(bias):
    halves = bias.reshape(HEADS, 2, HD)
    return jnp.stack([halves[:, 0], jnp.zeros_like(halves[:, 0]), halves[:, 1]], axis=1).reshape(3 * D)

def layer(stream, state_a, state_z, retain, weights):
    gain, shift, assoc, w_write, w_qkv, b_qv, w_out, out_bias, w_fc, b_fc, w_proj = weights
    row_count = stream.shape[0]
    normed = low(norm_rows(stream, gain[0], shift[0]))
    read_keys = low(low_back(highdot(normed, assoc[:KD].T)))
    feat_q = features(read_keys)
    used_a = retain * state_a
    used_z = retain * state_z
    numer = low_back(highdot(low(feat_q), low(used_a)))
    denom = highdot(feat_q, used_z) + 1.0
    read = low(numer / denom[:, None])
    tail = normed[row_count - NMEM:]
    feat_k = low(features(highdot(tail, assoc[KD:].T)))
    write_vals = low(low_back(highdot(tail, w_write)))
    next_a = used_a + highdot(feat_k.T, write_vals)
    next_z = used_z + lax.optimization_barrier(jnp.sum(feat_k, axis=0))
    mid = stream + read
    normed = low(norm_rows(mid, gain[1], shift[1]))
    packed = low(low_back(highdot(normed, w_qkv) + qv_bias(b_qv))).reshape(row_count, HEADS, 3, HD)
    queries, keys_head, values = (packed[:, :, 0], packed[:, :, 1], packed[:, :, 2])
    scores = low_back(jnp.einsum('qhd,khd->hqk', queries, keys_head, precision=lax.Precision.HIGHEST) * 0.125)
    positions = jnp.arange(row_count)
    scores = jnp.where(positions[None, :, None] >= positions[None, None, :], scores, -1e+30)
    probs = jax.nn.softmax(scores, axis=-1)
    mixed = low(low_back(jnp.einsum('hqk,khd->qhd', low(probs), values, precision=lax.Precision.HIGHEST)))
    after = mid + low_back(highdot(mixed.reshape(row_count, D), w_out)) + out_bias[0]
    normed = low(norm_rows(after, gain[2], shift[2]))
    hidden = low(jax.nn.gelu(low_back(highdot(normed, w_fc) + b_fc), approximate=True))
    result = after + low_back(highdot(hidden, w_proj)) + out_bias[1]
    return (result, next_a, next_z)

def forward(tokens, mem_tokens, segno, *params):

    def column(arrays):
        batch_tokens, batch_numbers = arrays

        def advance(carried, element):
            seg_tokens, number = element
            retain = (number != 0).astype(jnp.float32)
            stream = jnp.concatenate([mem_tokens, seg_tokens], axis=0)
            states = []
            for layer_id in range(LAYERS):
                weights = tuple((weight[layer_id] for weight in params))
                stream, new_a, new_z = layer(stream, carried[2 * layer_id], carried[2 * layer_id + 1], retain, weights)
                states = states + [new_a, new_z]
            return (tuple(states), stream)
        zero_a = jnp.zeros((PHI, D), jnp.float32)
        zero_z = jnp.zeros((PHI,), jnp.float32)
        start = tuple([zero_a, zero_z] * LAYERS)
        _, streams = lax.scan(jax.checkpoint(advance), start, (batch_tokens, batch_numbers))
        return streams
    streams = lax.map(column, (tokens, segno))
    return (streams[:, :, NMEM:], streams[:, :, :NMEM])

def reference(tokens, mem_tokens, segno, gains, shifts, assoc, w_write, w_qkv, b_query_value, w_out, out_bias, w_fc, b_fc, w_proj, cot_tokens, cot_memory):
    floats = [arr.astype(jnp.float32) for arr in (tokens, mem_tokens, gains, shifts, assoc, w_write, w_qkv, b_query_value, w_out, out_bias, w_fc, b_fc, w_proj)]

    def wrapped(*arrays):
        return forward(arrays[0], arrays[1], segno, *arrays[2:])
    results, pull = jax.vjp(wrapped, *floats)
    grads = pull((cot_tokens.astype(jnp.float32), cot_memory.astype(jnp.float32)))
    return (results[0].astype(jnp.bfloat16), results[1].astype(jnp.bfloat16), grads[0], grads[1], grads[2], grads[3], grads[4], grads[5], grads[6], grads[7], grads[8], grads[9], grads[10], grads[11], grads[12])
```

```python
import functools

import jax
import jax.numpy as jnp
from jax import lax
from jax.experimental import pallas as pl
from jax.experimental.pallas import tpu as pltpu
from jax.sharding import PartitionSpec as P

D = 768
HD = 64
NMEM = 16
LAYERS = 2
BF = jnp.bfloat16
F32 = jnp.float32
KERNELS = True


def value_of(item):
    return item[0][item[1]] if isinstance(item, tuple) else item


def phase(body, outs, *items):
    if not KERNELS:
        return body(*[value_of(item) for item in items])
    arrays, specs = [], []
    for item in items:
        if isinstance(item, tuple):
            array, layer = item
            rest = array.shape[1:]
            arrays.append(array)
            specs.append(
                pl.BlockSpec((None,) + rest, functools.partial(lambda l, n, i: (l,) + (0,) * n, layer, len(rest)))
            )
        else:
            arrays.append(item)
            specs.append(pl.BlockSpec(item.shape, functools.partial(lambda n, i: (0,) * n, item.ndim)))

    def kernel(*refs):
        results = body(*[r[...] for r in refs[: len(arrays)]])
        for ref, result in zip(refs[len(arrays) :], results):
            ref[...] = result

    shapes = [jax.ShapeDtypeStruct(s, t) for s, t in outs]
    return pl.pallas_call(
        kernel,
        grid=(1,),
        out_shape=shapes,
        in_specs=specs,
        out_specs=[pl.BlockSpec(s, functools.partial(lambda n, i: (0,) * n, len(s))) for s, _ in outs],
        compiler_params=pltpu.CompilerParams(vmem_limit_bytes=48 * 1024 * 1024),
        name=body.__name__,
    )(*arrays)


def wide(v):
    return v.astype(F32)


def dot(a, b):
    return lax.dot_general(a, b, (((1,), (0,)), ((), ())), preferred_element_type=F32)


def dot_nt(a, b):
    return lax.dot_general(a, b, (((1,), (1,)), ((), ())), preferred_element_type=F32)


def dot_tn(a, b):
    return lax.dot_general(a, b, (((0,), (0,)), ((), ())), preferred_element_type=F32)


def turn(v, by):
    size = v.shape[1]
    if KERNELS:
        return pltpu.roll(v, (-by) % size, 1)
    return jnp.roll(v, -by, axis=1)


def norm_parts(rows):
    centred = rows - jnp.mean(rows, axis=-1, keepdims=True)
    rstd = lax.rsqrt(jnp.mean(centred * centred, axis=-1, keepdims=True) + 1e-05)
    return centred * rstd, rstd


def norm_rows(rows, gain, shift):
    return norm_parts(rows)[0] * wide(gain) + wide(shift)


def norm_back(rows, gain, grad):
    hat, rstd = norm_parts(rows)
    d_hat = grad * wide(gain)
    d_rows = rstd * (
        d_hat
        - jnp.mean(d_hat, axis=-1, keepdims=True)
        - hat * jnp.mean(d_hat * hat, axis=-1, keepdims=True)
    )
    return d_rows, jnp.sum(grad * hat, axis=0, keepdims=True), jnp.sum(grad, axis=0, keepdims=True)


def paired(v):
    rest = jnp.log1p(jnp.exp(-jnp.abs(v)))
    return jnp.concatenate([jnp.maximum(v, 0.0) + rest, jnp.maximum(-v, 0.0) + rest], axis=1)


def features(v):
    c = paired(v)
    return jnp.concatenate([c * turn(c, 1), c * turn(c, 2), c * turn(c, 3)], axis=1)


def features_back(v, grad):
    c = paired(v)
    size = c.shape[1]
    d_c = jnp.zeros_like(c)
    for k in (1, 2, 3):
        part = grad[:, (k - 1) * size : k * size]
        d_c = d_c + part * turn(c, k) + turn(part * c, -k)
    half = v.shape[1]
    up = 1.0 / (1.0 + jnp.exp(-v))
    return d_c[:, :half] * up - d_c[:, half:] * (1.0 - up)


def write_keys(x, gains, shifts, assoc):
    normed = norm_rows(x, gains[0:1], shifts[0:1]).astype(BF)
    return (normed,)


def read_features(normed, assoc):
    keys = dot_nt(normed, assoc[: assoc.shape[0] // 2]).astype(BF)
    return (keys, features(wide(keys)).astype(BF))


def write_scores(tails, assoc, feat_q, mask):
    tail_keys = dot_nt(tails, assoc[assoc.shape[0] // 2 :])
    feat_k = features(tail_keys).astype(BF)
    scores = dot_nt(feat_q, feat_k) * mask
    denom = jnp.sum(scores, axis=1, keepdims=True) + 1.0
    return (tail_keys, feat_k, scores.astype(BF), jnp.broadcast_to(denom, mask.shape))


def write_values(tails, w_write):
    return (dot(tails, w_write).astype(BF),)


def read_memory(x, scores, values, denom, gains, shifts):
    read = (dot(scores, values) / denom[:, 0:1]).astype(BF)
    mid = x + wide(read)
    return (mid, norm_rows(mid, gains[1:2], shifts[1:2]).astype(BF))


def head_parts(packed, head):
    at = 3 * HD * head
    return packed[:, at : at + HD], packed[:, at + HD : at + 2 * HD], packed[:, at + 2 * HD : at + 3 * HD]


def head_probs(queries, keys, seen):
    scores = jnp.where(seen, dot_nt(queries, keys) * 0.125, -1e30)
    weights = jnp.exp(scores - jnp.max(scores, axis=1, keepdims=True))
    return weights / jnp.sum(weights, axis=1, keepdims=True)


def seen_rows(pos_rows, pos_cols):
    return pos_rows[:, 0:1] >= pos_cols[0:1, :]


def attention(own, other, w0, w1, bias0, bias1, o0, o1, pos_rows, pos_cols):
    rows = jnp.concatenate([own, other], axis=0)
    seen = seen_rows(pos_rows, pos_cols)
    half = own.shape[0]
    total, saved = 0.0, []
    for w, bias, o in ((w0, bias0, o0), (w1, bias1, o1)):
        packed = (dot(rows, w) + bias).astype(BF)
        mixed = []
        for head in range(packed.shape[1] // (3 * HD)):
            queries, keys, values = head_parts(packed, head)
            probs = head_probs(queries, keys, seen)
            mixed.append(dot(probs.astype(BF), values).astype(BF))
        mixed = jnp.concatenate(mixed, axis=1)
        total = total + dot(mixed, o)
        saved += [packed, mixed]
    return (total[:half], total[half:].astype(BF), saved[0], saved[2], saved[1], saved[3])


def after_attention(mid, part, arrived, bias, gains, shifts):
    after = mid + part + wide(arrived) + wide(bias[0:1])
    return (after, norm_rows(after, gains[2:3], shifts[2:3]).astype(BF))


def gelu_both(v):
    inner = 0.7978845608028654 * (v + 0.044715 * v * v * v)
    t = jnp.tanh(inner)
    slope = 0.5 * (1.0 + t) + 0.5 * v * (1.0 - t * t) * 0.7978845608028654 * (1.0 + 3 * 0.044715 * v * v)
    return 0.5 * v * (1.0 + t), slope


def feed_forward(own, other, w0, w1, bias0, bias1, p0, p1):
    rows = jnp.concatenate([own, other], axis=0)
    half = own.shape[0]
    total, hiddens, slopes = 0.0, [], []
    for w, bias, p in ((w0, bias0, p0), (w1, bias1, p1)):
        hidden, slope = gelu_both(dot(rows, w) + bias)
        hidden = hidden.astype(BF)
        total = total + dot(hidden, p)
        hiddens.append(hidden)
        slopes.append(slope.astype(BF))
    return (total[:half], total[half:].astype(BF), *hiddens, *slopes)


def after_feed(after, part, arrived, bias, next_gains, next_shifts):
    x = after + part + wide(arrived) + wide(bias[1:2])
    return (x, norm_rows(x, next_gains[0:1], next_shifts[0:1]).astype(BF))


def feed_back(own, other, w0, w1, p0, p1, slope0, slope1):
    grads = jnp.concatenate([own, other], axis=0)
    half = own.shape[0]
    total, saved = 0.0, []
    for w, p, slope in ((w0, p0, slope0), (w1, p1, slope1)):
        d_pre = (dot_nt(grads, p) * wide(slope)).astype(BF)
        total = total + dot_nt(d_pre, w)
        saved.append(d_pre)
    return (total[:half], total[half:].astype(BF), *saved)


def after_feed_back(grad, part, arrived, after, gains):
    d_rows, d_gain, d_shift = norm_back(after, gains[2:3], part + wide(arrived))
    d_after = grad + d_rows
    d_bias = jnp.sum(grad, axis=0, keepdims=True)
    return (d_after, d_after.astype(BF), d_gain, d_shift, d_bias)


def attention_back(own, other, w0, w1, o0, o1, packed0, packed1, pos_rows, pos_cols):
    grads = jnp.concatenate([own, other], axis=0)
    seen = seen_rows(pos_rows, pos_cols)
    half = own.shape[0]
    total, saved = 0.0, []
    for w, o, packed in ((w0, o0, packed0), (w1, o1, packed1)):
        d_mixed = dot_nt(grads, o).astype(BF)
        pieces = []
        for head in range(packed.shape[1] // (3 * HD)):
            queries, keys, values = head_parts(packed, head)
            dm = d_mixed[:, HD * head : HD * (head + 1)]
            probs = head_probs(queries, keys, seen)
            d_probs = dot_nt(dm, values)
            d_values = dot_tn(probs.astype(BF), dm)
            d_scores = (probs * (d_probs - jnp.sum(d_probs * probs, axis=1, keepdims=True))).astype(BF)
            pieces += [dot(d_scores, keys) * 0.125, dot_tn(d_scores, queries) * 0.125, d_values]
        d_packed = jnp.concatenate(pieces, axis=1).astype(BF)
        total = total + dot_nt(d_packed, w)
        saved.append(d_packed)
    return (total[:half], total[half:].astype(BF), *saved)


def after_attention_back(d_after, part, arrived, mid, gains, scores, values, denom, mask, feat_q, tail_keys):
    d_rows, d_gain, d_shift = norm_back(mid, gains[1:2], part + wide(arrived))
    d_mid = d_after + d_rows
    d_bias = jnp.sum(d_after, axis=0, keepdims=True)
    scale = 1.0 / denom[:, 0:1]
    d_numer = (d_mid * scale).astype(BF)
    d_denom = -jnp.sum(d_mid * dot(scores, values), axis=1, keepdims=True) * scale * scale
    d_scores = ((dot_nt(d_numer, values) + d_denom) * mask).astype(BF)
    d_keys = features_back(tail_keys, dot_tn(d_scores, feat_q))
    d_values = dot_tn(scores, d_numer)
    return (d_mid, d_scores, d_keys, d_values, d_gain, d_shift, d_bias)


def read_back(d_scores, feat_k, keys, assoc):
    d_keys = features_back(wide(keys), dot(d_scores, feat_k)).astype(BF)
    return (d_keys, dot(d_keys, assoc[: assoc.shape[0] // 2]))


def tail_back(d_keys, d_values, assoc, w_write):
    d_tail = dot(d_keys.astype(BF), assoc[assoc.shape[0] // 2 :]) + dot_nt(d_values.astype(BF), w_write)
    return (d_tail, d_values.astype(BF))


def layer_end_back(d_mid, d_norm, d_tail, x, gains):
    rows = d_norm.shape[0]
    d_norm = jnp.concatenate([d_norm[: rows - NMEM], d_norm[rows - NMEM :] + d_tail], axis=0)
    d_rows, d_gain, d_shift = norm_back(x, gains[0:1], d_norm)
    d_x = d_mid + d_rows
    return (d_x, d_x.astype(BF), d_gain, d_shift)


def two_products(a0, a1, a2, b0, b1):
    own = dot_tn(a0, b0) + dot_tn(jnp.concatenate([a1, a2], axis=0), b1)
    return (own.astype(BF),)


def toward(x, axis, bit):
    size = lax.axis_size(axis)
    return lax.ppermute(x, axis, [(i, i ^ bit) for i in range(size)])


def core_swap(x):
    return toward(x, "tp", 1)


def half_swap(x):
    return toward(x, "tp", 2)


def gather_segments(x):
    size = lax.axis_size("seg")
    me = lax.axis_index("seg")
    odd = (me & 1) == 1
    near = toward(x, "seg", 1)
    pair = jnp.where(odd, jnp.concatenate([near, x]), jnp.concatenate([x, near]))
    if size > 8:
        whole = lax.all_gather(x, "seg", axis=0, tiled=True)
        return whole
    whole = jnp.zeros((size // 2,) + pair.shape, x.dtype)
    for far in range(0, size, 2):
        other = toward(pair, "seg", far) if far else pair
        whole = lax.dynamic_update_slice(whole, other[None], ((me ^ far) // 2, 0, 0))
    return whole.reshape(-1, x.shape[1])


def scatter_segments(x):
    size = lax.axis_size("seg")
    blocks = lax.all_to_all(x.reshape(size, -1, x.shape[1]), "seg", 0, 0, tiled=True)
    return jnp.sum(wide(blocks), axis=0)


def sum_over_segments(x):
    size = lax.axis_size("seg")
    me = lax.axis_index("seg")
    bit = 1
    while bit < size:
        count = x.shape[0]
        halves = x.reshape((count // 2, 2) + x.shape[1:])
        mine = (me & bit) // bit
        keep = lax.dynamic_index_in_dim(halves, mine, 1, keepdims=False)
        send = lax.dynamic_index_in_dim(halves, 1 - mine, 1, keepdims=False)
        total = wide(keep) + wide(toward(send, "seg", bit))
        bit *= 2
        x = total if bit >= size else total.astype(BF)
    return x[0]


def sum_over_all(x):
    for bit in (1, 2):
        x = x + toward(x, "tp", bit)
    bit = 1
    while bit < lax.axis_size("seg"):
        x = x + toward(x, "seg", bit)
        bit *= 2
    return x


def fetch_other(w):
    odd = lax.axis_index("seg") & 1
    rows = w.shape[0] // 2
    part = half_swap(lax.dynamic_slice_in_dim(w, odd * rows, rows, axis=0))
    rest = toward(part, "seg", 1)
    first = odd == 0
    return jnp.where(
        first, jnp.concatenate([part, rest]), jnp.concatenate([rest, part])
    )


def local(
    tokens,
    mem_tokens,
    segno,
    gains,
    shifts,
    assoc,
    w_write,
    w_qkv,
    b_query_value,
    w_out,
    out_bias,
    w_fc,
    b_fc,
    w_proj,
    cot_tokens,
    cot_memory,
):
    mem_rows = mem_tokens.shape[0]
    block_rows = mem_rows + tokens.shape[2]
    own_rows = 2 * block_rows
    all_rows = 2 * own_rows
    segs = lax.axis_size("seg")
    me = lax.axis_index("seg")
    tp = lax.axis_index("tp")
    half, core = tp // 2, tp % 2
    slots = segs * NMEM
    key_dim = assoc.shape[1] // 2
    heads = w_qkv.shape[2] // (3 * HD)
    units = w_fc.shape[2]
    phi = 6 * key_dim

    def pick(pair, which):
        return lax.dynamic_index_in_dim(pair, which, 0, keepdims=False)

    def in_order(own, other):
        return jnp.where(half == 0, jnp.concatenate([own, other]), jnp.concatenate([other, own]))

    both = jnp.concatenate([jnp.broadcast_to(mem_tokens, (2,) + mem_tokens.shape), tokens[:, 0]], axis=1)
    x = wide(in_order(pick(both, half), half_swap(pick(both, 1 - half))))
    cots = jnp.concatenate([cot_memory[:, 0], cot_tokens[:, 0]], axis=1)

    bias_rows = jnp.concatenate([b_query_value, b_fc], axis=1)
    other_bias = half_swap(bias_rows)
    weights = []
    for l in range(LAYERS):
        other_write = fetch_other(w_write[l])
        mine = jnp.stack([w_write[l], other_write])
        mine = jnp.where(half == 0, mine, mine[::-1])
        theirs = core_swap(mine)
        left, right = jnp.where(core == 0, mine, theirs), jnp.where(core == 0, theirs, mine)
        full_write = jnp.concatenate([left[0], right[0], left[1], right[1]], axis=1)

        def spread_bias(row):
            parts = wide(row[: 2 * heads * HD]).reshape(heads, 2, HD)
            filled = jnp.stack([parts[:, 0], jnp.zeros_like(parts[:, 0]), parts[:, 1]], axis=1)
            return filled.reshape(1, -1), wide(row[2 * heads * HD :]).reshape(1, -1)

        qkv_bias, fc_bias = spread_bias(bias_rows[l])
        other_qkv_bias, other_fc_bias = spread_bias(other_bias[l])
        weights.append(
            dict(
                write=full_write,
                qkv=((w_qkv, l), fetch_other(w_qkv[l])),
                out=((w_out, l), fetch_other(w_out[l])),
                fc=((w_fc, l), fetch_other(w_fc[l])),
                proj=((w_proj, l), fetch_other(w_proj[l])),
                qkv_bias=(qkv_bias, other_qkv_bias),
                fc_bias=(fc_bias, other_fc_bias),
                gains=(gains, l),
                shifts=(shifts, l),
                assoc=(assoc, l),
                bias=(out_bias, l),
            )
        )

    def places(core_id):
        within = jnp.arange(block_rows)
        rows = []
        for block in (core_id, core_id + 2):
            rows.append(
                jnp.where(
                    within < mem_rows,
                    block * mem_rows + within,
                    4 * mem_rows + block * (block_rows - mem_rows) + within - mem_rows,
                )
            )
        return jnp.concatenate(rows)

    pos = jnp.concatenate([places(core), places(1 - core)]).astype(jnp.int32)
    pos_rows = jnp.broadcast_to(pos[:, None], (all_rows, 128))
    pos_cols = jnp.broadcast_to(pos[None, :], (8, all_rows))
    number = lax.dynamic_index_in_dim(segno[:, 0], half, 0, keepdims=False)
    segment_of = jnp.arange(slots) // NMEM
    mask = jnp.broadcast_to(
        ((segment_of < me) & (segment_of >= me - number)).astype(F32)[None, :], (own_rows, slots)
    )

    saved = []
    (normed,) = phase(
        write_keys, [((own_rows, D), BF)], x, weights[0]["gains"], weights[0]["shifts"], weights[0]["assoc"]
    )
    for l in range(LAYERS):
        w = weights[l]
        tail_own = normed[own_rows - NMEM :]
        tail = jnp.where(core == 1, tail_own, core_swap(tail_own))
        tails = gather_segments(tail)
        keys, feat_q = phase(
            read_features, [((own_rows, key_dim), BF), ((own_rows, phi), BF)], normed, w["assoc"]
        )
        tail_keys, feat_k, scores, denom = phase(
            write_scores,
            [((slots, key_dim), F32), ((slots, phi), BF), ((own_rows, slots), BF), ((own_rows, slots), F32)],
            tails,
            w["assoc"],
            feat_q,
            mask,
        )
        (values,) = phase(write_values, [((slots, D), BF)], tails, w["write"])
        mid, normed1 = phase(
            read_memory,
            [((own_rows, D), F32), ((own_rows, D), BF)],
            x,
            scores,
            values,
            denom,
            w["gains"],
            w["shifts"],
        )
        normed1_core = core_swap(normed1)
        part, sent, packed0, packed1, mixed0, mixed1 = phase(
            attention,
            [((own_rows, D), F32), ((own_rows, D), BF)]
            + [((all_rows, 3 * HD * heads), BF)] * 2
            + [((all_rows, HD * heads), BF)] * 2,
            normed1,
            normed1_core,
            *w["qkv"],
            *w["qkv_bias"],
            *w["out"],
            pos_rows,
            pos_cols,
        )
        after, normed2 = phase(
            after_attention,
            [((own_rows, D), F32), ((own_rows, D), BF)],
            mid,
            part,
            core_swap(sent),
            w["bias"],
            w["gains"],
            w["shifts"],
        )
        normed2_core = core_swap(normed2)
        part, sent, hidden0, hidden1, slope0, slope1 = phase(
            feed_forward,
            [((own_rows, D), F32), ((own_rows, D), BF)] + [((all_rows, units), BF)] * 4,
            normed2,
            normed2_core,
            *w["fc"],
            *w["fc_bias"],
            *w["proj"],
        )
        later = weights[min(l + 1, LAYERS - 1)]
        x_next, normed_next = phase(
            after_feed,
            [((own_rows, D), F32), ((own_rows, D), BF)],
            after,
            part,
            core_swap(sent),
            w["bias"],
            later["gains"],
            later["shifts"],
        )
        saved.append(
            dict(
                x=x, normed=normed, tails=tails, keys=keys, feat_q=feat_q, tail_keys=tail_keys, feat_k=feat_k,
                scores=scores, denom=denom, values=values, mid=mid, normed1=(normed1, normed1_core),
                packed=(packed0, packed1), mixed=(mixed0, mixed1), after=after,
                normed2=(normed2, normed2_core), hidden=(hidden0, hidden1), slope=(slope0, slope1),
            )
        )
        x, normed = x_next, normed_next

    def give_back(rows):
        blocks = rows.reshape(2, block_rows, -1)
        mine = pick(blocks, half)
        got = half_swap(pick(blocks, 1 - half))
        return jnp.where(half == 0, jnp.stack([mine, got]), jnp.stack([got, mine]))

    result = give_back(x.astype(BF))
    out_memory = result[:, :mem_rows][:, None]
    out_tokens = result[:, mem_rows:][:, None]

    grad_low = in_order(pick(cots, half), half_swap(pick(cots, 1 - half)))
    grad = wide(grad_low)
    vec = ((1, D), F32)
    layer_grads = [None] * LAYERS
    small = [None] * LAYERS

    def both_halves(own, core_rows):
        got = half_swap(own)
        return own, core_rows, got, core_swap(got)

    def wide_product(rows, own, other):
        first, second, third, fourth = rows
        arrived = half_swap(other)
        product = dot_tn(jnp.concatenate([first, second]), own) + dot_tn(jnp.concatenate([third, fourth]), arrived)
        sums = jnp.sum(wide(own), axis=0) + jnp.sum(wide(arrived), axis=0)
        return product.astype(BF), sums

    for l in reversed(range(LAYERS)):
        w, s = weights[l], saved[l]
        grad_core = core_swap(grad_low)
        part, sent, d_pre0, d_pre1 = phase(
            feed_back,
            [((own_rows, D), F32), ((own_rows, D), BF)] + [((all_rows, units), BF)] * 2,
            grad_low,
            grad_core,
            *w["fc"],
            *w["proj"],
            *s["slope"],
        )
        d_after, d_after_low, d_gain2, d_shift2, d_bias1 = phase(
            after_feed_back,
            [((own_rows, D), F32), ((own_rows, D), BF), vec, vec, vec],
            grad,
            part,
            core_swap(sent),
            s["after"],
            w["gains"],
        )
        d_after_core = core_swap(d_after_low)
        g_fc, g_bfc = wide_product(both_halves(*s["normed2"]), d_pre0, d_pre1)
        g_proj, _ = wide_product(both_halves(grad_low, grad_core), *s["hidden"])
        part, sent, d_packed0, d_packed1 = phase(
            attention_back,
            [((own_rows, D), F32), ((own_rows, D), BF)] + [((all_rows, 3 * HD * heads), BF)] * 2,
            d_after_low,
            d_after_core,
            *w["qkv"],
            *w["out"],
            *s["packed"],
            pos_rows,
            pos_cols,
        )
        d_mid, d_scores, d_keys, d_values, d_gain1, d_shift1, d_bias0 = phase(
            after_attention_back,
            [((own_rows, D), F32), ((own_rows, slots), BF), ((slots, key_dim), F32), ((slots, D), F32), vec, vec, vec],
            d_after,
            part,
            core_swap(sent),
            s["mid"],
            w["gains"],
            s["scores"],
            s["values"],
            s["denom"],
            mask,
            s["feat_q"],
            s["tail_keys"],
        )
        key_halves = jnp.stack([d_keys[:, : key_dim // 2], d_keys[:, key_dim // 2 :]])
        value_halves = jnp.stack([d_values[:, : D // 2], d_values[:, D // 2 :]])
        halves = jnp.concatenate([key_halves, value_halves], axis=2)
        written = pick(halves, core) + wide(core_swap(pick(halves, 1 - core).astype(BF)))
        written = scatter_segments(written.astype(BF))
        written_core = core_swap(written)
        left, right = jnp.where(core == 0, written, written_core), jnp.where(core == 0, written_core, written)
        cut = key_dim // 2
        d_tail, d_vals = phase(
            tail_back,
            [((NMEM, D), F32), ((NMEM, D), BF)],
            jnp.concatenate([left[:, :cut], right[:, :cut]], axis=1),
            jnp.concatenate([left[:, cut:], right[:, cut:]], axis=1),
            w["assoc"],
            w["write"],
        )
        d_tail = jnp.where(core == 1, d_tail, 0.0)
        d_read_keys, d_norm = phase(
            read_back, [((own_rows, key_dim), BF), ((own_rows, D), F32)], d_scores, s["feat_k"], s["keys"], w["assoc"]
        )
        d_x, d_x_low, d_gain0, d_shift0 = phase(
            layer_end_back,
            [((own_rows, D), F32), ((own_rows, D), BF), vec, vec],
            d_mid,
            d_norm,
            d_tail,
            s["x"],
            w["gains"],
        )
        g_qkv, sums = wide_product(both_halves(*s["normed1"]), d_packed0, d_packed1)
        g_out, _ = wide_product(both_halves(d_after_low, d_after_core), *s["mixed"])
        tail_own = s["normed"][own_rows - NMEM :]
        tail = jnp.where(core == 1, tail_own, core_swap(tail_own))
        columns = w_write.shape[2]
        blocks = jnp.moveaxis(d_vals.reshape(NMEM, 4, columns), 1, 0)
        other_vals = half_swap(pick(blocks, tp ^ 2))
        g_write = (dot_tn(tail, pick(blocks, tp)) + dot_tn(half_swap(tail), other_vals)).astype(BF)
        g_assoc = jnp.concatenate(
            [dot_tn(s["normed"], d_read_keys), dot_tn(s["tails"], d_keys.astype(BF))], axis=1
        ).astype(BF)
        g_assoc = g_assoc.reshape(segs, 2, 2, -1, 2 * key_dim)
        for which, bit, dim in ((core, 1, 2), (half, 2, 1)):
            keep = lax.dynamic_index_in_dim(g_assoc, which, dim, keepdims=False)
            send = lax.dynamic_index_in_dim(g_assoc, 1 - which, dim, keepdims=False)
            g_assoc = (wide(keep) + wide(toward(send, "tp", bit))).astype(BF)

        def owned(g):
            return sum_over_segments(g.reshape(segs, g.shape[0] // segs, g.shape[1]))

        bias_sums = sums.reshape(heads, 3, HD)
        g_qv = jnp.stack([bias_sums[:, 0], bias_sums[:, 2]], axis=1).reshape(-1)
        layer_grads[l] = dict(
            fc=owned(g_fc),
            proj=owned(g_proj).T,
            qkv=owned(g_qkv),
            out=owned(g_out).T,
            write=owned(g_write),
            assoc=sum_over_segments(g_assoc).T,
        )
        qv_full = lax.dynamic_update_slice(jnp.zeros((4 * g_qv.shape[0],), F32), g_qv, (tp * g_qv.shape[0],))
        bfc_full = lax.dynamic_update_slice(jnp.zeros((4 * units,), F32), g_bfc, (tp * units,))
        rows = [d_gain0, d_gain1, d_gain2, d_shift0, d_shift1, d_shift2, d_bias0, d_bias1]
        rows += [qv_full.reshape(-1, D), bfc_full.reshape(-1, D)]
        if l == 0:
            kept = d_x.reshape(2, block_rows, D)[:, :mem_rows]
            mem_full = lax.dynamic_update_slice(
                jnp.zeros((2, 2, mem_rows, D), F32), kept[:, None], (0, core, 0, 0)
            )
            rows.append(mem_full.reshape(-1, D))
        small[l] = sum_over_all(jnp.concatenate(rows))
        grad, grad_low = d_x, d_x_low

    result = give_back(grad)
    grad_tokens = result[:, mem_rows:][:, None]
    at = me * 4 + tp

    def own_columns(rows):
        return lax.dynamic_slice_in_dim(rows, at * (D // (4 * segs)), D // (4 * segs), axis=1)

    def own_entries(rows):
        flat = rows.reshape(1, -1)
        size = flat.shape[1] // (4 * segs)
        return lax.dynamic_slice_in_dim(flat, at * size, size, axis=1)[0]

    columns = [own_columns(r) for r in small]
    qv_rows = 2 * D // D
    stacked = {k: jnp.stack([layer_grads[l][k] for l in range(LAYERS)]) for k in layer_grads[0]}
    return (
        out_tokens,
        out_memory,
        grad_tokens,
        columns[0][14:],
        jnp.stack([c[0:3] for c in columns]),
        jnp.stack([c[3:6] for c in columns]),
        stacked["assoc"],
        stacked["write"],
        stacked["qkv"],
        jnp.stack([own_entries(r[8 : 8 + qv_rows]) for r in small]),
        stacked["out"],
        jnp.stack([c[6:8] for c in columns]),
        stacked["fc"],
        jnp.stack([own_entries(r[8 + qv_rows : 14]) for r in small]),
        stacked["proj"],
    )


def solution(mesh):
    return jax.shard_map(
        local,
        mesh=mesh,
        in_specs=(
            P(None, "seg", "tp", None),
            P("tp", None),
            P(None, "seg"),
            P(),
            P(),
            P(),
            P(None, None, "tp"),
            P(None, None, "tp"),
            P(None, "tp"),
            P(None, "tp", None),
            P(),
            P(None, None, "tp"),
            P(None, "tp"),
            P(None, "tp", None),
            P(None, "seg", "tp", None),
            P(None, "seg", "tp", None),
        ),
        out_specs=(
            P(None, "seg", "tp", None),
            P(None, "seg", "tp", None),
            P(None, "seg", "tp", None),
            P(None, ("seg", "tp")),
            P(None, None, ("seg", "tp")),
            P(None, None, ("seg", "tp")),
            P(None, None, ("seg", "tp")),
            P(None, "seg", "tp"),
            P(None, "seg", "tp"),
            P(None, ("seg", "tp")),
            P(None, "tp", "seg"),
            P(None, None, ("seg", "tp")),
            P(None, "seg", "tp"),
            P(None, ("seg", "tp")),
            P(None, "tp", "seg"),
        ),
        check_vma=False,
    )
```

```python
import functools

import jax
import jax.numpy as jnp
from jax import lax
from jax.experimental import pallas as pl
from jax.experimental.pallas import tpu as pltpu
from jax.sharding import PartitionSpec as P

D = 768
HD = 64
NMEM = 16
LAYERS = 2
BF = jnp.bfloat16
F32 = jnp.float32
VMEM_BYTES = 40 * 1024 * 1024


class Far:
    def __init__(self, item):
        self.item = item


def far(*items):
    return [Far(item) for item in items]


def scalars():
    seg, tp = lax.axis_index("seg"), lax.axis_index("tp")
    return [seg & 1, tp // 2, tp % 2, tp] + [(seg >> b) & 1 for b in range(lax.axis_size("seg").bit_length() - 1)]


def value_of(item):
    if isinstance(item, Far):
        item = item.item
    if not isinstance(item, tuple):
        return item
    if len(item) == 3:
        return item[0][item[1] * item[2] : item[1] * (item[2] + 1)]
    return item[0][item[1]]


def phase(body, outs, ids, *items, kernel=True, after=(), scratch=()):
    if not kernel:
        return body(False, ids, *[value_of(item) for item in items])
    arrays, specs = [], []
    for item in items:
        if isinstance(item, Far):
            item = item.item
            where = functools.partial(pltpu.with_memory_space_constraint, memory_space=pltpu.HBM)
            item = (where(item[0]), *item[1:]) if isinstance(item, tuple) else where(item)
        if isinstance(item, tuple) and len(item) == 3:
            array, rows, at = item
            arrays.append(array)
            specs.append(pl.BlockSpec((rows, array.shape[1]), functools.partial(lambda at, i: (at, 0), at)))
        elif isinstance(item, tuple):
            array, layer = item
            rest = array.shape[1:]
            arrays.append(array)
            specs.append(
                pl.BlockSpec((None,) + rest, functools.partial(lambda l, n, i: (l,) + (0,) * n, layer, len(rest)))
            )
        else:
            arrays.append(item)
            specs.append(pl.BlockSpec(item.shape, functools.partial(lambda n, i: (0,) * n, item.ndim)))
    count = len(arrays)
    for array in after:
        arrays.append(array)
        specs.append(pl.BlockSpec(memory_space=pl.ANY))

    def run(*refs):
        spaces = refs[len(arrays) + len(outs) :]
        results = body(True, scalars(), *spaces, *[r[...] for r in refs[:count]])
        for ref, result in zip(refs[len(arrays) :], results):
            ref[...] = result

    return pl.pallas_call(
        run,
        grid=(1,),
        out_shape=[pltpu.HBM(*out[:2]) if len(out) == 3 else jax.ShapeDtypeStruct(*out) for out in outs],
        in_specs=specs,
        out_specs=[pl.BlockSpec(out[0], functools.partial(lambda n, i: (0,) * n, len(out[0]))) for out in outs],
        scratch_shapes=[pltpu.VMEM(s, t) for s, t in scratch],
        compiler_params=pltpu.CompilerParams(vmem_limit_bytes=VMEM_BYTES),
        name=getattr(body, "func", body).__name__,
    )(*arrays)


def wide(v):
    return v.astype(F32)


def dot(a, b):
    return lax.dot_general(a, b, (((1,), (0,)), ((), ())), preferred_element_type=F32)


def dot_nt(a, b):
    return lax.dot_general(a, b, (((1,), (1,)), ((), ())), preferred_element_type=F32)


def dot_tn(a, b):
    return lax.dot_general(a, b, (((0,), (0,)), ((), ())), preferred_element_type=F32)


def turn(v, by, native):
    if native:
        return pltpu.roll(v, (-by) % v.shape[1], 1)
    return jnp.roll(v, -by, axis=1)


def rows_of(*pieces):
    return jnp.concatenate(pieces, axis=0)


def columns_of(*pieces):
    return jnp.concatenate(pieces, axis=1)


def ordered(flag, first, second):
    return jnp.where(flag == 1, second, first), jnp.where(flag == 1, first, second)


def split_blocks(total, rows, flag, place=0):
    keep, send = [], []
    step = rows << place
    for at in range(0, total.shape[0], 2 * step):
        mine, others = ordered(flag, total[at : at + step], total[at + step : at + 2 * step])
        keep.append(mine)
        send.append(others)
    return rows_of(*keep), rows_of(*send)


def place_row(row, at, first, count=16):
    index = lax.broadcasted_iota(jnp.int32, (count, row.shape[1]), 0)
    return jnp.where(index == first + at, jnp.broadcast_to(row, (count, row.shape[1])), 0.0)


ODD, HALF, CORE, TP, BIT = 0, 1, 2, 3, 4
FEED_ORDERS = (((0, 1), (1, 0)), ((0, 1),))
ATT_ORDERS = ((0, 1), (1, 0))
MEM_ORDERS = ((1, 0), (1, 0))


def norm_parts(rows):
    centred = rows - jnp.mean(rows, axis=-1, keepdims=True)
    rstd = lax.rsqrt(jnp.mean(centred * centred, axis=-1, keepdims=True) + 1e-05)
    return centred * rstd, rstd


def norm_rows(rows, gain, shift):
    return norm_parts(rows)[0] * wide(gain) + wide(shift)


def norm_back(rows, gain, grad):
    hat, rstd = norm_parts(rows)
    d_hat = grad * wide(gain)
    d_rows = rstd * (
        d_hat
        - jnp.mean(d_hat, axis=-1, keepdims=True)
        - hat * jnp.mean(d_hat * hat, axis=-1, keepdims=True)
    )
    return d_rows, jnp.sum(grad * hat, axis=0, keepdims=True), jnp.sum(grad, axis=0, keepdims=True)


def paired(v):
    rest = jnp.log1p(jnp.exp(-jnp.abs(v)))
    return columns_of(jnp.maximum(v, 0.0) + rest, jnp.maximum(-v, 0.0) + rest)


def features(v, native):
    c = paired(v)
    return columns_of(*[c * turn(c, k, native) for k in (1, 2, 3)])


def features_back(v, grad, native):
    c = paired(v)
    size = c.shape[1]
    d_c = jnp.zeros_like(c)
    for k in (1, 2, 3):
        part = grad[:, (k - 1) * size : k * size]
        d_c = d_c + part * turn(c, k, native) + turn(part * c, -k, native)
    half = v.shape[1]
    up = 1.0 / (1.0 + jnp.exp(-v))
    return d_c[:, :half] * up - d_c[:, half:] * (1.0 - up)


def other_rows(odd, part, rest, first=0, last=None):
    return rows_of(*ordered(odd, part[first:last], rest[first:last]))


def first_rows(native, ids, own, got, gains, shifts, sizes):
    count = own.shape[0]
    x = wide(rows_of(*ordered(ids[HALF], own, got[:count])))
    normed = norm_rows(x, gains[0:1], shifts[0:1]).astype(BF)
    pieces, at = [], count
    for size in sizes:
        pieces.append(got[at : at + size])
        at += size
    return (x, normed, normed[normed.shape[0] - NMEM :], *pieces)


def read_keys_of(normed, assoc):
    return wide(dot_nt(normed, assoc[: assoc.shape[0] // 2]).astype(BF))


def written_keys_of(tails, assoc):
    return dot_nt(tails, assoc[assoc.shape[0] // 2 :])


def write_scores(native, ids, normed, tails, assoc, mask, w_write, part, rest, out_bit):
    feat_q = features(read_keys_of(normed, assoc), native).astype(BF)
    feat_k = features(written_keys_of(tails, assoc), native).astype(BF)
    scores = dot_nt(feat_q, feat_k) * mask
    denom = jnp.sum(scores, axis=1, keepdims=True) + 1.0
    others = other_rows(ids[BIT + out_bit], part, rest)
    values = columns_of(*ordered(ids[HALF], dot_nt(tails, w_write), dot_nt(tails, others)))
    return (scores.astype(BF), jnp.broadcast_to(denom, mask.shape), values.astype(BF))


def read_memory(native, ids, x, scores, values, values_core, denom, gains, shifts):
    left, right = ordered(ids[CORE], values, values_core)
    width = left.shape[1] // 2
    values = columns_of(left[:, :width], right[:, :width], left[:, width:], right[:, width:])
    read = (dot(scores, values) / denom[:, 0:1]).astype(BF)
    mid = x + wide(read)
    return (mid, norm_rows(mid, gains[1:2], shifts[1:2]).astype(BF), values)


def head_parts(packed, head):
    at = 3 * HD * head
    return packed[:, at : at + HD], packed[:, at + HD : at + 2 * HD], packed[:, at + 2 * HD : at + 3 * HD]


def head_probs(queries, keys, hide):
    scores = dot_nt(queries, keys) * 0.125 + hide
    weights = jnp.exp(scores - jnp.max(scores, axis=1, keepdims=True))
    return weights / jnp.sum(weights, axis=1, keepdims=True)


def head_bias(row):
    row = wide(row)
    blank = jnp.zeros((1, HD), F32)
    pieces = []
    for at in range(0, row.shape[1], 2 * HD):
        pieces += [row[:, at : at + HD], blank, row[:, at + HD : at + 2 * HD]]
    return columns_of(*pieces)


def attention_weights(ids, out_bit, w_qkv, w_out, part, rest, out_part, out_rest):
    return (w_qkv, w_out), (other_rows(ids[BIT], part, rest), other_rows(ids[BIT + out_bit], out_part, out_rest))


def put_heads(space, at, packed, parts):
    for column in range(packed.shape[1] // HD):
        space[at + column // parts, column % parts] = packed[:, HD * column : HD * (column + 1)]


def take_heads(space, first, last):
    return columns_of(*[space[head, part] for head in range(first, last) for part in range(space.shape[1])])


def attention(native, ids, heads, mixed_heads, own, other, w_qkv, w_out, part, rest, out_part, out_rest, bias, biases, hide, layer, out_bit):
    rows = rows_of(own, other)
    half = own.shape[0]
    width = bias.shape[1]
    other_bias = biases[LAYERS : LAYERS + 1, layer * width : (layer + 1) * width]
    weights = attention_weights(ids, out_bit, w_qkv, w_out, part, rest, out_part, out_rest)
    count = width // (2 * HD)
    packs = []
    for block, ((w, _), row) in enumerate(zip(weights, (bias, other_bias))):
        packed = (dot_nt(rows, w) + head_bias(row)).astype(BF)
        put_heads(heads, block * count, packed, 3)
        packs.append(packed)

    def one(head, carried):
        probs = head_probs(heads[head, 0], heads[head, 1], hide)
        mixed_heads[head, 0] = dot(probs.astype(BF), heads[head, 2]).astype(BF)
        return carried

    lax.fori_loop(0, 2 * count, one, 0)
    total, mixes = 0.0, []
    for block, (_, o) in enumerate(weights):
        mixed = take_heads(mixed_heads, block * count, (block + 1) * count)
        total = total + dot(mixed, o)
        mixes.append(mixed)
    return (total[:half], total[half:].astype(BF), *packs, *mixes)


def after_attention(native, ids, mid, part, arrived, bias, gains, shifts):
    after = mid + part + wide(arrived) + wide(bias[0:1])
    return (after, norm_rows(after, gains[2:3], shifts[2:3]).astype(BF))


def gelu_both(v):
    inner = 0.7978845608028654 * (v + 0.044715 * v * v * v)
    t = jnp.tanh(inner)
    slope = 0.5 * (1.0 + t) + 0.5 * v * (1.0 - t * t) * 0.7978845608028654 * (1.0 + 3 * 0.044715 * v * v)
    return 0.5 * v * (1.0 + t), slope


def feed_weights(ids, w_fc, w_proj, part, rest, part_proj, rest_proj):
    return (w_fc, w_proj), (other_rows(ids[BIT], part, rest), other_rows(ids[BIT + 1], part_proj, rest_proj))


def feed_forward(
    native, ids, own, other, w_fc, w_proj, part, rest, part_proj, rest_proj, bias, biases, normed1, tail, layer
):
    rows = rows_of(own, other)
    half = own.shape[0]
    other_bias = biases[layer : layer + 1]
    total, hiddens, slopes = 0.0, [], []
    for (w, p), row in zip(
        feed_weights(ids, w_fc, w_proj, part, rest, part_proj, rest_proj), (bias, other_bias)
    ):
        hidden, slope = gelu_both(dot(rows, w) + wide(row))
        hidden = hidden.astype(BF)
        total = total + dot(hidden, p)
        hiddens.append(hidden)
        slopes.append(slope.astype(BF))
    return (total[:half], total[half:].astype(BF), hiddens[0], *slopes, rows_of(hiddens[1], normed1, own, tail))


def after_feed(native, ids, after, part, arrived, bias, next_gains, next_shifts):
    x = after + part + wide(arrived) + wide(bias[1:2])
    normed = norm_rows(x, next_gains[0:1], next_shifts[0:1]).astype(BF)
    return (x, normed, normed[normed.shape[0] - NMEM :])


def after_last(native, ids, after, part, arrived, bias):
    x = (after + part + wide(arrived) + wide(bias[1:2])).astype(BF)
    half = x.shape[0] // 2
    return ordered(ids[HALF], x[:half], x[half:])


def feed_back(native, ids, own, other, w_fc, w_proj, part, rest, part_proj, rest_proj, slope0, slope1):
    grads = rows_of(own, other)
    half = own.shape[0]
    total, saved = 0.0, []
    for (w, p), slope in zip(
        feed_weights(ids, w_fc, w_proj, part, rest, part_proj, rest_proj), (slope0, slope1)
    ):
        d_pre = (dot_nt(grads, p) * wide(slope)).astype(BF)
        total = total + dot_nt(d_pre, w)
        saved.append(d_pre)
    return (total[:half], total[half:].astype(BF), saved[0], rows_of(saved[1], own))


def after_feed_back(native, ids, grad, part, arrived, after, gains):
    grad = wide(grad[: after.shape[0]])
    d_rows, d_gain, d_shift = norm_back(after, gains[2:3], part + wide(arrived))
    d_after = grad + d_rows
    d_bias = jnp.sum(grad, axis=0, keepdims=True)
    small = place_row(d_gain, 2, 0) + place_row(d_shift, 5, 0) + place_row(d_bias, 7, 0)
    return (rows_of(d_after, small), d_after.astype(BF))


def attention_back(
    native, ids, heads, d_mixed_heads, d_heads, own, other, w_qkv, w_out, part, rest, out_part, out_rest, packed0, packed1, mixed1, hide, out_bit
):
    grads = rows_of(own, other)
    half = own.shape[0]
    count = packed0.shape[1] // (3 * HD)
    weights = attention_weights(ids, out_bit, w_qkv, w_out, part, rest, out_part, out_rest)
    for block, ((_, o), packed) in enumerate(zip(weights, (packed0, packed1))):
        put_heads(heads, block * count, packed, 3)
        put_heads(d_mixed_heads, block * count, dot_nt(grads, o).astype(BF), 1)

    def one(head, carried):
        queries, keys, values = heads[head, 0], heads[head, 1], heads[head, 2]
        dm = d_mixed_heads[head, 0]
        probs = head_probs(queries, keys, hide)
        d_probs = dot_nt(dm, values)
        d_scores = (probs * (d_probs - jnp.sum(d_probs * probs, axis=1, keepdims=True))).astype(BF)
        d_heads[head, 0] = (dot(d_scores, keys) * 0.125).astype(BF)
        d_heads[head, 1] = (dot_tn(d_scores, queries) * 0.125).astype(BF)
        d_heads[head, 2] = dot_tn(probs.astype(BF), dm).astype(BF)
        return carried

    lax.fori_loop(0, 2 * count, one, 0)
    total, saved = 0.0, []
    for block, (w, _) in enumerate(weights):
        d_packed = take_heads(d_heads, block * count, (block + 1) * count)
        total = total + dot(d_packed, w)
        saved.append(d_packed)
    return (total[:half], total[half:].astype(BF), saved[0], rows_of(columns_of(saved[1], mixed1), own))


def after_attention_back(native, ids, d_after, part, arrived, mid, gains, scores, values, denom, mask, normed, tails, assoc):
    d_after, small = d_after[: mid.shape[0]], d_after[mid.shape[0] :]
    d_rows, d_gain, d_shift = norm_back(mid, gains[1:2], part + wide(arrived))
    d_mid = d_after + d_rows
    d_bias = jnp.sum(d_after, axis=0, keepdims=True)
    small = small + place_row(d_gain, 1, 0) + place_row(d_shift, 4, 0) + place_row(d_bias, 6, 0)
    scale = 1.0 / denom[:, 0:1]
    d_numer = (d_mid * scale).astype(BF)
    d_denom = -jnp.sum(d_mid * dot(scores, values), axis=1, keepdims=True) * scale * scale
    d_scores = ((dot_nt(d_numer, values) + d_denom) * mask).astype(BF)
    feat_q = features(read_keys_of(normed, assoc), native).astype(BF)
    d_keys = features_back(written_keys_of(tails, assoc), dot_tn(d_scores, feat_q), native)
    d_values = dot_tn(scores, d_numer)
    cut, width = d_keys.shape[1] // 2, d_values.shape[1] // 4
    mine, others = ordered(
        ids[CORE],
        columns_of(d_keys[:, :cut], d_values[:, :width], d_values[:, 2 * width : 3 * width]),
        columns_of(d_keys[:, cut:], d_values[:, width : 2 * width], d_values[:, 3 * width :]),
    )
    return (rows_of(d_mid, small), d_scores, d_keys.astype(BF), mine, others.astype(BF))


def read_back(native, ids, d_scores, normed, tails, assoc, d_tail_keys, segs):
    feat_k = features(written_keys_of(tails, assoc), native).astype(BF)
    d_keys = features_back(read_keys_of(normed, assoc), dot(d_scores, feat_k), native).astype(BF)
    d_norm = dot(d_keys, assoc[: assoc.shape[0] // 2])
    product = columns_of(dot_tn(normed, d_keys), dot_tn(tails, d_tail_keys))
    keep, send = split_blocks(product, product.shape[0] // (4 * segs), ids[CORE])
    return (d_norm, keep.astype(BF), send.astype(BF))


def assoc_second(native, ids, keep, arrived, values, segs):
    total = wide(keep) + wide(arrived)
    keep, send = split_blocks(total, total.shape[0] // (2 * segs), ids[HALF])
    blank = jnp.zeros((values.shape[0], send.shape[1] - values.shape[1]), BF)
    return (keep.astype(BF), rows_of(send.astype(BF), columns_of(values, blank)))


def tail_back(native, ids, arrived, assoc, w_write, part, rest, out_bit):
    total = wide(arrived[:NMEM])
    for at in range(NMEM, arrived.shape[0], NMEM):
        total = total + wide(arrived[at : at + NMEM])
    cut = total.shape[1] // 3
    low = total.astype(BF)
    own, other = ordered(ids[HALF], low[:, cut : 2 * cut], low[:, 2 * cut :])
    size = assoc.shape[0] // 4
    used, _ = ordered(ids[CORE], assoc[2 * size : 3 * size], assoc[3 * size :])
    others = other_rows(ids[BIT + out_bit], part, rest)
    d_tail = dot(low[:, :cut], used) + dot(own, w_write) + dot(other, others)
    return (d_tail, own, other)


def layer_end_back(native, ids, d_mid, d_norm, d_tail, d_tail_core, x, gains):
    rows = d_norm.shape[0]
    d_mid, small = d_mid[:rows], d_mid[rows:]
    added = jnp.where(ids[CORE] == 1, d_tail + d_tail_core, 0.0)
    d_norm = rows_of(d_norm[: rows - NMEM], d_norm[rows - NMEM :] + added)
    d_rows, d_gain, d_shift = norm_back(x, gains[0:1], d_norm)
    d_x = d_mid + d_rows
    return (rows_of(d_x, small + place_row(d_gain, 0, 0) + place_row(d_shift, 3, 0)), d_x.astype(BF))


def feed_grads(
    native, ids, n_own, n_core, n_got, n_got_core, d_pre, d_pre_got, g_own, g_core, g_got, g_got_core, hidden, hidden_got, segs, orders
):
    fc = dot_tn(rows_of(n_own, n_core), d_pre) + dot_tn(rows_of(n_got, n_got_core), d_pre_got)
    proj = dot_tn(rows_of(g_own, g_core), hidden) + dot_tn(rows_of(g_got, g_got_core), hidden_got)
    sums = jnp.sum(wide(d_pre), axis=0, keepdims=True) + jnp.sum(wide(d_pre_got), axis=0, keepdims=True)
    cuts = []
    for order, product in zip(orders, (fc, proj) if len(orders) == 2 else (columns_of(fc, proj),)):
        for v in split_blocks(product, fc.shape[0] // segs, ids[BIT + order[0]], order[0]):
            cuts.append(v.astype(BF))
    return (*cuts, place_row(sums, ids[TP], 8))


def attention_grads(
    native, ids, n_own, n_core, n_got, n_got_core, d_packed, got, g_own, g_core, g_got, g_got_core, mixed, segs, order
):
    width = d_packed.shape[1]
    qkv = dot_tn(rows_of(n_own, n_core), d_packed) + dot_tn(rows_of(n_got, n_got_core), got[:, :width])
    out = dot_tn(rows_of(g_own, g_core), mixed) + dot_tn(rows_of(g_got, g_got_core), got[:, width:])
    sums = jnp.sum(wide(d_packed), axis=0, keepdims=True) + jnp.sum(wide(got[:, :width]), axis=0, keepdims=True)
    pieces = []
    for at in range(0, sums.shape[1], 3 * HD):
        pieces += [sums[:, at : at + HD], sums[:, at + 2 * HD : at + 3 * HD]]
    sums = columns_of(*pieces)
    blank = jnp.zeros_like(sums)
    row, _ = ordered(ids[CORE], columns_of(sums, blank), columns_of(blank, sums))
    keep, send = split_blocks(columns_of(qkv, out), qkv.shape[0] // segs, ids[BIT + order[0]], order[0])
    return (keep.astype(BF), send.astype(BF), place_row(row, ids[HALF], 12))


def memory_grads(native, ids, keep, arrived, tail, tail_got, d_own, segs, order):
    count = keep.shape[0]
    total = wide(keep) + wide(arrived[:count])
    write = dot_tn(tail, d_own) + dot_tn(tail_got, arrived[count:, : d_own.shape[1]])
    few, many = count // segs, write.shape[0] // segs
    blocks = []
    for s in range(segs):
        part = write[s * many : (s + 1) * many]
        folded = columns_of(*[part[i * few : (i + 1) * few] for i in range(4)])
        blocks.append(rows_of(total[s * few : (s + 1) * few], folded))
    keep, send = split_blocks(rows_of(*blocks), 2 * few, ids[BIT + order[0]], order[0])
    return (keep.astype(BF), send.astype(BF))


def next_cut(native, ids, keep, arrived, bit, place, rows):
    total = wide(keep) + wide(arrived)
    keep, send = split_blocks(total, rows, ids[BIT + bit], place)
    return (keep.astype(BF), send.astype(BF))


def both_layers(first_keep, first_got, second_keep, second_got):
    return jnp.stack([wide(first_keep) + wide(first_got), wide(second_keep) + wide(second_got)])


def feed_end(native, ids, fc_keep, fc_got, proj_keep, proj_got, both_keep, both_got):
    width = fc_keep.shape[1]
    both = wide(both_keep) + wide(both_got)
    fc, proj = wide(fc_keep) + wide(fc_got), wide(proj_keep) + wide(proj_got)
    return (jnp.stack([fc, both[:, :width]]), jnp.stack([proj, both[:, width:]]))


def attention_end(native, ids, *pairs, columns):
    total = both_layers(*pairs)
    return (total[:, :, :columns], total[:, :, columns:])


def memory_end(native, ids, *pairs):
    total = both_layers(*pairs)
    few = total.shape[1] // 2
    width = total.shape[2] // 4
    folded = total[:, few:]
    return (total[:, :few], jnp.concatenate([folded[:, :, i * width : (i + 1) * width] for i in range(4)], axis=1))


def pack_rows(*refs, count):
    weights, packed, at = refs[1 : 1 + count], refs[-1], 0
    for w in weights:
        packed[at : at + w.shape[0]] = w[...]
        at += w.shape[0]


def pack(ids, layer, weights, front=(), after=()):
    halves = [w.shape[1] // 2 for w, _ in weights]
    rows = sum(f.shape[0] for f in front) + sum(halves)
    return pl.pallas_call(
        functools.partial(pack_rows, count=len(front) + len(weights)),
        grid_spec=pltpu.PrefetchScalarGridSpec(
            num_scalar_prefetch=1,
            grid=(1,),
            in_specs=[pl.BlockSpec(f.shape, lambda i, ids: (0, 0)) for f in front]
            + [
                pl.BlockSpec((None, n, w.shape[2]), functools.partial(lambda b, i, ids: (layer, ids[BIT + b], 0), bit))
                for n, (w, bit) in zip(halves, weights)
            ]
            + [pl.BlockSpec(memory_space=pl.ANY) for _ in after],
            out_specs=pl.BlockSpec((rows, D), lambda i, ids: (0, 0)),
        ),
        out_shape=pltpu.HBM((rows, D), BF),
        compiler_params=pltpu.CompilerParams(vmem_limit_bytes=VMEM_BYTES),
        name="pack_rows",
    )(ids, *front, *[pltpu.with_memory_space_constraint(w, pltpu.HBM) for w, _ in weights], *after)


def relay(x, *after):
    anywhere = pl.BlockSpec(memory_space=pl.ANY)
    return pl.pallas_call(
        lambda *refs: None,
        in_specs=[anywhere] * (1 + len(after)),
        out_specs=anywhere,
        out_shape=jax.ShapeDtypeStruct(x.shape, x.dtype),
        input_output_aliases={0: 0},
        name="relay",
    )(x, *after)


def toward(x, axis, bit):
    size = lax.axis_size(axis)
    return lax.ppermute(x, axis, [(i, i ^ bit) for i in range(size)])


def core_swap(x):
    return toward(x, "tp", 1)


def half_swap(x):
    return toward(x, "tp", 2)


def gather_segments(x):
    size = lax.axis_size("seg")
    spread = jnp.broadcast_to(x, (size,) + x.shape)
    return lax.all_to_all(spread, "seg", 0, 0, tiled=True).reshape(-1, x.shape[1])


def sum_over_all(x, gates):
    steps = [("tp", 1), ("tp", 2)] + [("seg", 1 << b) for b in range(lax.axis_size("seg").bit_length() - 1)]
    for i, (axis, bit) in enumerate(steps):
        arrived = toward(x, axis, bit)
        x = x + (relay(arrived, gates[i]) if i < len(gates) else arrived)
    return x


def local(
    tokens,
    mem_tokens,
    segno,
    gains,
    shifts,
    assoc,
    w_write,
    w_qkv,
    b_query_value,
    w_out,
    out_bias,
    w_fc,
    b_fc,
    w_proj,
    cot_tokens,
    cot_memory,
):
    mem_rows = mem_tokens.shape[0]
    block_rows = mem_rows + tokens.shape[2]
    own_rows = 2 * block_rows
    all_rows = 2 * own_rows
    segs = lax.axis_size("seg")
    levels = segs.bit_length() - 1
    me = lax.axis_index("seg")
    tp = lax.axis_index("tp")
    half, core = tp // 2, tp % 2
    slots = segs * NMEM
    key_dim = assoc.shape[1] // 2
    heads = w_qkv.shape[2] // (3 * HD)
    units = w_fc.shape[2]
    columns = w_write.shape[2]
    phi = 6 * key_dim
    wide_blocks = (D // segs) % 16 == 0 and (D // (4 * segs)) % 8 == 0
    ids = jnp.stack([me & 1, half, core, tp] + [(me >> level) & 1 for level in range(levels)]).astype(jnp.int32)

    def pick(pair, which):
        return lax.dynamic_index_in_dim(pair, which, 0, keepdims=False)

    both = jnp.concatenate([jnp.broadcast_to(mem_tokens, (2,) + mem_tokens.shape), tokens[:, 0]], axis=1)
    cots = jnp.concatenate([cot_memory[:, 0], cot_tokens[:, 0]], axis=1)
    bias_rows = jnp.concatenate([b_fc, b_query_value.reshape(1, -1), jnp.zeros((16 - LAYERS - 1, D), BF)])
    qkv_rows, write_rows = jnp.swapaxes(w_qkv, 1, 2), jnp.swapaxes(w_write, 1, 2)

    attention_weights_of = ((qkv_rows, 0), (write_rows, 1), (w_out, 1))
    few, q_rows = columns // 2, qkv_rows.shape[1] // 2
    first_got = half_swap(jnp.concatenate([pick(both, 1 - half), bias_rows]))
    biases = (first_got, 16, block_rows // 16)

    def run(body, outs, *items, **more):
        return phase(body, outs, ids, *items, **more)

    def fetch(packed, bit):
        part = half_swap(packed)
        return part, toward(part, "seg", 1 << bit)

    def places(core_id):
        within = jnp.arange(block_rows)
        rows = []
        for block in (core_id, core_id + 2):
            rows.append(
                jnp.where(
                    within < mem_rows,
                    block * mem_rows + within,
                    4 * mem_rows + block * (block_rows - mem_rows) + within - mem_rows,
                )
            )
        return jnp.concatenate(rows)

    pos = jnp.concatenate([places(core), places(1 - core)]).astype(jnp.int32)
    hide = jnp.where(pos[:, None] >= pos[None, :], 0.0, -1e30).astype(F32)
    number = lax.dynamic_index_in_dim(segno[:, 0], half, 0, keepdims=False)
    segment_of = jnp.arange(slots) // NMEM
    mask = jnp.broadcast_to(
        ((segment_of < me) & (segment_of >= me - number)).astype(F32)[None, :], (own_rows, slots)
    )
    own_f32, own_low = ((own_rows, D), F32), ((own_rows, D), BF)
    tail_low = ((NMEM, D), BF)
    small_rows = ((16, D), F32)
    more_f32 = ((own_rows + 16, D), F32)

    saved = []
    x, normed, tail = run(
        functools.partial(first_rows, sizes=()),
        [own_f32, own_low, tail_low],
        pick(both, half),
        first_got,
        (gains, 0),
        (shifts, 0),
    )
    packs = pack(ids, 0, attention_weights_of[:1]), pack(ids, 0, attention_weights_of[1:])
    (q_part, q_rest), (o_part, o_rest) = fetch(packs[0], 0), fetch(packs[1], 1)
    fetched = dict(
        qkv=(q_part, q_rest), write=((o_part, few, 0), (o_rest, few, 0)), out=((o_part, few, 1), (o_rest, few, 1))
    )
    tail = relay(tail, *packs)
    for l in range(LAYERS):
        out_bit = 1 - l
        if l:
            tail = relay(tail, fetched["fc"][0])
        tail = jnp.where(core == 1, tail, core_swap(tail))
        tails = gather_segments(tail)
        if l == 0:
            packs = pack(ids, 0, ((w_fc, 0),), after=(x,)), pack(ids, 0, ((w_proj, 1),), after=(x,))
            fetched["fc"], fetched["proj"] = fetch(packs[0], 0), fetch(packs[1], 1)
        scores, denom, values = run(
            functools.partial(write_scores, out_bit=out_bit),
            [((own_rows, slots), BF), ((own_rows, slots), F32), ((slots, 2 * columns), BF)],
            normed,
            tails,
            Far((assoc, l)),
            mask,
            Far((write_rows, l)),
            *far(*fetched["write"]),
            after=(fetched["proj"][0],) if l else (q_part, *packs),
        )
        mid, normed1, values = run(
            read_memory,
            [own_f32, own_low, ((slots, D), BF)],
            x,
            scores,
            values,
            core_swap(values),
            denom,
            (gains, l),
            (shifts, l),
        )
        normed1_core = core_swap(normed1)
        if l == 0:
            pack_next = pack(ids, 1, [(w, 0) for w, _ in attention_weights_of], after=(normed1,))
            next_attention = fetch(pack_next, 0)
        part, sent, packed0, packed1, mixed0, mixed1 = run(
            functools.partial(attention, layer=l, out_bit=out_bit),
            [own_f32, own_low]
            + [((all_rows, 3 * HD * heads), BF)] * 2
            + [((all_rows, HD * heads), BF)] * 2,
            normed1,
            normed1_core,
            *far((qkv_rows, l), (w_out, l), *fetched["qkv"], *fetched["out"]),
            b_query_value[l : l + 1],
            biases,
            hide,
            scratch=[((2 * heads, 3, all_rows, HD), BF), ((2 * heads, 1, all_rows, HD), BF)],
            after=() if l else (fetched["fc"][0], pack_next),
        )
        after, normed2 = run(
            after_attention,
            [own_f32, own_low],
            mid,
            part,
            core_swap(sent),
            (out_bias, l),
            (gains, l),
            (shifts, l),
        )
        normed2_core = core_swap(normed2)
        if l == 0:
            packs = pack(ids, 1, ((w_fc, 0),), after=(normed2,)), pack(ids, 1, ((w_proj, 1),), after=(normed2,))
            next_fc, next_proj = fetch(packs[0], 0), fetch(packs[1], 1)
        part, sent, hidden, slope0, slope1, acts = run(
            functools.partial(feed_forward, layer=l),
            [own_f32, own_low]
            + [((all_rows, units), BF)] * 3
            + [((2 * all_rows + NMEM, D), BF, True)],
            normed2,
            normed2_core,
            *far((w_fc, l), (w_proj, l), *fetched["fc"], *fetched["proj"]),
            b_fc[l : l + 1],
            biases,
            normed1,
            tail,
            after=() if l else packs,
        )
        saved.append(
            dict(
                x=x, normed=normed, tail=tail, tails=tails, scores=scores, denom=denom, values=values, mid=mid,
                normed1=(normed1, normed1_core), packed=(packed0, packed1), mixed=(mixed0, mixed1), after=after,
                normed2=(normed2, normed2_core), hidden=hidden, slope=(slope0, slope1), acts=acts, fetched=fetched,
            )
        )
        if l == 0:
            x, normed, tail = run(
                after_feed,
                [own_f32, own_low, tail_low],
                after,
                part,
                core_swap(sent),
                (out_bias, l),
                (gains, l + 1),
                (shifts, l + 1),
                after=(next_attention[0],),
            )
            place = q_rows // few
            fetched = dict(
                qkv=[(m, q_rows, 0) for m in next_attention],
                write=[(m, few, place) for m in next_attention],
                out=[(m, few, place + 1) for m in next_attention],
                fc=next_fc,
                proj=next_proj,
            )
        else:
            mine, given = run(
                after_last, [((block_rows, D), BF, True)] * 2, after, part, core_swap(sent), (out_bias, l)
            )

    def both_batches(mine, got):
        return jnp.where(half == 0, jnp.stack([mine, got]), jnp.stack([got, mine]))

    result = both_batches(mine, half_swap(given))
    out_memory = result[:, :mem_rows][:, None]
    out_tokens = result[:, mem_rows:][:, None]

    cot_own, cot_got = pick(cots, half), half_swap(pick(cots, 1 - half))
    grad_low = jnp.where(half == 0, jnp.concatenate([cot_own, cot_got]), jnp.concatenate([cot_got, cot_own]))
    grad = grad_low
    cut_rows = D * (segs // 2) // segs
    early = [None] * LAYERS

    block, folded = D // segs, D // (2 * segs)

    def arrival(level, pair, order):
        bits = list(order) + list(range(2, levels))
        return toward(pair[1], "seg", 1 << bits[level - 1])

    def cut(level, pair, order, rows, after=(), got=None):
        bits = list(order) + list(range(2, levels))
        left = [b for b in range(levels) if b not in bits[:level]]
        keep, send = pair
        got = arrival(level, pair, order) if got is None else got
        return run(
            functools.partial(next_cut, bit=bits[level], place=left.index(bits[level]), rows=rows),
            [((keep.shape[0] // 2, keep.shape[1]), BF)] * 2,
            keep,
            got,
            kernel=wide_blocks,
            after=after,
        )

    def end_of(level, pair, order, rows, after=()):
        while level < levels:
            pair = cut(level, pair, order, rows, after)
            level += 1
        bits = list(order) + list(range(2, levels))
        return pair[0], toward(pair[1], "seg", 1 << bits[-1])

    def feed_gradients(l, s, d_pre, sent_got, rows, after):
        orders = FEED_ORDERS[l]
        shapes = [((cut_rows, D), BF, True)] * 4 if len(orders) == 2 else [((cut_rows, D + units), BF, True)] * 2
        got, got_core = s["acts"]
        return run(
            functools.partial(feed_grads, segs=segs, orders=orders),
            shapes + [small_rows],
            *far(*s["normed2"], (got, own_rows, 3), (got_core, own_rows, 3)),
            *far(d_pre, (sent_got[0], all_rows, 0)),
            *far(*rows, (sent_got[0], own_rows, 2), (sent_got[1], own_rows, 2)),
            *far(s["hidden"], (got, all_rows, 0)),
            kernel=wide_blocks,
            after=after,
        )

    def attention_gradients(l, s, d_packed, sent_got, rows, after):
        got, got_core = s["acts"]
        return run(
            functools.partial(attention_grads, segs=segs, order=ATT_ORDERS[l]),
            [((cut_rows, 3 * HD * heads + HD * heads), BF, True)] * 2 + [small_rows],
            *far(*s["normed1"], (got, own_rows, 2), (got_core, own_rows, 2)),
            *far(d_packed, (sent_got[0], all_rows, 0)),
            *far(*rows, (sent_got[0], own_rows, 2), (sent_got[1], own_rows, 2)),
            Far(s["mixed"][0]),
            kernel=wide_blocks,
            after=after,
        )

    def memory_gradients(l, s, assoc_keep, assoc_got, vals_own, after):
        return run(
            functools.partial(memory_grads, segs=segs, order=MEM_ORDERS[l]),
            [((cut_rows // 2, D), BF, True)] * 2,
            *far(assoc_keep, assoc_got, s["tail"], (s["acts"][0], NMEM, 2 * all_rows // NMEM), vals_own),
            kernel=wide_blocks,
            after=after,
        )

    def with_core(sent, *gate):
        got = relay(half_swap(sent), *gate)
        return got, core_swap(got)

    for s in saved:
        s["acts"] = with_core(s["acts"], s["normed2"][0])

    waiting = None
    pins = (mine, saved[0]["acts"][0])
    for l in reversed(range(LAYERS)):
        s, out_bit = saved[l], 1 - l
        grad_core = core_swap(grad_low)
        feed_rows = (grad_low, grad_core)
        part, sent, d_pre, feed_sent = run(
            feed_back,
            [own_f32, own_low, ((all_rows, units), BF), ((all_rows + own_rows, D), BF, True)],
            grad_low,
            grad_core,
            *far((w_fc, l), (w_proj, l), *s["fetched"]["fc"], *s["fetched"]["proj"], *s["slope"]),
            after=pins,
        )
        pins = ()
        if waiting:
            *feed_pair, small_f = feed_gradients(1, *waiting["feed"], (sent,))
            early[1] = early[1] + small_f
            pins = (feed_pair[0],)
        d_after, d_after_low = run(
            after_feed_back,
            [more_f32, own_low],
            grad,
            part,
            core_swap(sent),
            s["after"],
            (gains, l),
            after=pins,
        )
        d_after_core = core_swap(d_after_low)
        attention_rows = (d_after_low, d_after_core)
        pins = ()
        if waiting:
            later, later_packed, later_sent, later_rows = waiting["attention"]
            later_got = with_core(later_sent, part)
            *att_pair, small_g = attention_gradients(1, later, later_packed, later_got, later_rows, (d_after_low,))
            early[1] = early[1] + small_g
            pins = (att_pair[0],)
            later_feed = feed_pair
        part, sent, d_packed, attention_sent = run(
            functools.partial(attention_back, out_bit=out_bit),
            [own_f32, own_low, ((all_rows, 3 * HD * heads), BF), ((all_rows + own_rows, D), BF, True)],
            d_after_low,
            d_after_core,
            *far((qkv_rows, l), (w_out, l), *s["fetched"]["qkv"], *s["fetched"]["out"]),
            *far(*s["packed"], s["mixed"][1]),
            hide,
            after=pins,
            scratch=[
                ((2 * heads, 3, all_rows, HD), BF),
                ((2 * heads, 1, all_rows, HD), BF),
                ((2 * heads, 3, all_rows, HD), BF),
            ],
        )
        if waiting:
            att_next = cut(1, att_pair, ATT_ORDERS[1], block, (sent,))
            feed_next = cut(1, later_feed, FEED_ORDERS[1][0], block, (att_next[0],))
            feed_got = with_core(feed_sent, d_after_low)
            pins = (feed_next[0], feed_got[0])
        else:
            pins = (s["acts"][0],)
        d_mid, d_scores, d_keys, y_mine, y_sent = run(
            after_attention_back,
            [
                more_f32,
                ((own_rows, slots), BF),
                ((slots, key_dim), BF),
                ((slots, key_dim // 2 + 2 * columns), F32),
                ((slots, key_dim // 2 + 2 * columns), BF),
            ],
            d_after,
            part,
            core_swap(sent),
            *far(s["mid"], (gains, l), s["scores"], s["values"], s["denom"], mask, s["normed"], s["tails"], (assoc, l)),
            after=pins,
        )
        written = (y_mine + wide(core_swap(y_sent))).astype(BF)
        written_all = lax.all_to_all(written.reshape(segs, NMEM, -1), "seg", 0, 0, tiled=True).reshape(slots, -1)
        d_norm, assoc_keep, assoc_send = run(
            functools.partial(read_back, segs=segs),
            [own_f32, ((D // 2, 2 * key_dim), BF), ((D // 2, 2 * key_dim), BF)],
            d_scores,
            *far(s["normed"], s["tails"], (assoc, l)),
            d_keys,
            kernel=wide_blocks,
            after=(written,),
        )
        pins = (d_norm,)
        if l == 0:
            mem_later = memory_gradients(1, *waiting["memory"], (d_norm,))
            attention_got = with_core(attention_sent, d_mid)
            att_got = arrival(2, att_next, ATT_ORDERS[1])
            feed_got_next = arrival(2, feed_next, FEED_ORDERS[1][0])
            pins = (mem_later[0],)
        d_tail, vals_own, vals_other = run(
            functools.partial(tail_back, out_bit=out_bit),
            [((NMEM, D), F32)] + [((NMEM, columns), BF)] * 2,
            written_all,
            *far((assoc, l), (write_rows, l), *s["fetched"]["write"]),
            after=pins,
        )
        assoc_keep, assoc_send = run(
            functools.partial(assoc_second, segs=segs),
            [((D // 4, 2 * key_dim), BF, True), ((D // 4 + NMEM, 2 * key_dim), BF, True)],
            assoc_keep,
            core_swap(assoc_send),
            vals_other,
            kernel=wide_blocks,
        )
        if l == 0:
            *feed_pair, small_f = feed_gradients(
                0, s, d_pre, feed_got, feed_rows, (d_tail, attention_got[0], att_got, feed_got_next)
            )
        d_x, d_x_low = run(
            layer_end_back,
            [more_f32, own_low],
            *far(d_mid, d_norm),
            d_tail,
            core_swap(d_tail),
            *far(s["x"], (gains, l)),
            after=(assoc_keep,) if l else (assoc_keep, feed_pair[0]),
        )
        early[l] = d_x[own_rows:]
        memory = (s, assoc_keep, half_swap(assoc_send), vals_own)
        pins = ()
        if l > 0:
            waiting = dict(
                feed=(s, d_pre, with_core(feed_sent, d_x), feed_rows),
                attention=(s, d_packed, attention_sent, attention_rows),
                memory=memory,
            )
        else:
            feed_next = cut(2, feed_next, FEED_ORDERS[1][0], block, (d_x,), feed_got_next)
            att_next = cut(2, att_next, ATT_ORDERS[1], block, (feed_next[0],), att_got)
            *att_pair, small_g = attention_gradients(0, s, d_packed, attention_got, attention_rows, (att_next[0],))
            early[0] = early[0] + small_f + small_g
            fc_got = arrival(1, feed_pair[:2], FEED_ORDERS[0][0])
            proj_got = arrival(1, feed_pair[2:], FEED_ORDERS[0][1])
            fc = cut(1, feed_pair[:2], FEED_ORDERS[0][0], block, (att_pair[0],), fc_got)
            proj = cut(1, feed_pair[2:], FEED_ORDERS[0][1], block, (fc[0],), proj_got)
            mem_pair = memory_gradients(0, *memory, (proj[0],))
        grad, grad_low = d_x, d_x_low

    fc_order, proj_order = FEED_ORDERS[0]
    later_sums = [end_of(3, feed_next, FEED_ORDERS[1][0], block), end_of(3, att_next, ATT_ORDERS[1], block)]
    gates = [proj[0], mem_pair[0]]
    mem_next = cut(1, mem_later, MEM_ORDERS[1], folded, (mem_pair[0],))
    att_pair = cut(1, att_pair, ATT_ORDERS[0], block, (mem_next[0],))
    gates.append(att_pair[0])
    fc = cut(2, fc, fc_order, block, (att_pair[0], later_sums[0][1]))
    proj = cut(2, proj, proj_order, block, (fc[0],))
    mem_pair = cut(1, mem_pair, MEM_ORDERS[0], folded, (proj[0],))
    gates.append(mem_pair[0])
    mem_next = cut(2, mem_next, MEM_ORDERS[1], folded, (mem_pair[0],))
    att_pair = cut(2, att_pair, ATT_ORDERS[0], block, (mem_next[0], later_sums[1][1]))
    fc, proj = end_of(3, fc, fc_order, block), end_of(3, proj, proj_order, block)
    mem_pair = cut(2, mem_pair, MEM_ORDERS[0], folded, (att_pair[0], fc[1]))
    later_sums.append(end_of(3, mem_next, MEM_ORDERS[1], folded))
    last_sums = [fc, proj, end_of(3, att_pair, ATT_ORDERS[0], block), end_of(3, mem_pair, MEM_ORDERS[0], folded)]

    grad = grad[:own_rows]
    mine = pick(grad.reshape(2, block_rows, D), half)
    given = half_swap(pick(grad_low.reshape(2, block_rows, D), 1 - half))
    grad_tokens = both_batches(mine, wide(given))[:, mem_rows:][:, None]

    kept = grad.reshape(2, block_rows, D)[:, :mem_rows]
    mem_full = lax.dynamic_update_slice(jnp.zeros((2, 2, mem_rows, D), F32), kept[:, None], (0, core, 0, 0))
    smalls = sum_over_all(jnp.concatenate(early + [mem_full.reshape(-1, D)]), gates)

    at = me * 4 + tp
    own = lax.dynamic_slice_in_dim(smalls, at * (D // (4 * segs)), D // (4 * segs), axis=1)
    own_layers = own[: 16 * LAYERS].reshape(LAYERS, 16, -1)

    def own_entries(first, last):
        flat = smalls[: 16 * LAYERS].reshape(LAYERS, 16, D)[:, first:last].reshape(LAYERS, -1)
        size = flat.shape[1] // (4 * segs)
        return lax.dynamic_slice_in_dim(flat, at * size, size, axis=1)

    few, many = D // (4 * segs), D // segs
    qkv_columns = 3 * HD * heads
    g_fc, g_proj = run(
        feed_end,
        [((LAYERS, many, units), F32), ((LAYERS, many, units), F32)],
        *last_sums[0],
        *last_sums[1],
        *later_sums[0],
        kernel=wide_blocks,
    )
    g_qkv, g_out = run(
        functools.partial(attention_end, columns=qkv_columns),
        [((LAYERS, many, qkv_columns), F32), ((LAYERS, many, columns), F32)],
        *last_sums[2],
        *later_sums[1],
        kernel=wide_blocks,
    )
    g_assoc, g_write = run(
        memory_end,
        [((LAYERS, few, D), F32), ((LAYERS, many, columns), F32)],
        *last_sums[3],
        *later_sums[2],
        kernel=wide_blocks,
    )
    return (
        out_tokens,
        out_memory,
        grad_tokens,
        own[16 * LAYERS :],
        own_layers[:, 0:3],
        own_layers[:, 3:6],
        jnp.swapaxes(g_assoc, 1, 2),
        g_write,
        g_qkv,
        own_entries(12, 14),
        jnp.swapaxes(g_out, 1, 2),
        own_layers[:, 6:8],
        g_fc,
        own_entries(8, 12),
        jnp.swapaxes(g_proj, 1, 2),
    )


def solution(mesh):
    return jax.shard_map(
        local,
        mesh=mesh,
        in_specs=(
            P(None, "seg", "tp", None),
            P("tp", None),
            P(None, "seg"),
            P(),
            P(),
            P(),
            P(None, None, "tp"),
            P(None, None, "tp"),
            P(None, "tp"),
            P(None, "tp", None),
            P(),
            P(None, None, "tp"),
            P(None, "tp"),
            P(None, "tp", None),
            P(None, "seg", "tp", None),
            P(None, "seg", "tp", None),
        ),
        out_specs=(
            P(None, "seg", "tp", None),
            P(None, "seg", "tp", None),
            P(None, "seg", "tp", None),
            P(None, ("seg", "tp")),
            P(None, None, ("seg", "tp")),
            P(None, None, ("seg", "tp")),
            P(None, None, ("seg", "tp")),
            P(None, "seg", "tp"),
            P(None, "seg", "tp"),
            P(None, ("seg", "tp")),
            P(None, "tp", "seg"),
            P(None, None, ("seg", "tp")),
            P(None, "seg", "tp"),
            P(None, ("seg", "tp")),
            P(None, "tp", "seg"),
        ),
        check_vma=False,
    )
```

```python
import functools

import jax
import jax.numpy as jnp
from jax import lax
from jax.experimental import pallas as pl
from jax.experimental.pallas import tpu as pltpu
from jax.sharding import PartitionSpec as P

D = 768
HD = 64
NMEM = 16
LAYERS = 2
BF = jnp.bfloat16
F32 = jnp.float32
VMEM_BYTES = 40 * 1024 * 1024


class Far:
    def __init__(self, item):
        self.item = item


def far(*items):
    return [Far(item) for item in items]


IN_HBM = []


def lives_in_hbm(x):
    IN_HBM.append(x)
    return x


def settled(x):
    if any(x is known for known in IN_HBM):
        return pltpu.with_memory_space_constraint(x, pltpu.HBM)
    return x


def scalars():
    seg, tp = lax.axis_index("seg"), lax.axis_index("tp")
    return [seg & 1, tp // 2, tp % 2, tp] + [(seg >> b) & 1 for b in range(lax.axis_size("seg").bit_length() - 1)]


def value_of(item):
    if isinstance(item, Far):
        item = item.item
    if not isinstance(item, tuple):
        return item
    if len(item) == 3:
        return item[0][item[1] * item[2] : item[1] * (item[2] + 1)]
    return item[0][item[1]]


def phase(body, outs, ids, *items, kernel=True, after=(), scratch=()):
    if not kernel:
        return body(False, ids, *[value_of(item) for item in items])
    arrays, specs = [], []
    for item in items:
        if isinstance(item, Far):
            item = item.item
            where = functools.partial(pltpu.with_memory_space_constraint, memory_space=pltpu.HBM)
            item = (where(item[0]), *item[1:]) if isinstance(item, tuple) else where(item)
        if isinstance(item, tuple) and len(item) == 3:
            array, rows, at = item
            arrays.append(array)
            specs.append(pl.BlockSpec((rows, array.shape[1]), functools.partial(lambda at, i: (at, 0), at)))
        elif isinstance(item, tuple):
            array, layer = item
            rest = array.shape[1:]
            arrays.append(array)
            specs.append(
                pl.BlockSpec((None,) + rest, functools.partial(lambda l, n, i: (l,) + (0,) * n, layer, len(rest)))
            )
        else:
            arrays.append(item)
            specs.append(pl.BlockSpec(item.shape, functools.partial(lambda n, i: (0,) * n, item.ndim)))
    count = len(arrays)
    for array in after:
        arrays.append(settled(array))
        specs.append(pl.BlockSpec(memory_space=pl.ANY))

    def run(*refs):
        spaces = refs[len(arrays) + len(outs) :]
        results = body(True, scalars(), *spaces, *[r[...] for r in refs[:count]])
        for ref, result in zip(refs[len(arrays) :], results):
            ref[...] = result

    results = pl.pallas_call(
        run,
        grid=(1,),
        out_shape=[pltpu.HBM(*out[:2]) if len(out) == 3 else jax.ShapeDtypeStruct(*out) for out in outs],
        in_specs=specs,
        out_specs=[pl.BlockSpec(out[0], functools.partial(lambda n, i: (0,) * n, len(out[0]))) for out in outs],
        scratch_shapes=[pltpu.VMEM(s, t) for s, t in scratch],
        compiler_params=pltpu.CompilerParams(vmem_limit_bytes=VMEM_BYTES),
        name=getattr(body, "func", body).__name__,
    )(*arrays)
    return [lives_in_hbm(r) if len(out) == 3 else r for out, r in zip(outs, results)]


def wide(v):
    return v.astype(F32)


def dot(a, b):
    return lax.dot_general(a, b, (((1,), (0,)), ((), ())), preferred_element_type=F32)


def dot_nt(a, b):
    return lax.dot_general(a, b, (((1,), (1,)), ((), ())), preferred_element_type=F32)


def dot_tn(a, b):
    return lax.dot_general(a, b, (((0,), (0,)), ((), ())), preferred_element_type=F32)


def turn(v, by, native):
    if native:
        return pltpu.roll(v, (-by) % v.shape[1], 1)
    return jnp.roll(v, -by, axis=1)


def rows_of(*pieces):
    return jnp.concatenate(pieces, axis=0)


def columns_of(*pieces):
    return jnp.concatenate(pieces, axis=1)


def ordered(flag, first, second):
    return jnp.where(flag == 1, second, first), jnp.where(flag == 1, first, second)


def split_blocks(total, rows, flag, place=0):
    keep, send = [], []
    step = rows << place
    for at in range(0, total.shape[0], 2 * step):
        mine, others = ordered(flag, total[at : at + step], total[at + step : at + 2 * step])
        keep.append(mine)
        send.append(others)
    return rows_of(*keep), rows_of(*send)


def place_row(row, at, first, count=16):
    index = lax.broadcasted_iota(jnp.int32, (count, row.shape[1]), 0)
    return jnp.where(index == first + at, jnp.broadcast_to(row, (count, row.shape[1])), 0.0)


ODD, HALF, CORE, TP, BIT = 0, 1, 2, 3, 4
FEED_ORDERS = (((0, 1), (1, 0)), ((0, 1),))
ATT_ORDERS = ((0, 1), (1, 0))
MEM_ORDERS = ((1, 0), (1, 0))


def norm_parts(rows):
    centred = rows - jnp.mean(rows, axis=-1, keepdims=True)
    rstd = lax.rsqrt(jnp.mean(centred * centred, axis=-1, keepdims=True) + 1e-05)
    return centred * rstd, rstd


def norm_rows(rows, gain, shift):
    return norm_parts(rows)[0] * wide(gain) + wide(shift)


def norm_back(rows, gain, grad):
    hat, rstd = norm_parts(rows)
    d_hat = grad * wide(gain)
    d_rows = rstd * (
        d_hat
        - jnp.mean(d_hat, axis=-1, keepdims=True)
        - hat * jnp.mean(d_hat * hat, axis=-1, keepdims=True)
    )
    return d_rows, jnp.sum(grad * hat, axis=0, keepdims=True), jnp.sum(grad, axis=0, keepdims=True)


def paired(v):
    rest = jnp.log1p(jnp.exp(-jnp.abs(v)))
    return columns_of(jnp.maximum(v, 0.0) + rest, jnp.maximum(-v, 0.0) + rest)


def features(v, native):
    c = paired(v)
    return columns_of(*[c * turn(c, k, native) for k in (1, 2, 3)])


def features_back(v, grad, native):
    c = paired(v)
    size = c.shape[1]
    d_c = jnp.zeros_like(c)
    for k in (1, 2, 3):
        part = grad[:, (k - 1) * size : k * size]
        d_c = d_c + part * turn(c, k, native) + turn(part * c, -k, native)
    half = v.shape[1]
    up = 1.0 / (1.0 + jnp.exp(-v))
    return d_c[:, :half] * up - d_c[:, half:] * (1.0 - up)


def other_rows(odd, part, rest, first=0, last=None):
    return rows_of(*ordered(odd, part[first:last], rest[first:last]))


def first_rows(native, ids, own, got, gains, shifts, sizes):
    count = own.shape[0]
    x = wide(rows_of(*ordered(ids[HALF], own, got[:count])))
    normed = norm_rows(x, gains[0:1], shifts[0:1]).astype(BF)
    pieces, at = [], count
    for size in sizes:
        pieces.append(got[at : at + size])
        at += size
    return (x, normed, normed[normed.shape[0] - NMEM :], *pieces)


def read_keys_of(normed, assoc):
    return wide(dot_nt(normed, assoc[: assoc.shape[0] // 2]).astype(BF))


def written_keys_of(tails, assoc):
    return dot_nt(tails, assoc[assoc.shape[0] // 2 :])


def write_scores(native, ids, normed, tails, assoc, mask, w_write, part, rest, out_bit):
    feat_q = features(read_keys_of(normed, assoc), native).astype(BF)
    feat_k = features(written_keys_of(tails, assoc), native).astype(BF)
    scores = dot_nt(feat_q, feat_k) * mask
    denom = jnp.sum(scores, axis=1, keepdims=True) + 1.0
    others = other_rows(ids[BIT + out_bit], part, rest)
    values = columns_of(*ordered(ids[HALF], dot_nt(tails, w_write), dot_nt(tails, others)))
    return (scores.astype(BF), jnp.broadcast_to(denom, mask.shape), values.astype(BF))


def read_memory(native, ids, x, scores, values, values_core, denom, gains, shifts):
    left, right = ordered(ids[CORE], values, values_core)
    width = left.shape[1] // 2
    values = columns_of(left[:, :width], right[:, :width], left[:, width:], right[:, width:])
    read = (dot(scores, values) / denom[:, 0:1]).astype(BF)
    mid = x + wide(read)
    return (mid, norm_rows(mid, gains[1:2], shifts[1:2]).astype(BF), values)


def head_parts(packed, head):
    at = 3 * HD * head
    return packed[:, at : at + HD], packed[:, at + HD : at + 2 * HD], packed[:, at + 2 * HD : at + 3 * HD]


def head_probs(queries, keys, hide):
    scores = dot_nt(queries, keys) * 0.125 + hide
    weights = jnp.exp(scores - jnp.max(scores, axis=1, keepdims=True))
    return weights / jnp.sum(weights, axis=1, keepdims=True)


def head_bias(row):
    row = wide(row)
    blank = jnp.zeros((1, HD), F32)
    pieces = []
    for at in range(0, row.shape[1], 2 * HD):
        pieces += [row[:, at : at + HD], blank, row[:, at + HD : at + 2 * HD]]
    return columns_of(*pieces)


def attention_weights(ids, out_bit, w_qkv, w_out, part, rest, out_part, out_rest):
    return (w_qkv, w_out), (other_rows(ids[BIT], part, rest), other_rows(ids[BIT + out_bit], out_part, out_rest))


def put_heads(space, at, packed, parts):
    for column in range(packed.shape[1] // HD):
        space[at + column // parts, column % parts] = packed[:, HD * column : HD * (column + 1)]


def take_heads(space, first, last):
    return columns_of(*[space[head, part] for head in range(first, last) for part in range(space.shape[1])])


def attention(native, ids, heads, mixed_heads, own, other, w_qkv, w_out, part, rest, out_part, out_rest, bias, biases, hide, layer, out_bit):
    rows = rows_of(own, other)
    half = own.shape[0]
    width = bias.shape[1]
    other_bias = biases[LAYERS : LAYERS + 1, layer * width : (layer + 1) * width]
    weights = attention_weights(ids, out_bit, w_qkv, w_out, part, rest, out_part, out_rest)
    count = width // (2 * HD)
    packs = []
    for block, ((w, _), row) in enumerate(zip(weights, (bias, other_bias))):
        packed = (dot_nt(rows, w) + head_bias(row)).astype(BF)
        put_heads(heads, block * count, packed, 3)
        packs.append(packed)

    def one(head, carried):
        probs = head_probs(heads[head, 0], heads[head, 1], hide)
        mixed_heads[head, 0] = dot(probs.astype(BF), heads[head, 2]).astype(BF)
        return carried

    lax.fori_loop(0, 2 * count, one, 0)
    total, mixes = 0.0, []
    for block, (_, o) in enumerate(weights):
        mixed = take_heads(mixed_heads, block * count, (block + 1) * count)
        total = total + dot(mixed, o)
        mixes.append(mixed)
    return (total[:half], total[half:].astype(BF), *packs, *mixes)


def after_attention(native, ids, mid, part, arrived, bias, gains, shifts):
    after = mid + part + wide(arrived) + wide(bias[0:1])
    return (after, norm_rows(after, gains[2:3], shifts[2:3]).astype(BF))


def gelu_both(v):
    inner = 0.7978845608028654 * (v + 0.044715 * v * v * v)
    t = jnp.tanh(inner)
    slope = 0.5 * (1.0 + t) + 0.5 * v * (1.0 - t * t) * 0.7978845608028654 * (1.0 + 3 * 0.044715 * v * v)
    return 0.5 * v * (1.0 + t), slope


def feed_weights(ids, w_fc, w_proj, part, rest, part_proj, rest_proj):
    return (w_fc, w_proj), (other_rows(ids[BIT], part, rest), other_rows(ids[BIT + 1], part_proj, rest_proj))


def feed_forward(
    native, ids, own, other, w_fc, w_proj, part, rest, part_proj, rest_proj, bias, biases, normed1, tail, layer
):
    rows = rows_of(own, other)
    half = own.shape[0]
    other_bias = biases[layer : layer + 1]
    total, hiddens, slopes = 0.0, [], []
    for (w, p), row in zip(
        feed_weights(ids, w_fc, w_proj, part, rest, part_proj, rest_proj), (bias, other_bias)
    ):
        hidden, slope = gelu_both(dot(rows, w) + wide(row))
        hidden = hidden.astype(BF)
        total = total + dot(hidden, p)
        hiddens.append(hidden)
        slopes.append(slope.astype(BF))
    return (total[:half], total[half:].astype(BF), hiddens[0], *slopes, rows_of(hiddens[1], normed1, own, tail))


def after_feed(native, ids, after, part, arrived, bias, next_gains, next_shifts):
    x = after + part + wide(arrived) + wide(bias[1:2])
    normed = norm_rows(x, next_gains[0:1], next_shifts[0:1]).astype(BF)
    return (x, normed, normed[normed.shape[0] - NMEM :])


def after_last(native, ids, after, part, arrived, bias):
    x = (after + part + wide(arrived) + wide(bias[1:2])).astype(BF)
    half = x.shape[0] // 2
    return ordered(ids[HALF], x[:half], x[half:])


def feed_back(native, ids, own, other, w_fc, w_proj, part, rest, part_proj, rest_proj, slope0, slope1):
    grads = rows_of(own, other)
    half = own.shape[0]
    total, saved = 0.0, []
    for (w, p), slope in zip(
        feed_weights(ids, w_fc, w_proj, part, rest, part_proj, rest_proj), (slope0, slope1)
    ):
        d_pre = (dot_nt(grads, p) * wide(slope)).astype(BF)
        total = total + dot_nt(d_pre, w)
        saved.append(d_pre)
    return (total[:half], total[half:].astype(BF), saved[0], rows_of(saved[1], own))


def after_feed_back(native, ids, grad, part, arrived, after, gains):
    grad = wide(grad[: after.shape[0]])
    d_rows, d_gain, d_shift = norm_back(after, gains[2:3], part + wide(arrived))
    d_after = grad + d_rows
    d_bias = jnp.sum(grad, axis=0, keepdims=True)
    small = place_row(d_gain, 2, 0) + place_row(d_shift, 5, 0) + place_row(d_bias, 7, 0)
    return (rows_of(d_after, small), d_after.astype(BF))


def attention_back(
    native, ids, heads, d_mixed_heads, d_heads, own, other, w_qkv, w_out, part, rest, out_part, out_rest, packed0, packed1, mixed1, hide, out_bit
):
    grads = rows_of(own, other)
    half = own.shape[0]
    count = packed0.shape[1] // (3 * HD)
    weights = attention_weights(ids, out_bit, w_qkv, w_out, part, rest, out_part, out_rest)
    for block, ((_, o), packed) in enumerate(zip(weights, (packed0, packed1))):
        put_heads(heads, block * count, packed, 3)
        put_heads(d_mixed_heads, block * count, dot_nt(grads, o).astype(BF), 1)

    def one(head, carried):
        queries, keys, values = heads[head, 0], heads[head, 1], heads[head, 2]
        dm = d_mixed_heads[head, 0]
        probs = head_probs(queries, keys, hide)
        d_probs = dot_nt(dm, values)
        d_scores = (probs * (d_probs - jnp.sum(d_probs * probs, axis=1, keepdims=True))).astype(BF)
        d_heads[head, 0] = (dot(d_scores, keys) * 0.125).astype(BF)
        d_heads[head, 1] = (dot_tn(d_scores, queries) * 0.125).astype(BF)
        d_heads[head, 2] = dot_tn(probs.astype(BF), dm).astype(BF)
        return carried

    lax.fori_loop(0, 2 * count, one, 0)
    total, saved = 0.0, []
    for block, (w, _) in enumerate(weights):
        d_packed = take_heads(d_heads, block * count, (block + 1) * count)
        total = total + dot(d_packed, w)
        saved.append(d_packed)
    return (total[:half], total[half:].astype(BF), saved[0], rows_of(columns_of(saved[1], mixed1), own))


def after_attention_back(native, ids, d_after, part, arrived, mid, gains, scores, values, denom, mask, normed, tails, assoc):
    d_after, small = d_after[: mid.shape[0]], d_after[mid.shape[0] :]
    d_rows, d_gain, d_shift = norm_back(mid, gains[1:2], part + wide(arrived))
    d_mid = d_after + d_rows
    d_bias = jnp.sum(d_after, axis=0, keepdims=True)
    small = small + place_row(d_gain, 1, 0) + place_row(d_shift, 4, 0) + place_row(d_bias, 6, 0)
    scale = 1.0 / denom[:, 0:1]
    d_numer = (d_mid * scale).astype(BF)
    d_denom = -jnp.sum(d_mid * dot(scores, values), axis=1, keepdims=True) * scale * scale
    d_scores = ((dot_nt(d_numer, values) + d_denom) * mask).astype(BF)
    feat_q = features(read_keys_of(normed, assoc), native).astype(BF)
    d_keys = features_back(written_keys_of(tails, assoc), dot_tn(d_scores, feat_q), native)
    d_values = dot_tn(scores, d_numer)
    cut, width = d_keys.shape[1] // 2, d_values.shape[1] // 4
    mine, others = ordered(
        ids[CORE],
        columns_of(d_keys[:, :cut], d_values[:, :width], d_values[:, 2 * width : 3 * width]),
        columns_of(d_keys[:, cut:], d_values[:, width : 2 * width], d_values[:, 3 * width :]),
    )
    return (rows_of(d_mid, small), d_scores, d_keys.astype(BF), mine, others.astype(BF))


def read_back(native, ids, d_scores, normed, tails, assoc, d_tail_keys, segs):
    feat_k = features(written_keys_of(tails, assoc), native).astype(BF)
    d_keys = features_back(read_keys_of(normed, assoc), dot(d_scores, feat_k), native).astype(BF)
    d_norm = dot(d_keys, assoc[: assoc.shape[0] // 2])
    product = columns_of(dot_tn(normed, d_keys), dot_tn(tails, d_tail_keys))
    keep, send = split_blocks(product, product.shape[0] // (4 * segs), ids[CORE])
    return (d_norm, keep.astype(BF), send.astype(BF))


def assoc_second(native, ids, keep, arrived, values, segs):
    total = wide(keep) + wide(arrived)
    keep, send = split_blocks(total, total.shape[0] // (2 * segs), ids[HALF])
    blank = jnp.zeros((values.shape[0], send.shape[1] - values.shape[1]), BF)
    return (keep.astype(BF), rows_of(send.astype(BF), columns_of(values, blank)))


def tail_back(native, ids, arrived, assoc, w_write, part, rest, out_bit):
    total = wide(arrived[:NMEM])
    for at in range(NMEM, arrived.shape[0], NMEM):
        total = total + wide(arrived[at : at + NMEM])
    cut = total.shape[1] // 3
    low = total.astype(BF)
    own, other = ordered(ids[HALF], low[:, cut : 2 * cut], low[:, 2 * cut :])
    size = assoc.shape[0] // 4
    used, _ = ordered(ids[CORE], assoc[2 * size : 3 * size], assoc[3 * size :])
    others = other_rows(ids[BIT + out_bit], part, rest)
    d_tail = dot(low[:, :cut], used) + dot(own, w_write) + dot(other, others)
    return (d_tail, own, other)


def layer_end_back(native, ids, d_mid, d_norm, d_tail, d_tail_core, x, gains):
    rows = d_norm.shape[0]
    d_mid, small = d_mid[:rows], d_mid[rows:]
    added = jnp.where(ids[CORE] == 1, d_tail + d_tail_core, 0.0)
    d_norm = rows_of(d_norm[: rows - NMEM], d_norm[rows - NMEM :] + added)
    d_rows, d_gain, d_shift = norm_back(x, gains[0:1], d_norm)
    d_x = d_mid + d_rows
    return (rows_of(d_x, small + place_row(d_gain, 0, 0) + place_row(d_shift, 3, 0)), d_x.astype(BF))


def feed_grads(
    native, ids, n_own, n_core, n_got, n_got_core, d_pre, d_pre_got, g_own, g_core, g_got, g_got_core, hidden, hidden_got, segs, orders
):
    fc = dot_tn(rows_of(n_own, n_core), d_pre) + dot_tn(rows_of(n_got, n_got_core), d_pre_got)
    proj = dot_tn(rows_of(g_own, g_core), hidden) + dot_tn(rows_of(g_got, g_got_core), hidden_got)
    sums = jnp.sum(wide(d_pre), axis=0, keepdims=True) + jnp.sum(wide(d_pre_got), axis=0, keepdims=True)
    cuts = []
    for order, product in zip(orders, (fc, proj) if len(orders) == 2 else (columns_of(fc, proj),)):
        for v in split_blocks(product, fc.shape[0] // segs, ids[BIT + order[0]], order[0]):
            cuts.append(v.astype(BF))
    return (*cuts, place_row(sums, ids[TP], 8))


def attention_grads(
    native, ids, n_own, n_core, n_got, n_got_core, d_packed, got, g_own, g_core, g_got, g_got_core, mixed, segs, order
):
    width = d_packed.shape[1]
    qkv = dot_tn(rows_of(n_own, n_core), d_packed) + dot_tn(rows_of(n_got, n_got_core), got[:, :width])
    out = dot_tn(rows_of(g_own, g_core), mixed) + dot_tn(rows_of(g_got, g_got_core), got[:, width:])
    sums = jnp.sum(wide(d_packed), axis=0, keepdims=True) + jnp.sum(wide(got[:, :width]), axis=0, keepdims=True)
    pieces = []
    for at in range(0, sums.shape[1], 3 * HD):
        pieces += [sums[:, at : at + HD], sums[:, at + 2 * HD : at + 3 * HD]]
    sums = columns_of(*pieces)
    blank = jnp.zeros_like(sums)
    row, _ = ordered(ids[CORE], columns_of(sums, blank), columns_of(blank, sums))
    keep, send = split_blocks(columns_of(qkv, out), qkv.shape[0] // segs, ids[BIT + order[0]], order[0])
    return (keep.astype(BF), send.astype(BF), place_row(row, ids[HALF], 12))


def memory_grads(native, ids, keep, arrived, tail, tail_got, d_own, segs, order):
    count = keep.shape[0]
    total = wide(keep) + wide(arrived[:count])
    write = dot_tn(tail, d_own) + dot_tn(tail_got, arrived[count:, : d_own.shape[1]])
    few, many = count // segs, write.shape[0] // segs
    blocks = []
    for s in range(segs):
        part = write[s * many : (s + 1) * many]
        folded = columns_of(*[part[i * few : (i + 1) * few] for i in range(4)])
        blocks.append(rows_of(total[s * few : (s + 1) * few], folded))
    keep, send = split_blocks(rows_of(*blocks), 2 * few, ids[BIT + order[0]], order[0])
    return (keep.astype(BF), send.astype(BF))


def small_end(native, ids, first, second, few):
    total = first + second
    size = total.shape[1]
    at = lax.axis_index("seg") * 4 + lax.axis_index("tp")

    def own(rows, width, count):
        start = at * width
        row = start // size
        chosen = rows[0:1]
        for i in range(1, count):
            chosen = jnp.where(row == i, rows[i : i + 1], chosen)
        return pltpu.roll(jnp.broadcast_to(chosen, (8, size)), size - start % size, 1)[0:1, :width]

    mine = pltpu.roll(total, size - at * few, 1)[:, :few]
    layers = [mine[16 * l : 16 * (l + 1)] for l in range(LAYERS)]
    return (
        mine[16 * LAYERS :],
        jnp.stack([rows_of(*[m[i : i + 1] for m in layers]) for i in range(3)]),
        jnp.stack([rows_of(*[m[3 + i : 4 + i] for m in layers]) for i in range(3)]),
        jnp.stack([m[6:8] for m in layers]),
        rows_of(*[own(total[16 * l + 12 : 16 * l + 14], 2 * few, 2) for l in range(LAYERS)]),
        rows_of(*[own(total[16 * l + 8 : 16 * l + 12], 4 * few, 4) for l in range(LAYERS)]),
    )


def next_cut(native, ids, keep, arrived, bit, place, rows):
    total = wide(keep) + wide(arrived)
    keep, send = split_blocks(total, rows, ids[BIT + bit], place)
    return (keep.astype(BF), send.astype(BF))


def both_layers(first_keep, first_got, second_keep, second_got):
    return jnp.stack([wide(first_keep) + wide(first_got), wide(second_keep) + wide(second_got)])


def feed_end(native, ids, fc_keep, fc_got, proj_keep, proj_got, both_keep, both_got):
    width = fc_keep.shape[1]
    both = wide(both_keep) + wide(both_got)
    fc, proj = wide(fc_keep) + wide(fc_got), wide(proj_keep) + wide(proj_got)
    return (jnp.stack([fc, both[:, :width]]), jnp.stack([proj, both[:, width:]]))


def attention_end(native, ids, *pairs, columns):
    total = both_layers(*pairs)
    return (total[:, :, :columns], total[:, :, columns:])


def memory_end(native, ids, *pairs):
    total = both_layers(*pairs)
    few = total.shape[1] // 2
    width = total.shape[2] // 4
    folded = total[:, few:]
    return (total[:, :few], jnp.concatenate([folded[:, :, i * width : (i + 1) * width] for i in range(4)], axis=1))


def pack_rows(*refs, count):
    weights, packed, at = refs[1 : 1 + count], refs[-1], 0
    for w in weights:
        packed[at : at + w.shape[0]] = w[...]
        at += w.shape[0]


def pack(ids, layer, weights, front=(), after=()):
    halves = [w.shape[1] // 2 for w, _ in weights]
    rows = sum(f.shape[0] for f in front) + sum(halves)
    packed = pl.pallas_call(
        functools.partial(pack_rows, count=len(front) + len(weights)),
        grid_spec=pltpu.PrefetchScalarGridSpec(
            num_scalar_prefetch=1,
            grid=(1,),
            in_specs=[pl.BlockSpec(f.shape, lambda i, ids: (0, 0)) for f in front]
            + [
                pl.BlockSpec((None, n, w.shape[2]), functools.partial(lambda b, i, ids: (layer, ids[BIT + b], 0), bit))
                for n, (w, bit) in zip(halves, weights)
            ]
            + [pl.BlockSpec(memory_space=pl.ANY) for _ in after],
            out_specs=pl.BlockSpec((rows, D), lambda i, ids: (0, 0)),
        ),
        out_shape=pltpu.HBM((rows, D), BF),
        compiler_params=pltpu.CompilerParams(vmem_limit_bytes=VMEM_BYTES),
        name="pack_rows",
    )(ids, *front, *[pltpu.with_memory_space_constraint(w, pltpu.HBM) for w, _ in weights], *map(settled, after))
    return lives_in_hbm(packed)


def relay(x, *after):
    anywhere = pl.BlockSpec(memory_space=pl.ANY)
    result = pl.pallas_call(
        lambda *refs: None,
        in_specs=[anywhere] * (1 + len(after)),
        out_specs=anywhere,
        out_shape=jax.ShapeDtypeStruct(x.shape, x.dtype),
        input_output_aliases={0: 0},
        name="relay",
    )(settled(x), *map(settled, after))
    return lives_in_hbm(result) if any(x is known for known in IN_HBM) else result


def toward(x, axis, bit):
    size = lax.axis_size(axis)
    moved = lax.ppermute(x, axis, [(i, i ^ bit) for i in range(size)])
    return moved if (axis, bit) == ("tp", 1) else lives_in_hbm(moved)


def core_swap(x):
    return toward(x, "tp", 1)


def half_swap(x):
    return toward(x, "tp", 2)


def gather_segments(x):
    size = lax.axis_size("seg")
    spread = jnp.broadcast_to(x, (size,) + x.shape)
    return lax.all_to_all(spread, "seg", 0, 0, tiled=True).reshape(-1, x.shape[1])


def sum_over_all(x, gates):
    steps = [("tp", 1), ("tp", 2)] + [("seg", 1 << b) for b in range(lax.axis_size("seg").bit_length() - 1)]
    for i, (axis, bit) in enumerate(steps):
        arrived = toward(x, axis, bit)
        if i + 1 == len(steps):
            return x, arrived
        x = x + (relay(arrived, gates[i]) if i < len(gates) else arrived)


def local(
    tokens,
    mem_tokens,
    segno,
    gains,
    shifts,
    assoc,
    w_write,
    w_qkv,
    b_query_value,
    w_out,
    out_bias,
    w_fc,
    b_fc,
    w_proj,
    cot_tokens,
    cot_memory,
):
    IN_HBM.clear()
    mem_rows = mem_tokens.shape[0]
    block_rows = mem_rows + tokens.shape[2]
    own_rows = 2 * block_rows
    all_rows = 2 * own_rows
    segs = lax.axis_size("seg")
    levels = segs.bit_length() - 1
    me = lax.axis_index("seg")
    tp = lax.axis_index("tp")
    half, core = tp // 2, tp % 2
    slots = segs * NMEM
    key_dim = assoc.shape[1] // 2
    heads = w_qkv.shape[2] // (3 * HD)
    units = w_fc.shape[2]
    columns = w_write.shape[2]
    phi = 6 * key_dim
    wide_blocks = (D // segs) % 16 == 0 and (D // (4 * segs)) % 8 == 0
    ids = jnp.stack([me & 1, half, core, tp] + [(me >> level) & 1 for level in range(levels)]).astype(jnp.int32)

    def pick(pair, which):
        return lax.dynamic_index_in_dim(pair, which, 0, keepdims=False)

    both = jnp.concatenate([jnp.broadcast_to(mem_tokens, (2,) + mem_tokens.shape), tokens[:, 0]], axis=1)
    cots = jnp.concatenate([cot_memory[:, 0], cot_tokens[:, 0]], axis=1)
    bias_rows = jnp.concatenate([b_fc, b_query_value.reshape(1, -1), jnp.zeros((16 - LAYERS - 1, D), BF)])
    qkv_rows, write_rows = jnp.swapaxes(w_qkv, 1, 2), jnp.swapaxes(w_write, 1, 2)

    attention_weights_of = ((qkv_rows, 0), (write_rows, 1), (w_out, 1))
    few, q_rows = columns // 2, qkv_rows.shape[1] // 2
    first_got = half_swap(jnp.concatenate([pick(both, 1 - half), bias_rows]))
    biases = (first_got, 16, block_rows // 16)

    def run(body, outs, *items, **more):
        return phase(body, outs, ids, *items, **more)

    def fetch(packed, bit):
        part = half_swap(packed)
        return part, toward(part, "seg", 1 << bit)

    def places(core_id):
        within = jnp.arange(block_rows)
        rows = []
        for block in (core_id, core_id + 2):
            rows.append(
                jnp.where(
                    within < mem_rows,
                    block * mem_rows + within,
                    4 * mem_rows + block * (block_rows - mem_rows) + within - mem_rows,
                )
            )
        return jnp.concatenate(rows)

    pos = jnp.concatenate([places(core), places(1 - core)]).astype(jnp.int32)
    hide = jnp.where(pos[:, None] >= pos[None, :], 0.0, -1e30).astype(F32)
    number = lax.dynamic_index_in_dim(segno[:, 0], half, 0, keepdims=False)
    segment_of = jnp.arange(slots) // NMEM
    mask = jnp.broadcast_to(
        ((segment_of < me) & (segment_of >= me - number)).astype(F32)[None, :], (own_rows, slots)
    )
    own_f32, own_low = ((own_rows, D), F32), ((own_rows, D), BF)
    tail_low = ((NMEM, D), BF)
    small_rows = ((16, D), F32)
    more_f32 = ((own_rows + 16, D), F32)

    saved = []
    x, normed, tail = run(
        functools.partial(first_rows, sizes=()),
        [own_f32, own_low, tail_low],
        pick(both, half),
        first_got,
        (gains, 0),
        (shifts, 0),
    )
    packs = pack(ids, 0, attention_weights_of[:1]), pack(ids, 0, attention_weights_of[1:])
    (q_part, q_rest), (o_part, o_rest) = fetch(packs[0], 0), fetch(packs[1], 1)
    fetched = dict(
        qkv=(q_part, q_rest), write=((o_part, few, 0), (o_rest, few, 0)), out=((o_part, few, 1), (o_rest, few, 1))
    )
    feed_packs = pack(ids, 0, ((w_fc, 0),), after=(x,)), pack(ids, 0, ((w_proj, 1),), after=(x,))
    fetched["fc"], fetched["proj"] = fetch(feed_packs[0], 0), fetch(feed_packs[1], 1)
    tail = relay(tail, *packs, *feed_packs)
    for l in range(LAYERS):
        out_bit = 1 - l
        if l:
            tail = relay(tail, fetched["fc"][0])
        tail = jnp.where(core == 1, tail, core_swap(tail))
        tails = gather_segments(tail)
        scores, denom, values = run(
            functools.partial(write_scores, out_bit=out_bit),
            [((own_rows, slots), BF), ((own_rows, slots), F32), ((slots, 2 * columns), BF)],
            normed,
            tails,
            Far((assoc, l)),
            mask,
            Far((write_rows, l)),
            *far(*fetched["write"]),
            after=(fetched["proj"][0],) if l else (q_part,),
        )
        mid, normed1, values = run(
            read_memory,
            [own_f32, own_low, ((slots, D), BF)],
            x,
            scores,
            values,
            core_swap(values),
            denom,
            (gains, l),
            (shifts, l),
        )
        normed1_core = core_swap(normed1)
        if l == 0:
            pack_next = pack(ids, 1, [(w, 0) for w, _ in attention_weights_of], after=(normed1,))
            next_attention = fetch(pack_next, 0)
        part, sent, packed0, packed1, mixed0, mixed1 = run(
            functools.partial(attention, layer=l, out_bit=out_bit),
            [own_f32, own_low]
            + [((all_rows, 3 * HD * heads), BF)] * 2
            + [((all_rows, HD * heads), BF, True)] * 2,
            normed1,
            normed1_core,
            *far((qkv_rows, l), (w_out, l), *fetched["qkv"], *fetched["out"]),
            b_query_value[l : l + 1],
            biases,
            hide,
            scratch=[((2 * heads, 3, all_rows, HD), BF), ((2 * heads, 1, all_rows, HD), BF)],
            after=() if l else (fetched["fc"][0], pack_next),
        )
        after, normed2 = run(
            after_attention,
            [own_f32, own_low],
            mid,
            part,
            core_swap(sent),
            (out_bias, l),
            (gains, l),
            (shifts, l),
        )
        normed2_core = core_swap(normed2)
        if l == 0:
            packs = pack(ids, 1, ((w_fc, 0),), after=(normed2,)), pack(ids, 1, ((w_proj, 1),), after=(normed2,))
            next_fc, next_proj = fetch(packs[0], 0), fetch(packs[1], 1)
        part, sent, hidden, slope0, slope1, acts = run(
            functools.partial(feed_forward, layer=l),
            [own_f32, own_low]
            + [((all_rows, units), BF, True)] * 3
            + [((2 * all_rows + NMEM, D), BF, True)],
            normed2,
            normed2_core,
            *far((w_fc, l), (w_proj, l), *fetched["fc"], *fetched["proj"]),
            b_fc[l : l + 1],
            biases,
            normed1,
            tail,
            after=() if l else packs,
        )
        saved.append(
            dict(
                x=x, normed=normed, tail=tail, tails=tails, scores=scores, denom=denom, values=values, mid=mid,
                normed1=(normed1, normed1_core), packed=(packed0, packed1), mixed=(mixed0, mixed1), after=after,
                normed2=(normed2, normed2_core), hidden=hidden, slope=(slope0, slope1), acts=acts, fetched=fetched,
            )
        )
        if l == 0:
            x, normed, tail = run(
                after_feed,
                [own_f32, own_low, tail_low],
                after,
                part,
                core_swap(sent),
                (out_bias, l),
                (gains, l + 1),
                (shifts, l + 1),
                after=(next_attention[0],),
            )
            place = q_rows // few
            fetched = dict(
                qkv=[(m, q_rows, 0) for m in next_attention],
                write=[(m, few, place) for m in next_attention],
                out=[(m, few, place + 1) for m in next_attention],
                fc=next_fc,
                proj=next_proj,
            )
        else:
            mine, given = run(
                after_last, [((block_rows, D), BF, True)] * 2, after, part, core_swap(sent), (out_bias, l)
            )

    def both_batches(mine, got):
        return jnp.where(half == 0, jnp.stack([mine, got]), jnp.stack([got, mine]))

    result = both_batches(mine, half_swap(given))
    out_memory = result[:, :mem_rows][:, None]
    out_tokens = result[:, mem_rows:][:, None]

    cot_own, cot_got = pick(cots, half), half_swap(pick(cots, 1 - half))
    grad_low = jnp.where(half == 0, jnp.concatenate([cot_own, cot_got]), jnp.concatenate([cot_got, cot_own]))
    grad = grad_low
    cut_rows = D * (segs // 2) // segs
    early = [None] * LAYERS

    block, folded = D // segs, D // (2 * segs)

    def arrival(level, pair, order):
        bits = list(order) + list(range(2, levels))
        return toward(pair[1], "seg", 1 << bits[level - 1])

    def cut(level, pair, order, rows, after=(), got=None):
        bits = list(order) + list(range(2, levels))
        left = [b for b in range(levels) if b not in bits[:level]]
        keep, send = pair
        got = arrival(level, pair, order) if got is None else got
        return run(
            functools.partial(next_cut, bit=bits[level], place=left.index(bits[level]), rows=rows),
            [((keep.shape[0] // 2, keep.shape[1]), BF)] * 2,
            *[Far(v) if any(v is known for known in IN_HBM) else v for v in (keep, got)],
            kernel=wide_blocks,
            after=after,
        )

    def end_of(level, pair, order, rows, after=()):
        while level < levels:
            pair = cut(level, pair, order, rows, after)
            level += 1
        bits = list(order) + list(range(2, levels))
        return pair[0], toward(pair[1], "seg", 1 << bits[-1])

    def feed_gradients(l, s, d_pre, sent_got, rows, after):
        orders = FEED_ORDERS[l]
        shapes = [((cut_rows, D), BF, True)] * 4 if len(orders) == 2 else [((cut_rows, D + units), BF, True)] * 2
        got, got_core = s["acts"]
        return run(
            functools.partial(feed_grads, segs=segs, orders=orders),
            shapes + [small_rows],
            *far(*s["normed2"], (got, own_rows, 3), (got_core, own_rows, 3)),
            *far(d_pre, (sent_got[0], all_rows, 0)),
            *far(*rows, (sent_got[0], own_rows, 2), (sent_got[1], own_rows, 2)),
            *far(s["hidden"], (got, all_rows, 0)),
            kernel=wide_blocks,
            after=after,
        )

    def attention_gradients(l, s, d_packed, sent_got, rows, after):
        got, got_core = s["acts"]
        return run(
            functools.partial(attention_grads, segs=segs, order=ATT_ORDERS[l]),
            [((cut_rows, 3 * HD * heads + HD * heads), BF, True)] * 2 + [small_rows],
            *far(*s["normed1"], (got, own_rows, 2), (got_core, own_rows, 2)),
            *far(d_packed, (sent_got[0], all_rows, 0)),
            *far(*rows, (sent_got[0], own_rows, 2), (sent_got[1], own_rows, 2)),
            Far(s["mixed"][0]),
            kernel=wide_blocks,
            after=after,
        )

    def memory_gradients(l, s, assoc_keep, assoc_got, vals_own, after):
        return run(
            functools.partial(memory_grads, segs=segs, order=MEM_ORDERS[l]),
            [((cut_rows // 2, D), BF, True)] * 2,
            *far(assoc_keep, assoc_got, s["tail"], (s["acts"][0], NMEM, 2 * all_rows // NMEM), vals_own),
            kernel=wide_blocks,
            after=after,
        )

    def with_core(sent, *gate):
        got = relay(half_swap(sent), *gate)
        return got, core_swap(got)

    for s in saved:
        s["acts"] = with_core(s["acts"], s["normed2"][0])

    waiting = None
    pins = (mine, saved[0]["acts"][0])
    for l in reversed(range(LAYERS)):
        s, out_bit = saved[l], 1 - l
        grad_core = core_swap(grad_low)
        feed_rows = (grad_low, grad_core)
        part, sent, d_pre, feed_sent = run(
            feed_back,
            [own_f32, own_low, ((all_rows, units), BF), ((all_rows + own_rows, D), BF, True)],
            grad_low,
            grad_core,
            *far((w_fc, l), (w_proj, l), *s["fetched"]["fc"], *s["fetched"]["proj"], *s["slope"]),
            after=pins,
        )
        pins = ()
        if waiting:
            *feed_pair, small_f = feed_gradients(1, *waiting["feed"], (sent,))
            early[1] = early[1] + small_f
            pins = (feed_pair[0],)
        d_after, d_after_low = run(
            after_feed_back,
            [more_f32, own_low],
            grad,
            part,
            core_swap(sent),
            s["after"],
            (gains, l),
            after=pins,
        )
        d_after_core = core_swap(d_after_low)
        attention_rows = (d_after_low, d_after_core)
        pins = ()
        if waiting:
            later, later_packed, later_sent, later_rows = waiting["attention"]
            later_got = with_core(later_sent, feed_pair[0])
            *att_pair, small_g = attention_gradients(1, later, later_packed, later_got, later_rows, (d_after_low,))
            early[1] = early[1] + small_g
            pins = (att_pair[0],)
            later_feed = feed_pair
        part, sent, d_packed, attention_sent = run(
            functools.partial(attention_back, out_bit=out_bit),
            [own_f32, own_low, ((all_rows, 3 * HD * heads), BF), ((all_rows + own_rows, D), BF, True)],
            d_after_low,
            d_after_core,
            *far((qkv_rows, l), (w_out, l), *s["fetched"]["qkv"], *s["fetched"]["out"]),
            *far(*s["packed"], s["mixed"][1]),
            hide,
            after=pins,
            scratch=[
                ((2 * heads, 3, all_rows, HD), BF),
                ((2 * heads, 1, all_rows, HD), BF),
                ((2 * heads, 3, all_rows, HD), BF),
            ],
        )
        if waiting:
            feed_got = with_core(feed_sent, d_after_low)
            pins = (feed_got[0],)
        else:
            pins = (s["acts"][0],)
        d_mid, d_scores, d_keys, y_mine, y_sent = run(
            after_attention_back,
            [
                more_f32,
                ((own_rows, slots), BF),
                ((slots, key_dim), BF),
                ((slots, key_dim // 2 + 2 * columns), F32),
                ((slots, key_dim // 2 + 2 * columns), BF),
            ],
            d_after,
            part,
            core_swap(sent),
            *far(s["mid"], (gains, l), s["scores"], s["values"], s["denom"], mask, s["normed"], s["tails"], (assoc, l)),
            after=pins,
        )
        written = (y_mine + wide(core_swap(y_sent))).astype(BF)
        written_all = lax.all_to_all(written.reshape(segs, NMEM, -1), "seg", 0, 0, tiled=True).reshape(slots, -1)
        d_norm, assoc_keep, assoc_send = run(
            functools.partial(read_back, segs=segs),
            [own_f32, ((D // 2, 2 * key_dim), BF), ((D // 2, 2 * key_dim), BF)],
            d_scores,
            *far(s["normed"], s["tails"], (assoc, l)),
            d_keys,
            kernel=wide_blocks,
            after=(written,),
        )
        pins = (d_norm,)
        if l == 0:
            att_next = cut(1, att_pair, ATT_ORDERS[1], block, (d_norm,))
            feed_next = cut(1, later_feed, FEED_ORDERS[1][0], block, (att_next[0],))
            mem_later = memory_gradients(1, *waiting["memory"], (feed_next[0],))
            mem_later_got = arrival(1, mem_later, MEM_ORDERS[1])
            attention_got = with_core(attention_sent, d_mid)
            att_got = arrival(2, att_next, ATT_ORDERS[1])
            feed_got_next = arrival(2, feed_next, FEED_ORDERS[1][0])
            pins = (mem_later[0],)
        d_tail, vals_own, vals_other = run(
            functools.partial(tail_back, out_bit=out_bit),
            [((NMEM, D), F32)] + [((NMEM, columns), BF)] * 2,
            written_all,
            *far((assoc, l), (write_rows, l), *s["fetched"]["write"]),
            after=pins,
        )
        assoc_keep, assoc_send = run(
            functools.partial(assoc_second, segs=segs),
            [((D // 4, 2 * key_dim), BF, True), ((D // 4 + NMEM, 2 * key_dim), BF, True)],
            assoc_keep,
            core_swap(assoc_send),
            vals_other,
            kernel=wide_blocks,
        )
        if l == 0:
            *feed_pair, small_f = feed_gradients(
                0, s, d_pre, feed_got, feed_rows, (d_tail, attention_got[0])
            )
        d_x, d_x_low = run(
            layer_end_back,
            [more_f32, own_low],
            *far(d_mid, d_norm),
            d_tail,
            core_swap(d_tail),
            *far(s["x"], (gains, l)),
            after=(assoc_keep,) if l else (assoc_keep, feed_pair[0], att_got),
        )
        early[l] = d_x[own_rows:]
        memory = (s, assoc_keep, half_swap(assoc_send), vals_own)
        pins = ()
        if l > 0:
            waiting = dict(
                feed=(s, d_pre, with_core(feed_sent, d_x), feed_rows),
                attention=(s, d_packed, attention_sent, attention_rows),
                memory=memory,
            )
        else:
            feed_next = cut(2, feed_next, FEED_ORDERS[1][0], block, (d_x,), feed_got_next)
            att_next = cut(2, att_next, ATT_ORDERS[1], block, (feed_next[0],), att_got)
            *att_pair, small_g = attention_gradients(
                0, s, d_packed, attention_got, attention_rows, (att_next[0], mem_later_got)
            )
            early[0] = early[0] + small_f + small_g
            fc_got = arrival(1, feed_pair[:2], FEED_ORDERS[0][0])
            proj_got = arrival(1, feed_pair[2:], FEED_ORDERS[0][1])
            fc = cut(1, feed_pair[:2], FEED_ORDERS[0][0], block, (att_pair[0],), fc_got)
            proj = cut(1, feed_pair[2:], FEED_ORDERS[0][1], block, (fc[0],), proj_got)
            mem_pair = memory_gradients(0, *memory, (proj[0],))
        grad, grad_low = d_x, d_x_low

    fc_order, proj_order = FEED_ORDERS[0]
    later_sums = [end_of(3, feed_next, FEED_ORDERS[1][0], block), end_of(3, att_next, ATT_ORDERS[1], block)]
    gates = [proj[0], mem_pair[0]]
    mem_next = cut(1, mem_later, MEM_ORDERS[1], folded, (mem_pair[0],), mem_later_got)
    att_pair = cut(1, att_pair, ATT_ORDERS[0], block, (mem_next[0],))
    gates.append(att_pair[0])
    fc = cut(2, fc, fc_order, block, (att_pair[0], later_sums[0][1]))
    proj = cut(2, proj, proj_order, block, (fc[0],))
    mem_pair = cut(1, mem_pair, MEM_ORDERS[0], folded, (proj[0],))
    gates.append(mem_pair[0])
    mem_next = cut(2, mem_next, MEM_ORDERS[1], folded, (mem_pair[0],))
    att_pair = cut(2, att_pair, ATT_ORDERS[0], block, (mem_next[0], later_sums[1][1]))
    fc, proj = end_of(3, fc, fc_order, block), end_of(3, proj, proj_order, block)
    mem_pair = cut(2, mem_pair, MEM_ORDERS[0], folded, (att_pair[0],))
    later_sums.append(end_of(3, mem_next, MEM_ORDERS[1], folded))
    last_sums = [fc, proj, end_of(3, att_pair, ATT_ORDERS[0], block), end_of(3, mem_pair, MEM_ORDERS[0], folded)]

    grad = grad[:own_rows]
    mine = pick(grad.reshape(2, block_rows, D), half)
    given = half_swap(pick(grad_low.reshape(2, block_rows, D), 1 - half))
    grad_tokens = both_batches(mine, wide(given))[:, mem_rows:][:, None]

    kept = grad.reshape(2, block_rows, D)[:, :mem_rows]
    mem_full = lax.dynamic_update_slice(jnp.zeros((2, 2, mem_rows, D), F32), kept[:, None], (0, core, 0, 0))
    smalls = sum_over_all(jnp.concatenate(early + [mem_full.reshape(-1, D)]), gates)

    few, many = D // (4 * segs), D // segs
    g_mem, g_gains, g_shifts, g_bias, g_qv, g_bfc = run(
        functools.partial(small_end, few=few),
        [
            ((4 * mem_rows, few), F32),
            ((3, LAYERS, few), F32),
            ((3, LAYERS, few), F32),
            ((LAYERS, 2, few), F32),
            ((LAYERS, 2 * few), F32),
            ((LAYERS, 4 * few), F32),
        ],
        *smalls,
    )
    qkv_columns = 3 * HD * heads
    g_fc, g_proj = run(
        feed_end,
        [((LAYERS, many, units), F32), ((LAYERS, many, units), F32)],
        *last_sums[0],
        *last_sums[1],
        *later_sums[0],
        kernel=wide_blocks,
    )
    g_qkv, g_out = run(
        functools.partial(attention_end, columns=qkv_columns),
        [((LAYERS, many, qkv_columns), F32), ((LAYERS, many, columns), F32)],
        *last_sums[2],
        *later_sums[1],
        kernel=wide_blocks,
    )
    g_assoc, g_write = run(
        memory_end,
        [((LAYERS, few, D), F32), ((LAYERS, many, columns), F32)],
        *last_sums[3],
        *later_sums[2],
        kernel=wide_blocks,
    )
    return (
        out_tokens,
        out_memory,
        grad_tokens,
        g_mem,
        jnp.swapaxes(g_gains, 0, 1),
        jnp.swapaxes(g_shifts, 0, 1),
        jnp.swapaxes(g_assoc, 1, 2),
        g_write,
        g_qkv,
        g_qv,
        jnp.swapaxes(g_out, 1, 2),
        g_bias,
        g_fc,
        g_bfc,
        jnp.swapaxes(g_proj, 1, 2),
    )


def solution(mesh):
    return jax.shard_map(
        local,
        mesh=mesh,
        in_specs=(
            P(None, "seg", "tp", None),
            P("tp", None),
            P(None, "seg"),
            P(),
            P(),
            P(),
            P(None, None, "tp"),
            P(None, None, "tp"),
            P(None, "tp"),
            P(None, "tp", None),
            P(),
            P(None, None, "tp"),
            P(None, "tp"),
            P(None, "tp", None),
            P(None, "seg", "tp", None),
            P(None, "seg", "tp", None),
        ),
        out_specs=(
            P(None, "seg", "tp", None),
            P(None, "seg", "tp", None),
            P(None, "seg", "tp", None),
            P(None, ("seg", "tp")),
            P(None, None, ("seg", "tp")),
            P(None, None, ("seg", "tp")),
            P(None, None, ("seg", "tp")),
            P(None, "seg", "tp"),
            P(None, "seg", "tp"),
            P(None, ("seg", "tp")),
            P(None, "tp", "seg"),
            P(None, None, ("seg", "tp")),
            P(None, "seg", "tp"),
            P(None, ("seg", "tp")),
            P(None, "tp", "seg"),
        ),
        check_vma=False,
    )
```

```python
import functools

import jax
import jax.numpy as jnp
from jax import lax
from jax.experimental import pallas as pl
from jax.experimental.pallas import tpu as pltpu
from jax.sharding import PartitionSpec as P

D = 768
HD = 64
NMEM = 16
LAYERS = 2
BF = jnp.bfloat16
F32 = jnp.float32
VMEM_BYTES = 40 * 1024 * 1024


class Far:
    def __init__(self, item):
        self.item = item


def far(*items):
    return [Far(item) for item in items]


IN_HBM = []


def lives_in_hbm(x):
    IN_HBM.append(x)
    return x


def settled(x):
    if any(x is known for known in IN_HBM):
        return pltpu.with_memory_space_constraint(x, pltpu.HBM)
    return x


def scalars():
    seg, tp = lax.axis_index("seg"), lax.axis_index("tp")
    return [seg & 1, tp // 2, tp % 2, tp] + [(seg >> b) & 1 for b in range(lax.axis_size("seg").bit_length() - 1)]


def value_of(item):
    if isinstance(item, Far):
        item = item.item
    if not isinstance(item, tuple):
        return item
    if len(item) == 3:
        return item[0][item[1] * item[2] : item[1] * (item[2] + 1)]
    return item[0][item[1]]


def phase(body, outs, ids, *items, kernel=True, after=(), scratch=()):
    if not kernel:
        return body(False, ids, *[value_of(item) for item in items])
    arrays, specs = [], []
    for item in items:
        if isinstance(item, Far):
            item = item.item
            where = functools.partial(pltpu.with_memory_space_constraint, memory_space=pltpu.HBM)
            item = (where(item[0]), *item[1:]) if isinstance(item, tuple) else where(item)
        if isinstance(item, tuple) and len(item) == 3:
            array, rows, at = item
            arrays.append(array)
            specs.append(pl.BlockSpec((rows, array.shape[1]), functools.partial(lambda at, i: (at, 0), at)))
        elif isinstance(item, tuple):
            array, layer = item
            rest = array.shape[1:]
            arrays.append(array)
            specs.append(
                pl.BlockSpec((None,) + rest, functools.partial(lambda l, n, i: (l,) + (0,) * n, layer, len(rest)))
            )
        else:
            arrays.append(item)
            specs.append(pl.BlockSpec(item.shape, functools.partial(lambda n, i: (0,) * n, item.ndim)))
    count = len(arrays)
    for array in after:
        arrays.append(settled(array))
        specs.append(pl.BlockSpec(memory_space=pl.ANY))

    def run(*refs):
        spaces = refs[len(arrays) + len(outs) :]
        results = body(True, scalars(), *spaces, *[r[...] for r in refs[:count]])
        for ref, result in zip(refs[len(arrays) :], results):
            ref[...] = result

    results = pl.pallas_call(
        run,
        grid=(1,),
        out_shape=[pltpu.HBM(*out[:2]) if len(out) == 3 else jax.ShapeDtypeStruct(*out) for out in outs],
        in_specs=specs,
        out_specs=[pl.BlockSpec(out[0], functools.partial(lambda n, i: (0,) * n, len(out[0]))) for out in outs],
        scratch_shapes=[pltpu.VMEM(s, t) for s, t in scratch],
        compiler_params=pltpu.CompilerParams(vmem_limit_bytes=VMEM_BYTES),
        name=getattr(body, "func", body).__name__,
    )(*arrays)
    return [lives_in_hbm(r) if len(out) == 3 else r for out, r in zip(outs, results)]


def wide(v):
    return v.astype(F32)


def dot(a, b):
    return lax.dot_general(a, b, (((1,), (0,)), ((), ())), preferred_element_type=F32)


def dot_nt(a, b):
    return lax.dot_general(a, b, (((1,), (1,)), ((), ())), preferred_element_type=F32)


def dot_tn(a, b):
    return lax.dot_general(a, b, (((0,), (0,)), ((), ())), preferred_element_type=F32)


def turn(v, by, native):
    if native:
        return pltpu.roll(v, (-by) % v.shape[1], 1)
    return jnp.roll(v, -by, axis=1)


def rows_of(*pieces):
    return jnp.concatenate(pieces, axis=0)


def columns_of(*pieces):
    return jnp.concatenate(pieces, axis=1)


def ordered(flag, first, second):
    return jnp.where(flag == 1, second, first), jnp.where(flag == 1, first, second)


def split_blocks(total, rows, flag, place=0):
    keep, send = [], []
    step = rows << place
    for at in range(0, total.shape[0], 2 * step):
        mine, others = ordered(flag, total[at : at + step], total[at + step : at + 2 * step])
        keep.append(mine)
        send.append(others)
    return rows_of(*keep), rows_of(*send)


def place_row(row, at, first, count=16):
    index = lax.broadcasted_iota(jnp.int32, (count, row.shape[1]), 0)
    return jnp.where(index == first + at, jnp.broadcast_to(row, (count, row.shape[1])), 0.0)


ODD, HALF, CORE, TP, BIT = 0, 1, 2, 3, 4
FEED_ORDERS = (((0, 1), (1, 0)), ((0, 1),))
ATT_ORDERS = ((0, 1), (1, 0))
MEM_ORDERS = ((1, 0), (1, 0))


def norm_parts(rows):
    centred = rows - jnp.mean(rows, axis=-1, keepdims=True)
    rstd = lax.rsqrt(jnp.mean(centred * centred, axis=-1, keepdims=True) + 1e-05)
    return centred * rstd, rstd


def norm_rows(rows, gain, shift):
    return norm_parts(rows)[0] * wide(gain) + wide(shift)


def norm_back(rows, gain, grad):
    hat, rstd = norm_parts(rows)
    d_hat = grad * wide(gain)
    d_rows = rstd * (
        d_hat
        - jnp.mean(d_hat, axis=-1, keepdims=True)
        - hat * jnp.mean(d_hat * hat, axis=-1, keepdims=True)
    )
    return d_rows, jnp.sum(grad * hat, axis=0, keepdims=True), jnp.sum(grad, axis=0, keepdims=True)


def paired(v):
    rest = jnp.log1p(jnp.exp(-jnp.abs(v)))
    return columns_of(jnp.maximum(v, 0.0) + rest, jnp.maximum(-v, 0.0) + rest)


def features(v, native):
    c = paired(v)
    return columns_of(*[c * turn(c, k, native) for k in (1, 2, 3)])


def features_back(v, grad, native):
    c = paired(v)
    size = c.shape[1]
    d_c = jnp.zeros_like(c)
    for k in (1, 2, 3):
        part = grad[:, (k - 1) * size : k * size]
        d_c = d_c + part * turn(c, k, native) + turn(part * c, -k, native)
    half = v.shape[1]
    up = 1.0 / (1.0 + jnp.exp(-v))
    return d_c[:, :half] * up - d_c[:, half:] * (1.0 - up)


def other_rows(odd, part, rest, first=0, last=None):
    return rows_of(*ordered(odd, part[first:last], rest[first:last]))


def first_rows(native, ids, own, got, gains, shifts, sizes):
    count = own.shape[0]
    x = wide(rows_of(*ordered(ids[HALF], own, got[:count])))
    normed = norm_rows(x, gains[0:1], shifts[0:1]).astype(BF)
    pieces, at = [], count
    for size in sizes:
        pieces.append(got[at : at + size])
        at += size
    return (x, normed, normed[normed.shape[0] - NMEM :], *pieces)


def read_keys_of(normed, assoc):
    return wide(dot_nt(normed, assoc[: assoc.shape[0] // 2]).astype(BF))


def written_keys_of(tails, assoc):
    return dot_nt(tails, assoc[assoc.shape[0] // 2 :])


def write_scores(native, ids, normed, tails, assoc, mask, w_write, part, rest, out_bit):
    feat_q = features(read_keys_of(normed, assoc), native).astype(BF)
    feat_k = features(written_keys_of(tails, assoc), native).astype(BF)
    scores = dot_nt(feat_q, feat_k) * mask
    denom = jnp.sum(scores, axis=1, keepdims=True) + 1.0
    others = other_rows(ids[BIT + out_bit], part, rest)
    values = columns_of(*ordered(ids[HALF], dot_nt(tails, w_write), dot_nt(tails, others)))
    return (scores.astype(BF), jnp.broadcast_to(denom, mask.shape), values.astype(BF))


def read_memory(native, ids, x, scores, values, values_core, denom, gains, shifts):
    left, right = ordered(ids[CORE], values, values_core)
    width = left.shape[1] // 2
    values = columns_of(left[:, :width], right[:, :width], left[:, width:], right[:, width:])
    read = (dot(scores, values) / denom[:, 0:1]).astype(BF)
    mid = x + wide(read)
    return (mid, norm_rows(mid, gains[1:2], shifts[1:2]).astype(BF), values)


def head_parts(packed, head):
    at = 3 * HD * head
    return packed[:, at : at + HD], packed[:, at + HD : at + 2 * HD], packed[:, at + 2 * HD : at + 3 * HD]


def head_probs(queries, keys, hide):
    scores = dot_nt(queries, keys) * 0.125 + hide
    weights = jnp.exp(scores - jnp.max(scores, axis=1, keepdims=True))
    return weights / jnp.sum(weights, axis=1, keepdims=True)


def head_bias(row):
    row = wide(row)
    blank = jnp.zeros((1, HD), F32)
    pieces = []
    for at in range(0, row.shape[1], 2 * HD):
        pieces += [row[:, at : at + HD], blank, row[:, at + HD : at + 2 * HD]]
    return columns_of(*pieces)


def attention_weights(ids, out_bit, w_qkv, w_out, part, rest, out_part, out_rest):
    return (w_qkv, w_out), (other_rows(ids[BIT], part, rest), other_rows(ids[BIT + out_bit], out_part, out_rest))


def put_heads(space, at, packed, parts):
    for column in range(packed.shape[1] // HD):
        space[at + column // parts, column % parts] = packed[:, HD * column : HD * (column + 1)]


def take_heads(space, first, last):
    return columns_of(*[space[head, part] for head in range(first, last) for part in range(space.shape[1])])


def attention(native, ids, heads, mixed_heads, own, other, w_qkv, w_out, part, rest, out_part, out_rest, bias, biases, hide, layer, out_bit):
    rows = rows_of(own, other)
    half = own.shape[0]
    width = bias.shape[1]
    other_bias = biases[LAYERS : LAYERS + 1, layer * width : (layer + 1) * width]
    weights = attention_weights(ids, out_bit, w_qkv, w_out, part, rest, out_part, out_rest)
    count = width // (2 * HD)
    packs = []
    for block, ((w, _), row) in enumerate(zip(weights, (bias, other_bias))):
        packed = (dot_nt(rows, w) + head_bias(row)).astype(BF)
        put_heads(heads, block * count, packed, 3)
        packs.append(packed)

    def one(head, carried):
        probs = head_probs(heads[head, 0], heads[head, 1], hide)
        mixed_heads[head, 0] = dot(probs.astype(BF), heads[head, 2]).astype(BF)
        return carried

    lax.fori_loop(0, 2 * count, one, 0, unroll=2)
    total, mixes = 0.0, []
    for block, (_, o) in enumerate(weights):
        mixed = take_heads(mixed_heads, block * count, (block + 1) * count)
        total = total + dot(mixed, o)
        mixes.append(mixed)
    return (total[:half], total[half:].astype(BF), *packs, *mixes)


def after_attention(native, ids, mid, part, arrived, bias, gains, shifts):
    after = mid + part + wide(arrived) + wide(bias[0:1])
    return (after, norm_rows(after, gains[2:3], shifts[2:3]).astype(BF))


def gelu_both(v):
    inner = 0.7978845608028654 * (v + 0.044715 * v * v * v)
    t = jnp.tanh(inner)
    slope = 0.5 * (1.0 + t) + 0.5 * v * (1.0 - t * t) * 0.7978845608028654 * (1.0 + 3 * 0.044715 * v * v)
    return 0.5 * v * (1.0 + t), slope


def by_halves(flag, rows, part, rest):
    cut = part.shape[0]
    first, second = ordered(flag, rows[:, :cut], rows[:, cut:])
    return dot(first, part) + dot(second, rest)


def back_by_halves(flag, rows, part, rest):
    return columns_of(*ordered(flag, dot_nt(rows, part), dot_nt(rows, rest)))


def feed_forward(
    native, ids, own, other, w_fc, w_proj, part, rest, part_proj, rest_proj, bias, biases, normed1, tail, layer
):
    rows = rows_of(own, other)
    half = own.shape[0]
    other_bias = biases[layer : layer + 1]
    hidden0, slope0 = gelu_both(dot(rows, w_fc) + wide(bias))
    hidden0 = hidden0.astype(BF)
    hidden1, slope1 = gelu_both(by_halves(ids[BIT], rows, part, rest) + wide(other_bias))
    hidden1 = hidden1.astype(BF)
    total = dot(hidden0, w_proj) + by_halves(ids[BIT + 1], hidden1, part_proj, rest_proj)
    return (
        total[:half],
        total[half:].astype(BF),
        hidden0,
        slope0.astype(BF),
        slope1.astype(BF),
        rows_of(hidden1, normed1, own, tail),
    )


def after_feed(native, ids, after, part, arrived, bias, next_gains, next_shifts):
    x = after + part + wide(arrived) + wide(bias[1:2])
    normed = norm_rows(x, next_gains[0:1], next_shifts[0:1]).astype(BF)
    return (x, normed, normed[normed.shape[0] - NMEM :])


def after_last(native, ids, after, part, arrived, bias):
    x = (after + part + wide(arrived) + wide(bias[1:2])).astype(BF)
    half = x.shape[0] // 2
    return ordered(ids[HALF], x[:half], x[half:])


def feed_back(native, ids, own, other, w_fc, w_proj, part, rest, part_proj, rest_proj, slope0, slope1):
    grads = rows_of(own, other)
    half = own.shape[0]
    d_pre0 = (dot_nt(grads, w_proj) * wide(slope0)).astype(BF)
    d_pre1 = (back_by_halves(ids[BIT + 1], grads, part_proj, rest_proj) * wide(slope1)).astype(BF)
    total = dot_nt(d_pre0, w_fc) + back_by_halves(ids[BIT], d_pre1, part, rest)
    return (total[:half], total[half:].astype(BF), d_pre0, rows_of(d_pre1, own))


def after_feed_back(native, ids, grad, part, arrived, after, gains):
    grad = wide(grad[: after.shape[0]])
    d_rows, d_gain, d_shift = norm_back(after, gains[2:3], part + wide(arrived))
    d_after = grad + d_rows
    d_bias = jnp.sum(grad, axis=0, keepdims=True)
    small = place_row(d_gain, 2, 0) + place_row(d_shift, 5, 0) + place_row(d_bias, 7, 0)
    return (rows_of(d_after, small), d_after.astype(BF))


def attention_back(
    native, ids, heads, d_mixed_heads, d_heads, own, other, w_qkv, w_out, part, rest, out_part, out_rest, packed0, packed1, mixed1, hide, out_bit
):
    grads = rows_of(own, other)
    half = own.shape[0]
    count = packed0.shape[1] // (3 * HD)
    weights = attention_weights(ids, out_bit, w_qkv, w_out, part, rest, out_part, out_rest)
    for block, ((_, o), packed) in enumerate(zip(weights, (packed0, packed1))):
        put_heads(heads, block * count, packed, 3)
        put_heads(d_mixed_heads, block * count, dot_nt(grads, o).astype(BF), 1)

    def one(head, carried):
        queries, keys, values = heads[head, 0], heads[head, 1], heads[head, 2]
        dm = d_mixed_heads[head, 0]
        probs = head_probs(queries, keys, hide)
        d_probs = dot_nt(dm, values)
        d_scores = (probs * (d_probs - jnp.sum(d_probs * probs, axis=1, keepdims=True))).astype(BF)
        d_heads[head, 0] = (dot(d_scores, keys) * 0.125).astype(BF)
        d_heads[head, 1] = (dot_tn(d_scores, queries) * 0.125).astype(BF)
        d_heads[head, 2] = dot_tn(probs.astype(BF), dm).astype(BF)
        return carried

    lax.fori_loop(0, 2 * count, one, 0)
    total, saved = 0.0, []
    for block, (w, _) in enumerate(weights):
        d_packed = take_heads(d_heads, block * count, (block + 1) * count)
        total = total + dot(d_packed, w)
        saved.append(d_packed)
    return (total[:half], total[half:].astype(BF), saved[0], rows_of(columns_of(saved[1], mixed1), own))


def after_attention_back(native, ids, d_after, part, arrived, mid, gains, scores, values, denom, mask, normed, tails, assoc):
    d_after, small = d_after[: mid.shape[0]], d_after[mid.shape[0] :]
    d_rows, d_gain, d_shift = norm_back(mid, gains[1:2], part + wide(arrived))
    d_mid = d_after + d_rows
    d_bias = jnp.sum(d_after, axis=0, keepdims=True)
    small = small + place_row(d_gain, 1, 0) + place_row(d_shift, 4, 0) + place_row(d_bias, 6, 0)
    scale = 1.0 / denom[:, 0:1]
    d_numer = (d_mid * scale).astype(BF)
    d_denom = -jnp.sum(d_mid * dot(scores, values), axis=1, keepdims=True) * scale * scale
    d_scores = ((dot_nt(d_numer, values) + d_denom) * mask).astype(BF)
    feat_q = features(read_keys_of(normed, assoc), native).astype(BF)
    d_keys = features_back(written_keys_of(tails, assoc), dot_tn(d_scores, feat_q), native)
    d_values = dot_tn(scores, d_numer)
    cut, width = d_keys.shape[1] // 2, d_values.shape[1] // 4
    mine, others = ordered(
        ids[CORE],
        columns_of(d_keys[:, :cut], d_values[:, :width], d_values[:, 2 * width : 3 * width]),
        columns_of(d_keys[:, cut:], d_values[:, width : 2 * width], d_values[:, 3 * width :]),
    )
    return (rows_of(d_mid, small), d_scores, d_keys.astype(BF), mine, others.astype(BF))


def read_back(native, ids, d_scores, normed, tails, assoc, d_tail_keys, segs):
    feat_k = features(written_keys_of(tails, assoc), native).astype(BF)
    d_keys = features_back(read_keys_of(normed, assoc), dot(d_scores, feat_k), native).astype(BF)
    d_norm = dot(d_keys, assoc[: assoc.shape[0] // 2])
    product = columns_of(dot_tn(normed, d_keys), dot_tn(tails, d_tail_keys))
    keep, send = split_blocks(product, product.shape[0] // (4 * segs), ids[CORE])
    return (d_norm, keep.astype(BF), send.astype(BF))


def assoc_second(native, ids, keep, arrived, values, segs):
    total = wide(keep) + wide(arrived)
    keep, send = split_blocks(total, total.shape[0] // (2 * segs), ids[HALF])
    blank = jnp.zeros((values.shape[0], send.shape[1] - values.shape[1]), BF)
    return (keep.astype(BF), rows_of(send.astype(BF), columns_of(values, blank)))


def tail_back(native, ids, arrived, assoc, w_write, part, rest, out_bit):
    total = wide(arrived[:NMEM])
    for at in range(NMEM, arrived.shape[0], NMEM):
        total = total + wide(arrived[at : at + NMEM])
    cut = total.shape[1] // 3
    low = total.astype(BF)
    own, other = ordered(ids[HALF], low[:, cut : 2 * cut], low[:, 2 * cut :])
    size = assoc.shape[0] // 4
    used, _ = ordered(ids[CORE], assoc[2 * size : 3 * size], assoc[3 * size :])
    others = other_rows(ids[BIT + out_bit], part, rest)
    d_tail = dot(low[:, :cut], used) + dot(own, w_write) + dot(other, others)
    return (d_tail, own, other)


def layer_end_back(native, ids, d_mid, d_norm, d_tail, d_tail_core, x, gains):
    rows = d_norm.shape[0]
    d_mid, small = d_mid[:rows], d_mid[rows:]
    added = jnp.where(ids[CORE] == 1, d_tail + d_tail_core, 0.0)
    d_norm = rows_of(d_norm[: rows - NMEM], d_norm[rows - NMEM :] + added)
    d_rows, d_gain, d_shift = norm_back(x, gains[0:1], d_norm)
    d_x = d_mid + d_rows
    return (rows_of(d_x, small + place_row(d_gain, 0, 0) + place_row(d_shift, 3, 0)), d_x.astype(BF))


def feed_grads(
    native, ids, n_own, n_core, n_got, n_got_core, d_pre, d_pre_got, g_own, g_core, g_got, g_got_core, hidden, hidden_got, segs, orders
):
    fc = dot_tn(rows_of(n_own, n_core), d_pre) + dot_tn(rows_of(n_got, n_got_core), d_pre_got)
    proj = dot_tn(rows_of(g_own, g_core), hidden) + dot_tn(rows_of(g_got, g_got_core), hidden_got)
    sums = jnp.sum(wide(d_pre), axis=0, keepdims=True) + jnp.sum(wide(d_pre_got), axis=0, keepdims=True)
    cuts = []
    for order, product in zip(orders, (fc, proj) if len(orders) == 2 else (columns_of(fc, proj),)):
        for v in split_blocks(product, fc.shape[0] // segs, ids[BIT + order[0]], order[0]):
            cuts.append(v.astype(BF))
    return (*cuts, place_row(sums, ids[TP], 8))


def attention_grads(
    native, ids, n_own, n_core, n_got, n_got_core, d_packed, got, g_own, g_core, g_got, g_got_core, mixed, segs, order
):
    width = d_packed.shape[1]
    qkv = dot_tn(rows_of(n_own, n_core), d_packed) + dot_tn(rows_of(n_got, n_got_core), got[:, :width])
    out = dot_tn(rows_of(g_own, g_core), mixed) + dot_tn(rows_of(g_got, g_got_core), got[:, width:])
    sums = jnp.sum(wide(d_packed), axis=0, keepdims=True) + jnp.sum(wide(got[:, :width]), axis=0, keepdims=True)
    pieces = []
    for at in range(0, sums.shape[1], 3 * HD):
        pieces += [sums[:, at : at + HD], sums[:, at + 2 * HD : at + 3 * HD]]
    sums = columns_of(*pieces)
    blank = jnp.zeros_like(sums)
    row, _ = ordered(ids[CORE], columns_of(sums, blank), columns_of(blank, sums))
    keep, send = split_blocks(columns_of(qkv, out), qkv.shape[0] // segs, ids[BIT + order[0]], order[0])
    return (keep.astype(BF), send.astype(BF), place_row(row, ids[HALF], 12))


def memory_grads(native, ids, keep, arrived, tail, tail_got, d_own, segs, order):
    count = keep.shape[0]
    total = wide(keep) + wide(arrived[:count])
    write = dot_tn(tail, d_own) + dot_tn(tail_got, arrived[count:, : d_own.shape[1]])
    few, many = count // segs, write.shape[0] // segs
    blocks = []
    for s in range(segs):
        part = write[s * many : (s + 1) * many]
        folded = columns_of(*[part[i * few : (i + 1) * few] for i in range(4)])
        blocks.append(rows_of(total[s * few : (s + 1) * few], folded))
    keep, send = split_blocks(rows_of(*blocks), 2 * few, ids[BIT + order[0]], order[0])
    return (keep.astype(BF), send.astype(BF))


def small_end(native, ids, first, second, few):
    total = first + second
    size = total.shape[1]
    at = lax.axis_index("seg") * 4 + lax.axis_index("tp")

    def own(rows, width, count):
        start = at * width
        row = start // size
        chosen = rows[0:1]
        for i in range(1, count):
            chosen = jnp.where(row == i, rows[i : i + 1], chosen)
        return pltpu.roll(jnp.broadcast_to(chosen, (8, size)), size - start % size, 1)[0:1, :width]

    mine = pltpu.roll(total, size - at * few, 1)[:, :few]
    layers = [mine[16 * l : 16 * (l + 1)] for l in range(LAYERS)]
    return (
        mine[16 * LAYERS :],
        jnp.stack([rows_of(*[m[i : i + 1] for m in layers]) for i in range(3)]),
        jnp.stack([rows_of(*[m[3 + i : 4 + i] for m in layers]) for i in range(3)]),
        jnp.stack([m[6:8] for m in layers]),
        rows_of(*[own(total[16 * l + 12 : 16 * l + 14], 2 * few, 2) for l in range(LAYERS)]),
        rows_of(*[own(total[16 * l + 8 : 16 * l + 12], 4 * few, 4) for l in range(LAYERS)]),
    )


def next_cut(native, ids, keep, arrived, bit, place, rows):
    total = wide(keep) + wide(arrived)
    keep, send = split_blocks(total, rows, ids[BIT + bit], place)
    return (keep.astype(BF), send.astype(BF))


def both_layers(first_keep, first_got, second_keep, second_got):
    return jnp.stack([wide(first_keep) + wide(first_got), wide(second_keep) + wide(second_got)])


def feed_end(native, ids, fc_keep, fc_got, proj_keep, proj_got, both_keep, both_got):
    width = fc_keep.shape[1]
    both = wide(both_keep) + wide(both_got)
    fc, proj = wide(fc_keep) + wide(fc_got), wide(proj_keep) + wide(proj_got)
    return (jnp.stack([fc, both[:, :width]]), jnp.stack([proj, both[:, width:]]))


def attention_end(native, ids, *pairs, columns):
    total = both_layers(*pairs)
    return (total[:, :, :columns], total[:, :, columns:])


def memory_end(native, ids, *pairs):
    total = both_layers(*pairs)
    few = total.shape[1] // 2
    width = total.shape[2] // 4
    folded = total[:, few:]
    return (total[:, :few], jnp.concatenate([folded[:, :, i * width : (i + 1) * width] for i in range(4)], axis=1))


def pack_rows(*refs, count):
    weights, packed, at = refs[1 : 1 + count], refs[-1], 0
    for w in weights:
        packed[at : at + w.shape[0]] = w[...]
        at += w.shape[0]


def pack(ids, layer, weights, front=(), after=()):
    halves = [w.shape[1] // 2 for w, _ in weights]
    rows = sum(f.shape[0] for f in front) + sum(halves)
    packed = pl.pallas_call(
        functools.partial(pack_rows, count=len(front) + len(weights)),
        grid_spec=pltpu.PrefetchScalarGridSpec(
            num_scalar_prefetch=1,
            grid=(1,),
            in_specs=[pl.BlockSpec(f.shape, lambda i, ids: (0, 0)) for f in front]
            + [
                pl.BlockSpec((None, n, w.shape[2]), functools.partial(lambda b, i, ids: (layer, ids[BIT + b], 0), bit))
                for n, (w, bit) in zip(halves, weights)
            ]
            + [pl.BlockSpec(memory_space=pl.ANY) for _ in after],
            out_specs=pl.BlockSpec((rows, D), lambda i, ids: (0, 0)),
        ),
        out_shape=pltpu.HBM((rows, D), BF),
        compiler_params=pltpu.CompilerParams(vmem_limit_bytes=VMEM_BYTES),
        name="pack_rows",
    )(ids, *front, *[pltpu.with_memory_space_constraint(w, pltpu.HBM) for w, _ in weights], *map(settled, after))
    return lives_in_hbm(packed)


def relay(x, *after):
    anywhere = pl.BlockSpec(memory_space=pl.ANY)
    result = pl.pallas_call(
        lambda *refs: None,
        in_specs=[anywhere] * (1 + len(after)),
        out_specs=anywhere,
        out_shape=jax.ShapeDtypeStruct(x.shape, x.dtype),
        input_output_aliases={0: 0},
        name="relay",
    )(settled(x), *map(settled, after))
    return lives_in_hbm(result) if any(x is known for known in IN_HBM) else result


def toward(x, axis, bit):
    size = lax.axis_size(axis)
    moved = lax.ppermute(x, axis, [(i, i ^ bit) for i in range(size)])
    return moved if (axis, bit) == ("tp", 1) else lives_in_hbm(moved)


def core_swap(x):
    return toward(x, "tp", 1)


def half_swap(x):
    return toward(x, "tp", 2)


def gather_segments(x):
    size = lax.axis_size("seg")
    spread = jnp.broadcast_to(x, (size,) + x.shape)
    return lax.all_to_all(spread, "seg", 0, 0, tiled=True).reshape(-1, x.shape[1])


def sum_over_all(x, gates):
    steps = [("tp", 1), ("tp", 2)] + [("seg", 1 << b) for b in range(lax.axis_size("seg").bit_length() - 1)]
    for i, (axis, bit) in enumerate(steps):
        arrived = toward(x, axis, bit)
        if i + 1 == len(steps):
            return x, arrived
        x = x + (relay(arrived, gates[i]) if i < len(gates) else arrived)


def local(
    tokens,
    mem_tokens,
    segno,
    gains,
    shifts,
    assoc,
    w_write,
    w_qkv,
    b_query_value,
    w_out,
    out_bias,
    w_fc,
    b_fc,
    w_proj,
    cot_tokens,
    cot_memory,
):
    IN_HBM.clear()
    mem_rows = mem_tokens.shape[0]
    block_rows = mem_rows + tokens.shape[2]
    own_rows = 2 * block_rows
    all_rows = 2 * own_rows
    segs = lax.axis_size("seg")
    levels = segs.bit_length() - 1
    me = lax.axis_index("seg")
    tp = lax.axis_index("tp")
    half, core = tp // 2, tp % 2
    slots = segs * NMEM
    key_dim = assoc.shape[1] // 2
    heads = w_qkv.shape[2] // (3 * HD)
    units = w_fc.shape[2]
    columns = w_write.shape[2]
    phi = 6 * key_dim
    wide_blocks = (D // segs) % 16 == 0 and (D // (4 * segs)) % 8 == 0
    ids = jnp.stack([me & 1, half, core, tp] + [(me >> level) & 1 for level in range(levels)]).astype(jnp.int32)

    def pick(pair, which):
        return lax.dynamic_index_in_dim(pair, which, 0, keepdims=False)

    both = jnp.concatenate([jnp.broadcast_to(mem_tokens, (2,) + mem_tokens.shape), tokens[:, 0]], axis=1)
    cots = jnp.concatenate([cot_memory[:, 0], cot_tokens[:, 0]], axis=1)
    bias_rows = jnp.concatenate([b_fc, b_query_value.reshape(1, -1), jnp.zeros((16 - LAYERS - 1, D), BF)])
    qkv_rows, write_rows = jnp.swapaxes(w_qkv, 1, 2), jnp.swapaxes(w_write, 1, 2)

    attention_weights_of = ((qkv_rows, 0), (write_rows, 1), (w_out, 1))
    few, q_rows = columns // 2, qkv_rows.shape[1] // 2
    first_got = half_swap(jnp.concatenate([pick(both, 1 - half), bias_rows]))
    biases = (first_got, 16, block_rows // 16)

    def run(body, outs, *items, **more):
        return phase(body, outs, ids, *items, **more)

    def fetch(packed, bit):
        part = half_swap(packed)
        return part, toward(part, "seg", 1 << bit)

    def places(core_id):
        within = jnp.arange(block_rows)
        rows = []
        for block in (core_id, core_id + 2):
            rows.append(
                jnp.where(
                    within < mem_rows,
                    block * mem_rows + within,
                    4 * mem_rows + block * (block_rows - mem_rows) + within - mem_rows,
                )
            )
        return jnp.concatenate(rows)

    pos = jnp.concatenate([places(core), places(1 - core)]).astype(jnp.int32)
    hide = jnp.where(pos[:, None] >= pos[None, :], 0.0, -1e30).astype(F32)
    number = lax.dynamic_index_in_dim(segno[:, 0], half, 0, keepdims=False)
    segment_of = jnp.arange(slots) // NMEM
    mask = jnp.broadcast_to(
        ((segment_of < me) & (segment_of >= me - number)).astype(F32)[None, :], (own_rows, slots)
    )
    own_f32, own_low = ((own_rows, D), F32), ((own_rows, D), BF)
    tail_low = ((NMEM, D), BF)
    small_rows = ((16, D), F32)
    more_f32 = ((own_rows + 16, D), F32)

    saved = []
    x, normed, tail = run(
        functools.partial(first_rows, sizes=()),
        [own_f32, own_low, tail_low],
        pick(both, half),
        first_got,
        (gains, 0),
        (shifts, 0),
    )
    packs = pack(ids, 0, attention_weights_of[:1]), pack(ids, 0, attention_weights_of[1:])
    (q_part, q_rest), (o_part, o_rest) = fetch(packs[0], 0), fetch(packs[1], 1)
    fetched = dict(
        qkv=(q_part, q_rest), write=((o_part, few, 0), (o_rest, few, 0)), out=((o_part, few, 1), (o_rest, few, 1))
    )
    feed_packs = pack(ids, 0, ((w_fc, 0),), after=(x,)), pack(ids, 0, ((w_proj, 1),), after=(x,))
    fetched["fc"], fetched["proj"] = fetch(feed_packs[0], 0), fetch(feed_packs[1], 1)
    tail = relay(tail, *packs, *feed_packs)
    for l in range(LAYERS):
        out_bit = 1 - l
        if l:
            tail = relay(tail, fetched["fc"][0])
        tail = jnp.where(core == 1, tail, core_swap(tail))
        tails = gather_segments(tail)
        scores, denom, values = run(
            functools.partial(write_scores, out_bit=out_bit),
            [((own_rows, slots), BF), ((own_rows, slots), F32), ((slots, 2 * columns), BF)],
            normed,
            tails,
            Far((assoc, l)),
            mask,
            Far((write_rows, l)),
            *far(*fetched["write"]),
            after=(fetched["proj"][0],) if l else (q_part,),
        )
        mid, normed1, values = run(
            read_memory,
            [own_f32, own_low, ((slots, D), BF)],
            x,
            scores,
            values,
            core_swap(values),
            denom,
            (gains, l),
            (shifts, l),
        )
        normed1_core = core_swap(normed1)
        if l == 0:
            pack_next = pack(ids, 1, [(w, 0) for w, _ in attention_weights_of], after=(normed1,))
            next_attention = fetch(pack_next, 0)
        part, sent, packed0, packed1, mixed0, mixed1 = run(
            functools.partial(attention, layer=l, out_bit=out_bit),
            [own_f32, own_low]
            + [((all_rows, 3 * HD * heads), BF)] * 2
            + [((all_rows, HD * heads), BF, True)] * 2,
            normed1,
            normed1_core,
            *far((qkv_rows, l), (w_out, l), *fetched["qkv"], *fetched["out"]),
            b_query_value[l : l + 1],
            biases,
            hide,
            scratch=[((2 * heads, 3, all_rows, HD), BF), ((2 * heads, 1, all_rows, HD), BF)],
            after=() if l else (fetched["fc"][0], pack_next),
        )
        after, normed2 = run(
            after_attention,
            [own_f32, own_low],
            mid,
            part,
            core_swap(sent),
            (out_bias, l),
            (gains, l),
            (shifts, l),
        )
        normed2_core = core_swap(normed2)
        if l == 0:
            packs = pack(ids, 1, ((w_fc, 0),), after=(normed2,)), pack(ids, 1, ((w_proj, 1),), after=(normed2,))
            next_fc, next_proj = fetch(packs[0], 0), fetch(packs[1], 1)
        part, sent, hidden, slope0, slope1, acts = run(
            functools.partial(feed_forward, layer=l),
            [own_f32, own_low]
            + [((all_rows, units), BF, True)] * 3
            + [((2 * all_rows + NMEM, D), BF, True)],
            normed2,
            normed2_core,
            *far((w_fc, l), (w_proj, l), *fetched["fc"], *fetched["proj"]),
            b_fc[l : l + 1],
            biases,
            normed1,
            tail,
            after=() if l else packs,
        )
        saved.append(
            dict(
                x=x, normed=normed, tail=tail, tails=tails, scores=scores, denom=denom, values=values, mid=mid,
                normed1=(normed1, normed1_core), packed=(packed0, packed1), mixed=(mixed0, mixed1), after=after,
                normed2=(normed2, normed2_core), hidden=hidden, slope=(slope0, slope1), acts=acts, fetched=fetched,
            )
        )
        if l == 0:
            x, normed, tail = run(
                after_feed,
                [own_f32, own_low, tail_low],
                after,
                part,
                core_swap(sent),
                (out_bias, l),
                (gains, l + 1),
                (shifts, l + 1),
                after=(next_attention[0],),
            )
            place = q_rows // few
            fetched = dict(
                qkv=[(m, q_rows, 0) for m in next_attention],
                write=[(m, few, place) for m in next_attention],
                out=[(m, few, place + 1) for m in next_attention],
                fc=next_fc,
                proj=next_proj,
            )
        else:
            mine, given = run(
                after_last, [((block_rows, D), BF, True)] * 2, after, part, core_swap(sent), (out_bias, l)
            )

    def both_batches(mine, got):
        return jnp.where(half == 0, jnp.stack([mine, got]), jnp.stack([got, mine]))

    result = both_batches(mine, half_swap(given))
    out_memory = result[:, :mem_rows][:, None]
    out_tokens = result[:, mem_rows:][:, None]

    cot_own, cot_got = pick(cots, half), half_swap(pick(cots, 1 - half))
    grad_low = jnp.where(half == 0, jnp.concatenate([cot_own, cot_got]), jnp.concatenate([cot_got, cot_own]))
    grad = grad_low
    cut_rows = D * (segs // 2) // segs
    early = [None] * LAYERS

    block, folded = D // segs, D // (2 * segs)

    def arrival(level, pair, order):
        bits = list(order) + list(range(2, levels))
        return toward(pair[1], "seg", 1 << bits[level - 1])

    def cut(level, pair, order, rows, after=(), got=None):
        bits = list(order) + list(range(2, levels))
        left = [b for b in range(levels) if b not in bits[:level]]
        keep, send = pair
        got = arrival(level, pair, order) if got is None else got
        return run(
            functools.partial(next_cut, bit=bits[level], place=left.index(bits[level]), rows=rows),
            [((keep.shape[0] // 2, keep.shape[1]), BF)] * 2,
            *[Far(v) if any(v is known for known in IN_HBM) else v for v in (keep, got)],
            kernel=wide_blocks,
            after=after,
        )

    def end_of(level, pair, order, rows, after=()):
        while level < levels:
            pair = cut(level, pair, order, rows, after)
            level += 1
        bits = list(order) + list(range(2, levels))
        return pair[0], toward(pair[1], "seg", 1 << bits[-1])

    def feed_gradients(l, s, d_pre, sent_got, rows, after):
        orders = FEED_ORDERS[l]
        shapes = [((cut_rows, D), BF, True)] * 4 if len(orders) == 2 else [((cut_rows, D + units), BF, True)] * 2
        got, got_core = s["acts"]
        return run(
            functools.partial(feed_grads, segs=segs, orders=orders),
            shapes + [small_rows],
            *far(*s["normed2"], (got, own_rows, 3), (got_core, own_rows, 3)),
            *far(d_pre, (sent_got[0], all_rows, 0)),
            *far(*rows, (sent_got[0], own_rows, 2), (sent_got[1], own_rows, 2)),
            *far(s["hidden"], (got, all_rows, 0)),
            kernel=wide_blocks,
            after=after,
        )

    def attention_gradients(l, s, d_packed, sent_got, rows, after):
        got, got_core = s["acts"]
        return run(
            functools.partial(attention_grads, segs=segs, order=ATT_ORDERS[l]),
            [((cut_rows, 3 * HD * heads + HD * heads), BF, True)] * 2 + [small_rows],
            *far(*s["normed1"], (got, own_rows, 2), (got_core, own_rows, 2)),
            *far(d_packed, (sent_got[0], all_rows, 0)),
            *far(*rows, (sent_got[0], own_rows, 2), (sent_got[1], own_rows, 2)),
            Far(s["mixed"][0]),
            kernel=wide_blocks,
            after=after,
        )

    def memory_gradients(l, s, assoc_keep, assoc_got, vals_own, after):
        return run(
            functools.partial(memory_grads, segs=segs, order=MEM_ORDERS[l]),
            [((cut_rows // 2, D), BF, True)] * 2,
            *far(assoc_keep, assoc_got, s["tail"], (s["acts"][0], NMEM, 2 * all_rows // NMEM), vals_own),
            kernel=wide_blocks,
            after=after,
        )

    def with_core(sent, *gate):
        got = relay(half_swap(sent), *gate)
        return got, core_swap(got)

    for s in saved:
        s["acts"] = with_core(s["acts"], s["normed2"][0])

    waiting = None
    pins = (mine, saved[0]["acts"][0])
    for l in reversed(range(LAYERS)):
        s, out_bit = saved[l], 1 - l
        grad_core = core_swap(grad_low)
        feed_rows = (grad_low, grad_core)
        part, sent, d_pre, feed_sent = run(
            feed_back,
            [own_f32, own_low, ((all_rows, units), BF), ((all_rows + own_rows, D), BF, True)],
            grad_low,
            grad_core,
            *far((w_fc, l), (w_proj, l), *s["fetched"]["fc"], *s["fetched"]["proj"], *s["slope"]),
            after=pins,
        )
        pins = ()
        if waiting:
            *feed_pair, small_f = feed_gradients(1, *waiting["feed"], (sent,))
            early[1] = early[1] + small_f
            pins = (feed_pair[0],)
        d_after, d_after_low = run(
            after_feed_back,
            [more_f32, own_low],
            grad,
            part,
            core_swap(sent),
            s["after"],
            (gains, l),
            after=pins,
        )
        d_after_core = core_swap(d_after_low)
        attention_rows = (d_after_low, d_after_core)
        pins = ()
        if waiting:
            later, later_packed, later_sent, later_rows = waiting["attention"]
            later_got = with_core(later_sent, feed_pair[0])
            *att_pair, small_g = attention_gradients(1, later, later_packed, later_got, later_rows, (d_after_low,))
            early[1] = early[1] + small_g
            pins = (att_pair[0],)
            later_feed = feed_pair
        part, sent, d_packed, attention_sent = run(
            functools.partial(attention_back, out_bit=out_bit),
            [own_f32, own_low, ((all_rows, 3 * HD * heads), BF), ((all_rows + own_rows, D), BF, True)],
            d_after_low,
            d_after_core,
            *far((qkv_rows, l), (w_out, l), *s["fetched"]["qkv"], *s["fetched"]["out"]),
            *far(*s["packed"], s["mixed"][1]),
            hide,
            after=pins,
            scratch=[
                ((2 * heads, 3, all_rows, HD), BF),
                ((2 * heads, 1, all_rows, HD), BF),
                ((2 * heads, 3, all_rows, HD), BF),
            ],
        )
        if waiting:
            feed_got = with_core(feed_sent, d_after_low)
            pins = (feed_got[0],)
        else:
            pins = (s["acts"][0],)
        d_mid, d_scores, d_keys, y_mine, y_sent = run(
            after_attention_back,
            [
                more_f32,
                ((own_rows, slots), BF),
                ((slots, key_dim), BF),
                ((slots, key_dim // 2 + 2 * columns), F32),
                ((slots, key_dim // 2 + 2 * columns), BF),
            ],
            d_after,
            part,
            core_swap(sent),
            *far(s["mid"], (gains, l), s["scores"], s["values"], s["denom"], mask, s["normed"], s["tails"], (assoc, l)),
            after=pins,
        )
        written = (y_mine + wide(core_swap(y_sent))).astype(BF)
        written_all = lax.all_to_all(written.reshape(segs, NMEM, -1), "seg", 0, 0, tiled=True).reshape(slots, -1)
        d_norm, assoc_keep, assoc_send = run(
            functools.partial(read_back, segs=segs),
            [own_f32, ((D // 2, 2 * key_dim), BF), ((D // 2, 2 * key_dim), BF)],
            d_scores,
            *far(s["normed"], s["tails"], (assoc, l)),
            d_keys,
            kernel=wide_blocks,
            after=(written,),
        )
        pins = (d_norm,)
        if l == 0:
            att_next = cut(1, att_pair, ATT_ORDERS[1], block, (d_norm,))
            feed_next = cut(1, later_feed, FEED_ORDERS[1][0], block, (att_next[0],))
            attention_got = with_core(attention_sent, d_mid)
            att_got = arrival(2, att_next, ATT_ORDERS[1])
            feed_got_next = arrival(2, feed_next, FEED_ORDERS[1][0])
            *feed_pair, small_f = feed_gradients(0, s, d_pre, feed_got, feed_rows, (feed_next[0],))
            pins = (feed_pair[0],)
        d_tail, vals_own, vals_other = run(
            functools.partial(tail_back, out_bit=out_bit),
            [((NMEM, D), F32)] + [((NMEM, columns), BF)] * 2,
            written_all,
            *far((assoc, l), (write_rows, l), *s["fetched"]["write"]),
            after=pins,
        )
        assoc_keep, assoc_send = run(
            functools.partial(assoc_second, segs=segs),
            [((D // 4, 2 * key_dim), BF, True), ((D // 4 + NMEM, 2 * key_dim), BF, True)],
            assoc_keep,
            core_swap(assoc_send),
            vals_other,
            kernel=wide_blocks,
        )
        if l == 0:
            mem_later = memory_gradients(1, *waiting["memory"], (d_tail,))
            mem_later_got = arrival(1, mem_later, MEM_ORDERS[1])
        d_x, d_x_low = run(
            layer_end_back,
            [more_f32, own_low],
            *far(d_mid, d_norm),
            d_tail,
            core_swap(d_tail),
            *far(s["x"], (gains, l)),
            after=(assoc_keep,) if l else (assoc_keep, mem_later[0], att_got),
        )
        early[l] = d_x[own_rows:]
        memory = (s, assoc_keep, half_swap(assoc_send), vals_own)
        pins = ()
        if l > 0:
            waiting = dict(
                feed=(s, d_pre, with_core(feed_sent, d_x), feed_rows),
                attention=(s, d_packed, attention_sent, attention_rows),
                memory=memory,
            )
        else:
            feed_next = cut(2, feed_next, FEED_ORDERS[1][0], block, (d_x,), feed_got_next)
            att_next = cut(2, att_next, ATT_ORDERS[1], block, (feed_next[0],), att_got)
            *att_pair, small_g = attention_gradients(
                0, s, d_packed, attention_got, attention_rows, (att_next[0], mem_later_got)
            )
            early[0] = early[0] + small_f + small_g
            fc_got = arrival(1, feed_pair[:2], FEED_ORDERS[0][0])
            proj_got = arrival(1, feed_pair[2:], FEED_ORDERS[0][1])
            later_sums = [end_of(3, feed_next, FEED_ORDERS[1][0], block), end_of(3, att_next, ATT_ORDERS[1], block)]
            fc = cut(1, feed_pair[:2], FEED_ORDERS[0][0], block, (att_pair[0],), fc_got)
            proj = cut(1, feed_pair[2:], FEED_ORDERS[0][1], block, (fc[0], later_sums[0][1]), proj_got)
            mem_pair = memory_gradients(0, *memory, (proj[0], later_sums[1][1]))
        grad, grad_low = d_x, d_x_low

    fc_order, proj_order = FEED_ORDERS[0]
    gates = [proj[0], mem_pair[0]]
    fc = cut(2, fc, fc_order, block, (mem_pair[0],))
    proj = cut(2, proj, proj_order, block, (fc[0],))
    mem_next = cut(1, mem_later, MEM_ORDERS[1], folded, (proj[0],), mem_later_got)
    att_pair = cut(1, att_pair, ATT_ORDERS[0], block, (mem_next[0],))
    gates.append(att_pair[0])
    fc, proj = end_of(3, fc, fc_order, block), end_of(3, proj, proj_order, block)
    mem_pair = cut(1, mem_pair, MEM_ORDERS[0], folded, (att_pair[0],))
    gates.append(mem_pair[0])
    mem_next = cut(2, mem_next, MEM_ORDERS[1], folded, (mem_pair[0],))
    att_pair = cut(2, att_pair, ATT_ORDERS[0], block, (mem_next[0], fc[1]))
    mem_pair = cut(2, mem_pair, MEM_ORDERS[0], folded, (att_pair[0], proj[1]))
    later_sums.append(end_of(3, mem_next, MEM_ORDERS[1], folded))
    last_sums = [fc, proj, end_of(3, att_pair, ATT_ORDERS[0], block), end_of(3, mem_pair, MEM_ORDERS[0], folded)]

    grad = grad[:own_rows]
    mine = pick(grad.reshape(2, block_rows, D), half)
    given = half_swap(pick(grad_low.reshape(2, block_rows, D), 1 - half))
    grad_tokens = both_batches(mine, wide(given))[:, mem_rows:][:, None]

    kept = grad.reshape(2, block_rows, D)[:, :mem_rows]
    mem_full = lax.dynamic_update_slice(jnp.zeros((2, 2, mem_rows, D), F32), kept[:, None], (0, core, 0, 0))
    smalls = sum_over_all(jnp.concatenate(early + [mem_full.reshape(-1, D)]), gates)

    few, many = D // (4 * segs), D // segs
    g_mem, g_gains, g_shifts, g_bias, g_qv, g_bfc = run(
        functools.partial(small_end, few=few),
        [
            ((4 * mem_rows, few), F32),
            ((3, LAYERS, few), F32),
            ((3, LAYERS, few), F32),
            ((LAYERS, 2, few), F32),
            ((LAYERS, 2 * few), F32),
            ((LAYERS, 4 * few), F32),
        ],
        *smalls,
    )
    qkv_columns = 3 * HD * heads
    g_fc, g_proj = run(
        feed_end,
        [((LAYERS, many, units), F32), ((LAYERS, many, units), F32)],
        *last_sums[0],
        *last_sums[1],
        *later_sums[0],
        kernel=wide_blocks,
    )
    g_qkv, g_out = run(
        functools.partial(attention_end, columns=qkv_columns),
        [((LAYERS, many, qkv_columns), F32), ((LAYERS, many, columns), F32)],
        *last_sums[2],
        *later_sums[1],
        kernel=wide_blocks,
    )
    g_assoc, g_write = run(
        memory_end,
        [((LAYERS, few, D), F32), ((LAYERS, many, columns), F32)],
        *last_sums[3],
        *later_sums[2],
        kernel=wide_blocks,
    )
    return (
        out_tokens,
        out_memory,
        grad_tokens,
        g_mem,
        jnp.swapaxes(g_gains, 0, 1),
        jnp.swapaxes(g_shifts, 0, 1),
        jnp.swapaxes(g_assoc, 1, 2),
        g_write,
        g_qkv,
        g_qv,
        jnp.swapaxes(g_out, 1, 2),
        g_bias,
        g_fc,
        g_bfc,
        jnp.swapaxes(g_proj, 1, 2),
    )


def solution(mesh):
    return jax.shard_map(
        local,
        mesh=mesh,
        in_specs=(
            P(None, "seg", "tp", None),
            P("tp", None),
            P(None, "seg"),
            P(),
            P(),
            P(),
            P(None, None, "tp"),
            P(None, None, "tp"),
            P(None, "tp"),
            P(None, "tp", None),
            P(),
            P(None, None, "tp"),
            P(None, "tp"),
            P(None, "tp", None),
            P(None, "seg", "tp", None),
            P(None, "seg", "tp", None),
        ),
        out_specs=(
            P(None, "seg", "tp", None),
            P(None, "seg", "tp", None),
            P(None, "seg", "tp", None),
            P(None, ("seg", "tp")),
            P(None, None, ("seg", "tp")),
            P(None, None, ("seg", "tp")),
            P(None, None, ("seg", "tp")),
            P(None, "seg", "tp"),
            P(None, "seg", "tp"),
            P(None, ("seg", "tp")),
            P(None, "tp", "seg"),
            P(None, None, ("seg", "tp")),
            P(None, "seg", "tp"),
            P(None, ("seg", "tp")),
            P(None, "tp", "seg"),
        ),
        check_vma=False,
    )
```

```python
import functools

import jax
import jax.numpy as jnp
from jax import lax
from jax.experimental import pallas as pl
from jax.experimental.pallas import tpu as pltpu
from jax.sharding import PartitionSpec as P

D = 768
HD = 64
NMEM = 16
LAYERS = 2
BF = jnp.bfloat16
F32 = jnp.float32
VMEM_BYTES = 40 * 1024 * 1024


class Far:
    def __init__(self, item):
        self.item = item


def far(*items):
    return [Far(item) for item in items]


IN_HBM = []


def lives_in_hbm(x):
    IN_HBM.append(x)
    return x


def settled(x):
    if any(x is known for known in IN_HBM):
        return pltpu.with_memory_space_constraint(x, pltpu.HBM)
    return x


def scalars():
    seg, tp = lax.axis_index("seg"), lax.axis_index("tp")
    return [seg & 1, tp // 2, tp % 2, tp] + [(seg >> b) & 1 for b in range(lax.axis_size("seg").bit_length() - 1)]


def value_of(item):
    if isinstance(item, Far):
        item = item.item
    if not isinstance(item, tuple):
        return item
    if len(item) == 3:
        return item[0][item[1] * item[2] : item[1] * (item[2] + 1)]
    return item[0][item[1]]


def phase(body, outs, ids, *items, kernel=True, after=(), scratch=()):
    if not kernel:
        return body(False, ids, *[value_of(item) for item in items])
    arrays, specs = [], []
    for item in items:
        if isinstance(item, Far):
            item = item.item
            where = functools.partial(pltpu.with_memory_space_constraint, memory_space=pltpu.HBM)
            item = (where(item[0]), *item[1:]) if isinstance(item, tuple) else where(item)
        if isinstance(item, tuple) and len(item) == 3:
            array, rows, at = item
            arrays.append(array)
            specs.append(pl.BlockSpec((rows, array.shape[1]), functools.partial(lambda at, i: (at, 0), at)))
        elif isinstance(item, tuple):
            array, layer = item
            rest = array.shape[1:]
            arrays.append(array)
            specs.append(
                pl.BlockSpec((None,) + rest, functools.partial(lambda l, n, i: (l,) + (0,) * n, layer, len(rest)))
            )
        else:
            arrays.append(item)
            specs.append(pl.BlockSpec(item.shape, functools.partial(lambda n, i: (0,) * n, item.ndim)))
    count = len(arrays)
    for array in after:
        arrays.append(settled(array))
        specs.append(pl.BlockSpec(memory_space=pl.ANY))

    def run(*refs):
        spaces = refs[len(arrays) + len(outs) :]
        results = body(True, scalars(), *spaces, *[r[...] for r in refs[:count]])
        for ref, result in zip(refs[len(arrays) :], results):
            ref[...] = result

    results = pl.pallas_call(
        run,
        grid=(1,),
        out_shape=[pltpu.HBM(*out[:2]) if len(out) == 3 else jax.ShapeDtypeStruct(*out) for out in outs],
        in_specs=specs,
        out_specs=[pl.BlockSpec(out[0], functools.partial(lambda n, i: (0,) * n, len(out[0]))) for out in outs],
        scratch_shapes=[pltpu.VMEM(s, t) for s, t in scratch],
        compiler_params=pltpu.CompilerParams(vmem_limit_bytes=VMEM_BYTES),
        name=getattr(body, "func", body).__name__,
    )(*arrays)
    return [lives_in_hbm(r) if len(out) == 3 else r for out, r in zip(outs, results)]


def wide(v):
    return v.astype(F32)


def dot(a, b):
    return lax.dot_general(a, b, (((1,), (0,)), ((), ())), preferred_element_type=F32)


def dot_nt(a, b):
    return lax.dot_general(a, b, (((1,), (1,)), ((), ())), preferred_element_type=F32)


def dot_tn(a, b):
    return lax.dot_general(a, b, (((0,), (0,)), ((), ())), preferred_element_type=F32)


def turn(v, by, native):
    if native:
        return pltpu.roll(v, (-by) % v.shape[1], 1)
    return jnp.roll(v, -by, axis=1)


def rows_of(*pieces):
    return jnp.concatenate(pieces, axis=0)


def columns_of(*pieces):
    return jnp.concatenate(pieces, axis=1)


def ordered(flag, first, second):
    return jnp.where(flag == 1, second, first), jnp.where(flag == 1, first, second)


def split_blocks(total, rows, flag, place=0):
    keep, send = [], []
    step = rows << place
    for at in range(0, total.shape[0], 2 * step):
        mine, others = ordered(flag, total[at : at + step], total[at + step : at + 2 * step])
        keep.append(mine)
        send.append(others)
    return rows_of(*keep), rows_of(*send)


def place_row(row, at, first, count=16):
    index = lax.broadcasted_iota(jnp.int32, (count, row.shape[1]), 0)
    return jnp.where(index == first + at, jnp.broadcast_to(row, (count, row.shape[1])), 0.0)


ODD, HALF, CORE, TP, BIT = 0, 1, 2, 3, 4
FEED_ORDERS = (((0, 1), (1, 0)), ((0, 1),))
ATT_ORDERS = ((0, 1), (1, 0))
MEM_ORDERS = ((1, 0), (1, 0))


def norm_parts(rows):
    centred = rows - jnp.mean(rows, axis=-1, keepdims=True)
    rstd = lax.rsqrt(jnp.mean(centred * centred, axis=-1, keepdims=True) + 1e-05)
    return centred * rstd, rstd


def norm_rows(rows, gain, shift):
    return norm_parts(rows)[0] * wide(gain) + wide(shift)


def norm_back(rows, gain, grad):
    hat, rstd = norm_parts(rows)
    d_hat = grad * wide(gain)
    d_rows = rstd * (
        d_hat
        - jnp.mean(d_hat, axis=-1, keepdims=True)
        - hat * jnp.mean(d_hat * hat, axis=-1, keepdims=True)
    )
    return d_rows, jnp.sum(grad * hat, axis=0, keepdims=True), jnp.sum(grad, axis=0, keepdims=True)


def paired(v):
    rest = jnp.log1p(jnp.exp(-jnp.abs(v)))
    return columns_of(jnp.maximum(v, 0.0) + rest, jnp.maximum(-v, 0.0) + rest)


def features(v, native):
    c = paired(v)
    return columns_of(*[c * turn(c, k, native) for k in (1, 2, 3)])


def features_back(v, grad, native):
    c = paired(v)
    size = c.shape[1]
    d_c = jnp.zeros_like(c)
    for k in (1, 2, 3):
        part = grad[:, (k - 1) * size : k * size]
        d_c = d_c + part * turn(c, k, native) + turn(part * c, -k, native)
    half = v.shape[1]
    up = 1.0 / (1.0 + jnp.exp(-v))
    return d_c[:, :half] * up - d_c[:, half:] * (1.0 - up)


def other_rows(odd, part, rest, first=0, last=None):
    return rows_of(*ordered(odd, part[first:last], rest[first:last]))


def first_rows(native, ids, own, got, gains, shifts, sizes):
    count = own.shape[0]
    x = wide(rows_of(*ordered(ids[HALF], own, got[:count])))
    normed = norm_rows(x, gains[0:1], shifts[0:1]).astype(BF)
    pieces, at = [], count
    for size in sizes:
        pieces.append(got[at : at + size])
        at += size
    return (x, normed, normed[normed.shape[0] - NMEM :], *pieces)


def read_keys_of(normed, assoc):
    return wide(dot_nt(normed, assoc[: assoc.shape[0] // 2]).astype(BF))


def written_keys_of(tails, assoc):
    return dot_nt(tails, assoc[assoc.shape[0] // 2 :])


def write_scores(native, ids, normed, tails, assoc, mask, w_write, part, rest, out_bit):
    feat_q = features(read_keys_of(normed, assoc), native).astype(BF)
    feat_k = features(written_keys_of(tails, assoc), native).astype(BF)
    scores = dot_nt(feat_q, feat_k) * mask
    denom = jnp.sum(scores, axis=1, keepdims=True) + 1.0
    others = other_rows(ids[BIT + out_bit], part, rest)
    values = columns_of(*ordered(ids[HALF], dot_nt(tails, w_write), dot_nt(tails, others)))
    return (scores.astype(BF), jnp.broadcast_to(denom, mask.shape), values.astype(BF))


def read_memory(native, ids, x, scores, values, values_core, denom, gains, shifts):
    left, right = ordered(ids[CORE], values, values_core)
    width = left.shape[1] // 2
    values = columns_of(left[:, :width], right[:, :width], left[:, width:], right[:, width:])
    read = (dot(scores, values) / denom[:, 0:1]).astype(BF)
    mid = x + wide(read)
    return (mid, norm_rows(mid, gains[1:2], shifts[1:2]).astype(BF), values)


def head_parts(packed, head):
    at = 3 * HD * head
    return packed[:, at : at + HD], packed[:, at + HD : at + 2 * HD], packed[:, at + 2 * HD : at + 3 * HD]


def head_probs(queries, keys, hide):
    scores = dot_nt(queries, keys) * 0.125 + hide
    weights = jnp.exp(scores - jnp.max(scores, axis=1, keepdims=True))
    return weights / jnp.sum(weights, axis=1, keepdims=True)


def head_bias(row):
    row = wide(row)
    blank = jnp.zeros((1, HD), F32)
    pieces = []
    for at in range(0, row.shape[1], 2 * HD):
        pieces += [row[:, at : at + HD], blank, row[:, at + HD : at + 2 * HD]]
    return columns_of(*pieces)


def attention_weights(ids, out_bit, w_qkv, w_out, part, rest, out_part, out_rest):
    return (w_qkv, w_out), (other_rows(ids[BIT], part, rest), other_rows(ids[BIT + out_bit], out_part, out_rest))


def put_heads(space, at, packed, parts):
    for column in range(packed.shape[1] // HD):
        space[at + column // parts, column % parts] = packed[:, HD * column : HD * (column + 1)]


def take_heads(space, first, last):
    return columns_of(*[space[head, part] for head in range(first, last) for part in range(space.shape[1])])


def attention(native, ids, heads, mixed_heads, own, other, w_qkv, w_out, part, rest, out_part, out_rest, bias, biases, hide, layer, out_bit):
    rows = rows_of(own, other)
    half = own.shape[0]
    width = bias.shape[1]
    other_bias = biases[LAYERS : LAYERS + 1, layer * width : (layer + 1) * width]
    weights = attention_weights(ids, out_bit, w_qkv, w_out, part, rest, out_part, out_rest)
    count = width // (2 * HD)
    packs = []
    for block, ((w, _), row) in enumerate(zip(weights, (bias, other_bias))):
        packed = (dot_nt(rows, w) + head_bias(row)).astype(BF)
        put_heads(heads, block * count, packed, 3)
        packs.append(packed)

    def one(head, carried):
        probs = head_probs(heads[head, 0], heads[head, 1], hide)
        mixed_heads[head, 0] = dot(probs.astype(BF), heads[head, 2]).astype(BF)
        return carried

    lax.fori_loop(0, 2 * count, one, 0, unroll=2)
    total, mixes = 0.0, []
    for block, (_, o) in enumerate(weights):
        mixed = take_heads(mixed_heads, block * count, (block + 1) * count)
        total = total + dot(mixed, o)
        mixes.append(mixed)
    return (total[:half], total[half:].astype(BF), *packs, *mixes)


def after_attention(native, ids, mid, part, arrived, bias, gains, shifts):
    after = mid + part + wide(arrived) + wide(bias[0:1])
    return (after, norm_rows(after, gains[2:3], shifts[2:3]).astype(BF))


def gelu_both(v):
    inner = 0.7978845608028654 * (v + 0.044715 * v * v * v)
    t = jnp.tanh(inner)
    slope = 0.5 * (1.0 + t) + 0.5 * v * (1.0 - t * t) * 0.7978845608028654 * (1.0 + 3 * 0.044715 * v * v)
    return 0.5 * v * (1.0 + t), slope


def by_halves(flag, rows, part, rest):
    cut = part.shape[0]
    first, second = ordered(flag, rows[:, :cut], rows[:, cut:])
    return dot(first, part) + dot(second, rest)


def back_by_halves(flag, rows, part, rest):
    return columns_of(*ordered(flag, dot_nt(rows, part), dot_nt(rows, rest)))


def feed_forward(
    native, ids, own, other, w_fc, w_proj, part, rest, part_proj, rest_proj, bias, biases, normed1, tail, layer
):
    rows = rows_of(own, other)
    half = own.shape[0]
    other_bias = biases[layer : layer + 1]
    hidden0, slope0 = gelu_both(dot(rows, w_fc) + wide(bias))
    hidden0 = hidden0.astype(BF)
    hidden1, slope1 = gelu_both(by_halves(ids[BIT], rows, part, rest) + wide(other_bias))
    hidden1 = hidden1.astype(BF)
    total = dot(hidden0, w_proj) + by_halves(ids[BIT + 1], hidden1, part_proj, rest_proj)
    return (
        total[:half],
        total[half:].astype(BF),
        hidden0,
        slope0.astype(BF),
        slope1.astype(BF),
        rows_of(hidden1, normed1, own, tail),
    )


def after_feed(native, ids, after, part, arrived, bias, next_gains, next_shifts):
    x = after + part + wide(arrived) + wide(bias[1:2])
    normed = norm_rows(x, next_gains[0:1], next_shifts[0:1]).astype(BF)
    return (x, normed, normed[normed.shape[0] - NMEM :])


def after_last(native, ids, after, part, arrived, bias):
    x = (after + part + wide(arrived) + wide(bias[1:2])).astype(BF)
    half = x.shape[0] // 2
    return ordered(ids[HALF], x[:half], x[half:])


def feed_back(native, ids, own, other, w_fc, w_proj, part, rest, part_proj, rest_proj, slope0, slope1):
    grads = rows_of(own, other)
    half = own.shape[0]
    d_pre0 = (dot_nt(grads, w_proj) * wide(slope0)).astype(BF)
    d_pre1 = (back_by_halves(ids[BIT + 1], grads, part_proj, rest_proj) * wide(slope1)).astype(BF)
    total = dot_nt(d_pre0, w_fc) + back_by_halves(ids[BIT], d_pre1, part, rest)
    return (total[:half], total[half:].astype(BF), d_pre0, rows_of(d_pre1, own))


def after_feed_back(native, ids, grad, part, arrived, after, gains):
    grad = wide(grad[: after.shape[0]])
    d_rows, d_gain, d_shift = norm_back(after, gains[2:3], part + wide(arrived))
    d_after = grad + d_rows
    d_bias = jnp.sum(grad, axis=0, keepdims=True)
    small = place_row(d_gain, 2, 0) + place_row(d_shift, 5, 0) + place_row(d_bias, 7, 0)
    return (rows_of(d_after, small), d_after.astype(BF))


def attention_back(
    native, ids, heads, d_mixed_heads, d_heads, own, other, w_qkv, w_out, part, rest, out_part, out_rest, packed0, packed1, mixed1, hide, out_bit
):
    grads = rows_of(own, other)
    half = own.shape[0]
    count = packed0.shape[1] // (3 * HD)
    weights = attention_weights(ids, out_bit, w_qkv, w_out, part, rest, out_part, out_rest)
    for block, ((_, o), packed) in enumerate(zip(weights, (packed0, packed1))):
        put_heads(heads, block * count, packed, 3)
        put_heads(d_mixed_heads, block * count, dot_nt(grads, o).astype(BF), 1)

    def one(head, carried):
        queries, keys, values = heads[head, 0], heads[head, 1], heads[head, 2]
        dm = d_mixed_heads[head, 0]
        probs = head_probs(queries, keys, hide)
        d_probs = dot_nt(dm, values)
        d_scores = (probs * (d_probs - jnp.sum(d_probs * probs, axis=1, keepdims=True))).astype(BF)
        d_heads[head, 0] = (dot(d_scores, keys) * 0.125).astype(BF)
        d_heads[head, 1] = (dot_tn(d_scores, queries) * 0.125).astype(BF)
        d_heads[head, 2] = dot_tn(probs.astype(BF), dm).astype(BF)
        return carried

    lax.fori_loop(0, 2 * count, one, 0)
    total, saved = 0.0, []
    for block, (w, _) in enumerate(weights):
        d_packed = take_heads(d_heads, block * count, (block + 1) * count)
        total = total + dot(d_packed, w)
        saved.append(d_packed)
    return (total[:half], total[half:].astype(BF), saved[0], rows_of(columns_of(saved[1], mixed1), own))


def after_attention_back(native, ids, d_after, part, arrived, mid, gains, scores, values, denom, mask, normed, tails, assoc):
    d_after, small = d_after[: mid.shape[0]], d_after[mid.shape[0] :]
    d_rows, d_gain, d_shift = norm_back(mid, gains[1:2], part + wide(arrived))
    d_mid = d_after + d_rows
    d_bias = jnp.sum(d_after, axis=0, keepdims=True)
    small = small + place_row(d_gain, 1, 0) + place_row(d_shift, 4, 0) + place_row(d_bias, 6, 0)
    scale = 1.0 / denom[:, 0:1]
    d_numer = (d_mid * scale).astype(BF)
    d_denom = -jnp.sum(d_mid * dot(scores, values), axis=1, keepdims=True) * scale * scale
    d_scores = ((dot_nt(d_numer, values) + d_denom) * mask).astype(BF)
    feat_q = features(read_keys_of(normed, assoc), native).astype(BF)
    d_keys = features_back(written_keys_of(tails, assoc), dot_tn(d_scores, feat_q), native)
    d_values = dot_tn(scores, d_numer)
    cut, width = d_keys.shape[1] // 2, d_values.shape[1] // 4
    mine, others = ordered(
        ids[CORE],
        columns_of(d_keys[:, :cut], d_values[:, :width], d_values[:, 2 * width : 3 * width]),
        columns_of(d_keys[:, cut:], d_values[:, width : 2 * width], d_values[:, 3 * width :]),
    )
    return (rows_of(d_mid, small), d_scores, d_keys.astype(BF), mine, others.astype(BF))


def read_back(native, ids, d_scores, normed, tails, assoc, d_tail_keys, segs):
    feat_k = features(written_keys_of(tails, assoc), native).astype(BF)
    d_keys = features_back(read_keys_of(normed, assoc), dot(d_scores, feat_k), native).astype(BF)
    d_norm = dot(d_keys, assoc[: assoc.shape[0] // 2])
    product = columns_of(dot_tn(normed, d_keys), dot_tn(tails, d_tail_keys))
    keep, send = split_blocks(product, product.shape[0] // (4 * segs), ids[CORE])
    return (d_norm, keep.astype(BF), send.astype(BF))


def assoc_second(native, ids, keep, arrived, values, segs):
    total = wide(keep) + wide(arrived)
    keep, send = split_blocks(total, total.shape[0] // (2 * segs), ids[HALF])
    blank = jnp.zeros((values.shape[0], send.shape[1] - values.shape[1]), BF)
    return (keep.astype(BF), rows_of(send.astype(BF), columns_of(values, blank)))


def tail_back(native, ids, arrived, assoc, w_write, part, rest, out_bit):
    total = wide(arrived[:NMEM])
    for at in range(NMEM, arrived.shape[0], NMEM):
        total = total + wide(arrived[at : at + NMEM])
    cut = total.shape[1] // 3
    low = total.astype(BF)
    own, other = ordered(ids[HALF], low[:, cut : 2 * cut], low[:, 2 * cut :])
    size = assoc.shape[0] // 4
    used, _ = ordered(ids[CORE], assoc[2 * size : 3 * size], assoc[3 * size :])
    others = other_rows(ids[BIT + out_bit], part, rest)
    d_tail = dot(low[:, :cut], used) + dot(own, w_write) + dot(other, others)
    return (d_tail, own, other)


def layer_end_back(native, ids, d_mid, d_norm, d_tail, d_tail_core, x, gains):
    rows = d_norm.shape[0]
    d_mid, small = d_mid[:rows], d_mid[rows:]
    added = jnp.where(ids[CORE] == 1, d_tail + d_tail_core, 0.0)
    d_norm = rows_of(d_norm[: rows - NMEM], d_norm[rows - NMEM :] + added)
    d_rows, d_gain, d_shift = norm_back(x, gains[0:1], d_norm)
    d_x = d_mid + d_rows
    return (rows_of(d_x, small + place_row(d_gain, 0, 0) + place_row(d_shift, 3, 0)), d_x.astype(BF))


def feed_grads(
    native, ids, n_own, n_core, n_got, n_got_core, d_pre, d_pre_got, g_own, g_core, g_got, g_got_core, hidden, hidden_got, segs, orders
):
    fc = dot_tn(rows_of(n_own, n_core), d_pre) + dot_tn(rows_of(n_got, n_got_core), d_pre_got)
    proj = dot_tn(rows_of(g_own, g_core), hidden) + dot_tn(rows_of(g_got, g_got_core), hidden_got)
    sums = jnp.sum(wide(d_pre), axis=0, keepdims=True) + jnp.sum(wide(d_pre_got), axis=0, keepdims=True)
    cuts = []
    for order, product in zip(orders, (fc, proj) if len(orders) == 2 else (columns_of(fc, proj),)):
        for v in split_blocks(product, fc.shape[0] // segs, ids[BIT + order[0]], order[0]):
            cuts.append(v.astype(BF))
    return (*cuts, place_row(sums, ids[TP], 8))


def attention_grads(
    native, ids, n_own, n_core, n_got, n_got_core, d_packed, got, g_own, g_core, g_got, g_got_core, mixed, segs, order
):
    width = d_packed.shape[1]
    qkv = dot_tn(rows_of(n_own, n_core), d_packed) + dot_tn(rows_of(n_got, n_got_core), got[:, :width])
    out = dot_tn(rows_of(g_own, g_core), mixed) + dot_tn(rows_of(g_got, g_got_core), got[:, width:])
    sums = jnp.sum(wide(d_packed), axis=0, keepdims=True) + jnp.sum(wide(got[:, :width]), axis=0, keepdims=True)
    pieces = []
    for at in range(0, sums.shape[1], 3 * HD):
        pieces += [sums[:, at : at + HD], sums[:, at + 2 * HD : at + 3 * HD]]
    sums = columns_of(*pieces)
    blank = jnp.zeros_like(sums)
    row, _ = ordered(ids[CORE], columns_of(sums, blank), columns_of(blank, sums))
    keep, send = split_blocks(columns_of(qkv, out), qkv.shape[0] // segs, ids[BIT + order[0]], order[0])
    return (keep.astype(BF), send.astype(BF), place_row(row, ids[HALF], 12))


def memory_grads(native, ids, keep, arrived, tail, tail_got, d_own, segs, order):
    count = keep.shape[0]
    total = wide(keep) + wide(arrived[:count])
    write = dot_tn(tail, d_own) + dot_tn(tail_got, arrived[count:, : d_own.shape[1]])
    few, many = count // segs, write.shape[0] // segs
    blocks = []
    for s in range(segs):
        part = write[s * many : (s + 1) * many]
        folded = columns_of(*[part[i * few : (i + 1) * few] for i in range(4)])
        blocks.append(rows_of(total[s * few : (s + 1) * few], folded))
    keep, send = split_blocks(rows_of(*blocks), 2 * few, ids[BIT + order[0]], order[0])
    return (keep.astype(BF), send.astype(BF))


def small_end(native, ids, first, second, few):
    total = first + second
    size = total.shape[1]
    at = lax.axis_index("seg") * 4 + lax.axis_index("tp")

    def own(rows, width, count):
        start = at * width
        row = start // size
        chosen = rows[0:1]
        for i in range(1, count):
            chosen = jnp.where(row == i, rows[i : i + 1], chosen)
        return pltpu.roll(jnp.broadcast_to(chosen, (8, size)), size - start % size, 1)[0:1, :width]

    mine = pltpu.roll(total, size - at * few, 1)[:, :few]
    layers = [mine[16 * l : 16 * (l + 1)] for l in range(LAYERS)]
    return (
        mine[16 * LAYERS :],
        jnp.stack([rows_of(*[m[i : i + 1] for m in layers]) for i in range(3)]),
        jnp.stack([rows_of(*[m[3 + i : 4 + i] for m in layers]) for i in range(3)]),
        jnp.stack([m[6:8] for m in layers]),
        rows_of(*[own(total[16 * l + 12 : 16 * l + 14], 2 * few, 2) for l in range(LAYERS)]),
        rows_of(*[own(total[16 * l + 8 : 16 * l + 12], 4 * few, 4) for l in range(LAYERS)]),
    )


def next_cut(native, ids, keep, arrived, bit, place, rows):
    total = wide(keep) + wide(arrived)
    keep, send = split_blocks(total, rows, ids[BIT + bit], place)
    return (keep.astype(BF), send.astype(BF))


def both_layers(first_keep, first_got, second_keep, second_got):
    return jnp.stack([wide(first_keep) + wide(first_got), wide(second_keep) + wide(second_got)])


def feed_end(native, ids, fc_keep, fc_got, proj_keep, proj_got, both_keep, both_got):
    width = fc_keep.shape[1]
    both = wide(both_keep) + wide(both_got)
    fc, proj = wide(fc_keep) + wide(fc_got), wide(proj_keep) + wide(proj_got)
    return (jnp.stack([fc, both[:, :width]]), jnp.stack([proj, both[:, width:]]))


def attention_end(native, ids, *pairs, columns):
    total = both_layers(*pairs)
    return (total[:, :, :columns], total[:, :, columns:])


def memory_end(native, ids, *pairs):
    total = both_layers(*pairs)
    few = total.shape[1] // 2
    width = total.shape[2] // 4
    folded = total[:, few:]
    return (total[:, :few], jnp.concatenate([folded[:, :, i * width : (i + 1) * width] for i in range(4)], axis=1))


def pack_rows(*refs, count):
    weights, packed, at = refs[1 : 1 + count], refs[-1], 0
    for w in weights:
        packed[at : at + w.shape[0]] = w[...]
        at += w.shape[0]


def pack(ids, layer, weights, front=(), after=()):
    halves = [w.shape[1] // 2 for w, _ in weights]
    rows = sum(f.shape[0] for f in front) + sum(halves)
    packed = pl.pallas_call(
        functools.partial(pack_rows, count=len(front) + len(weights)),
        grid_spec=pltpu.PrefetchScalarGridSpec(
            num_scalar_prefetch=1,
            grid=(1,),
            in_specs=[pl.BlockSpec(f.shape, lambda i, ids: (0, 0)) for f in front]
            + [
                pl.BlockSpec((None, n, w.shape[2]), functools.partial(lambda b, i, ids: (layer, ids[BIT + b], 0), bit))
                for n, (w, bit) in zip(halves, weights)
            ]
            + [pl.BlockSpec(memory_space=pl.ANY) for _ in after],
            out_specs=pl.BlockSpec((rows, D), lambda i, ids: (0, 0)),
        ),
        out_shape=pltpu.HBM((rows, D), BF),
        compiler_params=pltpu.CompilerParams(vmem_limit_bytes=VMEM_BYTES),
        name="pack_rows",
    )(ids, *front, *[pltpu.with_memory_space_constraint(w, pltpu.HBM) for w, _ in weights], *map(settled, after))
    return lives_in_hbm(packed)


def relay(x, *after):
    anywhere = pl.BlockSpec(memory_space=pl.ANY)
    result = pl.pallas_call(
        lambda *refs: None,
        in_specs=[anywhere] * (1 + len(after)),
        out_specs=anywhere,
        out_shape=jax.ShapeDtypeStruct(x.shape, x.dtype),
        input_output_aliases={0: 0},
        name="relay",
    )(settled(x), *map(settled, after))
    return lives_in_hbm(result) if any(x is known for known in IN_HBM) else result


def toward(x, axis, bit):
    size = lax.axis_size(axis)
    moved = lax.ppermute(x, axis, [(i, i ^ bit) for i in range(size)])
    return moved if (axis, bit) == ("tp", 1) else lives_in_hbm(moved)


def core_swap(x):
    return toward(x, "tp", 1)


def half_swap(x):
    return toward(x, "tp", 2)


def gather_segments(x):
    size = lax.axis_size("seg")
    spread = jnp.broadcast_to(x, (size,) + x.shape)
    return lax.all_to_all(spread, "seg", 0, 0, tiled=True).reshape(-1, x.shape[1])


def sum_over_all(x, gates):
    steps = [("tp", 1), ("tp", 2)] + [("seg", 1 << b) for b in range(lax.axis_size("seg").bit_length() - 1)]
    for i, (axis, bit) in enumerate(steps):
        arrived = toward(x, axis, bit)
        if i + 1 == len(steps):
            return x, arrived
        x = x + (relay(arrived, gates[i]) if i < len(gates) else arrived)


def local(
    tokens,
    mem_tokens,
    segno,
    gains,
    shifts,
    assoc,
    w_write,
    w_qkv,
    b_query_value,
    w_out,
    out_bias,
    w_fc,
    b_fc,
    w_proj,
    cot_tokens,
    cot_memory,
):
    IN_HBM.clear()
    mem_rows = mem_tokens.shape[0]
    block_rows = mem_rows + tokens.shape[2]
    own_rows = 2 * block_rows
    all_rows = 2 * own_rows
    segs = lax.axis_size("seg")
    levels = segs.bit_length() - 1
    me = lax.axis_index("seg")
    tp = lax.axis_index("tp")
    half, core = tp // 2, tp % 2
    slots = segs * NMEM
    key_dim = assoc.shape[1] // 2
    heads = w_qkv.shape[2] // (3 * HD)
    units = w_fc.shape[2]
    columns = w_write.shape[2]
    phi = 6 * key_dim
    wide_blocks = (D // segs) % 16 == 0 and (D // (4 * segs)) % 8 == 0
    ids = jnp.stack([me & 1, half, core, tp] + [(me >> level) & 1 for level in range(levels)]).astype(jnp.int32)

    def pick(pair, which):
        return lax.dynamic_index_in_dim(pair, which, 0, keepdims=False)

    both = jnp.concatenate([jnp.broadcast_to(mem_tokens, (2,) + mem_tokens.shape), tokens[:, 0]], axis=1)
    cots = jnp.concatenate([cot_memory[:, 0], cot_tokens[:, 0]], axis=1)
    bias_rows = jnp.concatenate([b_fc, b_query_value.reshape(1, -1), jnp.zeros((16 - LAYERS - 1, D), BF)])
    qkv_rows, write_rows = jnp.swapaxes(w_qkv, 1, 2), jnp.swapaxes(w_write, 1, 2)

    attention_weights_of = ((qkv_rows, 0), (write_rows, 1), (w_out, 1))
    few, q_rows = columns // 2, qkv_rows.shape[1] // 2
    first_got = half_swap(jnp.concatenate([pick(both, 1 - half), bias_rows]))
    biases = (first_got, 16, block_rows // 16)

    def run(body, outs, *items, **more):
        return phase(body, outs, ids, *items, **more)

    def fetch(packed, bit):
        part = half_swap(packed)
        return part, toward(part, "seg", 1 << bit)

    def places(core_id):
        within = jnp.arange(block_rows)
        rows = []
        for block in (core_id, core_id + 2):
            rows.append(
                jnp.where(
                    within < mem_rows,
                    block * mem_rows + within,
                    4 * mem_rows + block * (block_rows - mem_rows) + within - mem_rows,
                )
            )
        return jnp.concatenate(rows)

    pos = jnp.concatenate([places(core), places(1 - core)]).astype(jnp.int32)
    hide = jnp.where(pos[:, None] >= pos[None, :], 0.0, -1e30).astype(F32)
    number = lax.dynamic_index_in_dim(segno[:, 0], half, 0, keepdims=False)
    segment_of = jnp.arange(slots) // NMEM
    mask = jnp.broadcast_to(
        ((segment_of < me) & (segment_of >= me - number)).astype(F32)[None, :], (own_rows, slots)
    )
    own_f32, own_low = ((own_rows, D), F32), ((own_rows, D), BF)
    tail_low = ((NMEM, D), BF)
    small_rows = ((16, D), F32)
    more_f32 = ((own_rows + 16, D), F32)

    saved = []
    x, normed, tail = run(
        functools.partial(first_rows, sizes=()),
        [own_f32, own_low, tail_low],
        pick(both, half),
        first_got,
        (gains, 0),
        (shifts, 0),
    )
    packs = pack(ids, 0, attention_weights_of[:1]), pack(ids, 0, attention_weights_of[1:])
    (q_part, q_rest), (o_part, o_rest) = fetch(packs[0], 0), fetch(packs[1], 1)
    fetched = dict(
        qkv=(q_part, q_rest), write=((o_part, few, 0), (o_rest, few, 0)), out=((o_part, few, 1), (o_rest, few, 1))
    )
    feed_packs = pack(ids, 0, ((w_fc, 0),), after=(x,)), pack(ids, 0, ((w_proj, 1),), after=(x,))
    fetched["fc"], fetched["proj"] = fetch(feed_packs[0], 0), fetch(feed_packs[1], 1)
    tail = relay(tail, *packs, *feed_packs)
    for l in range(LAYERS):
        out_bit = 1 - l
        if l:
            tail = relay(tail, fetched["fc"][0])
        tail = jnp.where(core == 1, tail, core_swap(tail))
        tails = gather_segments(tail)
        scores, denom, values = run(
            functools.partial(write_scores, out_bit=out_bit),
            [((own_rows, slots), BF), ((own_rows, slots), F32), ((slots, 2 * columns), BF)],
            normed,
            tails,
            Far((assoc, l)),
            mask,
            Far((write_rows, l)),
            *far(*fetched["write"]),
            after=(fetched["proj"][0],) if l else (q_part,),
        )
        mid, normed1, values = run(
            read_memory,
            [own_f32, own_low, ((slots, D), BF)],
            x,
            scores,
            values,
            core_swap(values),
            denom,
            (gains, l),
            (shifts, l),
        )
        normed1_core = core_swap(normed1)
        if l == 0:
            pack_next = pack(ids, 1, [(w, 0) for w, _ in attention_weights_of], after=(normed1,))
            next_attention = fetch(pack_next, 0)
        part, sent, packed0, packed1, mixed0, mixed1 = run(
            functools.partial(attention, layer=l, out_bit=out_bit),
            [own_f32, own_low]
            + [((all_rows, 3 * HD * heads), BF)] * 2
            + [((all_rows, HD * heads), BF, True)] * 2,
            normed1,
            normed1_core,
            *far((qkv_rows, l), (w_out, l), *fetched["qkv"], *fetched["out"]),
            b_query_value[l : l + 1],
            biases,
            hide,
            scratch=[((2 * heads, 3, all_rows, HD), BF), ((2 * heads, 1, all_rows, HD), BF)],
            after=() if l else (fetched["fc"][0], pack_next),
        )
        after, normed2 = run(
            after_attention,
            [own_f32, own_low],
            mid,
            part,
            core_swap(sent),
            (out_bias, l),
            (gains, l),
            (shifts, l),
        )
        normed2_core = core_swap(normed2)
        if l == 0:
            packs = pack(ids, 1, ((w_fc, 0),), after=(normed2,)), pack(ids, 1, ((w_proj, 1),), after=(normed2,))
            next_fc, next_proj = fetch(packs[0], 0), fetch(packs[1], 1)
        part, sent, hidden, slope0, slope1, acts = run(
            functools.partial(feed_forward, layer=l),
            [own_f32, own_low]
            + [((all_rows, units), BF, True)] * 3
            + [((2 * all_rows + NMEM, D), BF, True)],
            normed2,
            normed2_core,
            *far((w_fc, l), (w_proj, l), *fetched["fc"], *fetched["proj"]),
            b_fc[l : l + 1],
            biases,
            normed1,
            tail,
            after=() if l else packs,
        )
        saved.append(
            dict(
                x=x, normed=normed, tail=tail, tails=tails, scores=scores, denom=denom, values=values, mid=mid,
                normed1=(normed1, normed1_core), packed=(packed0, packed1), mixed=(mixed0, mixed1), after=after,
                normed2=(normed2, normed2_core), hidden=hidden, slope=(slope0, slope1), acts=acts, fetched=fetched,
            )
        )
        if l == 0:
            x, normed, tail = run(
                after_feed,
                [own_f32, own_low, tail_low],
                after,
                part,
                core_swap(sent),
                (out_bias, l),
                (gains, l + 1),
                (shifts, l + 1),
                after=(next_attention[0],),
            )
            place = q_rows // few
            fetched = dict(
                qkv=[(m, q_rows, 0) for m in next_attention],
                write=[(m, few, place) for m in next_attention],
                out=[(m, few, place + 1) for m in next_attention],
                fc=next_fc,
                proj=next_proj,
            )
        else:
            mine, given = run(
                after_last, [((block_rows, D), BF, True)] * 2, after, part, core_swap(sent), (out_bias, l)
            )

    def both_batches(mine, got):
        return jnp.where(half == 0, jnp.stack([mine, got]), jnp.stack([got, mine]))

    result = both_batches(mine, half_swap(given))
    out_memory = result[:, :mem_rows][:, None]
    out_tokens = result[:, mem_rows:][:, None]

    cot_own, cot_got = pick(cots, half), half_swap(pick(cots, 1 - half))
    grad_low = jnp.where(half == 0, jnp.concatenate([cot_own, cot_got]), jnp.concatenate([cot_got, cot_own]))
    grad = grad_low
    cut_rows = D * (segs // 2) // segs
    early = [None] * LAYERS

    block, folded = D // segs, D // (2 * segs)

    def arrival(level, pair, order):
        bits = list(order) + list(range(2, levels))
        return toward(pair[1], "seg", 1 << bits[level - 1])

    def cut(level, pair, order, rows, after=(), got=None):
        bits = list(order) + list(range(2, levels))
        left = [b for b in range(levels) if b not in bits[:level]]
        keep, send = pair
        got = arrival(level, pair, order) if got is None else got
        return run(
            functools.partial(next_cut, bit=bits[level], place=left.index(bits[level]), rows=rows),
            [((keep.shape[0] // 2, keep.shape[1]), BF)] * 2,
            *[Far(v) if any(v is known for known in IN_HBM) else v for v in (keep, got)],
            kernel=wide_blocks,
            after=after,
        )

    def end_of(level, pair, order, rows, after=()):
        while level < levels:
            pair = cut(level, pair, order, rows, after)
            level += 1
        bits = list(order) + list(range(2, levels))
        return pair[0], toward(pair[1], "seg", 1 << bits[-1])

    def feed_gradients(l, s, d_pre, sent_got, rows, after):
        orders = FEED_ORDERS[l]
        shapes = [((cut_rows, D), BF, True)] * 4 if len(orders) == 2 else [((cut_rows, D + units), BF, True)] * 2
        got, got_core = s["acts"]
        return run(
            functools.partial(feed_grads, segs=segs, orders=orders),
            shapes + [small_rows],
            *far(*s["normed2"], (got, own_rows, 3), (got_core, own_rows, 3)),
            *far(d_pre, (sent_got[0], all_rows, 0)),
            *far(*rows, (sent_got[0], own_rows, 2), (sent_got[1], own_rows, 2)),
            *far(s["hidden"], (got, all_rows, 0)),
            kernel=wide_blocks,
            after=after,
        )

    def attention_gradients(l, s, d_packed, sent_got, rows, after):
        got, got_core = s["acts"]
        return run(
            functools.partial(attention_grads, segs=segs, order=ATT_ORDERS[l]),
            [((cut_rows, 3 * HD * heads + HD * heads), BF, True)] * 2 + [small_rows],
            *far(*s["normed1"], (got, own_rows, 2), (got_core, own_rows, 2)),
            *far(d_packed, (sent_got[0], all_rows, 0)),
            *far(*rows, (sent_got[0], own_rows, 2), (sent_got[1], own_rows, 2)),
            Far(s["mixed"][0]),
            kernel=wide_blocks,
            after=after,
        )

    def memory_gradients(l, s, assoc_keep, assoc_got, vals_own, after):
        return run(
            functools.partial(memory_grads, segs=segs, order=MEM_ORDERS[l]),
            [((cut_rows // 2, D), BF, True)] * 2,
            *far(assoc_keep, assoc_got, s["tail"], (s["acts"][0], NMEM, 2 * all_rows // NMEM), vals_own),
            kernel=wide_blocks,
            after=after,
        )

    def with_core(sent, *gate):
        got = relay(half_swap(sent), *gate)
        return got, core_swap(got)

    for s in saved:
        s["acts"] = with_core(s["acts"], s["normed2"][0])

    waiting = None
    pins = (mine, saved[0]["acts"][0])
    for l in reversed(range(LAYERS)):
        s, out_bit = saved[l], 1 - l
        grad_core = core_swap(grad_low)
        feed_rows = (grad_low, grad_core)
        part, sent, d_pre, feed_sent = run(
            feed_back,
            [own_f32, own_low, ((all_rows, units), BF), ((all_rows + own_rows, D), BF, True)],
            grad_low,
            grad_core,
            *far((w_fc, l), (w_proj, l), *s["fetched"]["fc"], *s["fetched"]["proj"], *s["slope"]),
            after=pins,
        )
        pins = ()
        if waiting:
            *feed_pair, small_f = feed_gradients(1, *waiting["feed"], (sent,))
            early[1] = early[1] + small_f
            pins = (feed_pair[0],)
        d_after, d_after_low = run(
            after_feed_back,
            [more_f32, own_low],
            grad,
            part,
            core_swap(sent),
            s["after"],
            (gains, l),
            after=pins,
        )
        d_after_core = core_swap(d_after_low)
        attention_rows = (d_after_low, d_after_core)
        pins = ()
        if waiting:
            later, later_packed, later_sent, later_rows = waiting["attention"]
            later_got = with_core(later_sent, feed_pair[0])
            *att_pair, small_g = attention_gradients(1, later, later_packed, later_got, later_rows, (d_after_low,))
            early[1] = early[1] + small_g
            pins = (att_pair[0],)
            later_feed = feed_pair
        part, sent, d_packed, attention_sent = run(
            functools.partial(attention_back, out_bit=out_bit),
            [own_f32, own_low, ((all_rows, 3 * HD * heads), BF), ((all_rows + own_rows, D), BF, True)],
            d_after_low,
            d_after_core,
            *far((qkv_rows, l), (w_out, l), *s["fetched"]["qkv"], *s["fetched"]["out"]),
            *far(*s["packed"], s["mixed"][1]),
            hide,
            after=pins,
            scratch=[
                ((2 * heads, 3, all_rows, HD), BF),
                ((2 * heads, 1, all_rows, HD), BF),
                ((2 * heads, 3, all_rows, HD), BF),
            ],
        )
        if waiting:
            feed_got = with_core(feed_sent, d_after_low)
            pins = (feed_got[0],)
        else:
            pins = (s["acts"][0],)
        d_mid, d_scores, d_keys, y_mine, y_sent = run(
            after_attention_back,
            [
                more_f32,
                ((own_rows, slots), BF),
                ((slots, key_dim), BF),
                ((slots, key_dim // 2 + 2 * columns), F32),
                ((slots, key_dim // 2 + 2 * columns), BF),
            ],
            d_after,
            part,
            core_swap(sent),
            *far(s["mid"], (gains, l), s["scores"], s["values"], s["denom"], mask, s["normed"], s["tails"], (assoc, l)),
            after=pins,
        )
        written = (y_mine + wide(core_swap(y_sent))).astype(BF)
        written_all = lax.all_to_all(written.reshape(segs, NMEM, -1), "seg", 0, 0, tiled=True).reshape(slots, -1)
        d_norm, assoc_keep, assoc_send = run(
            functools.partial(read_back, segs=segs),
            [own_f32, ((D // 2, 2 * key_dim), BF), ((D // 2, 2 * key_dim), BF)],
            d_scores,
            *far(s["normed"], s["tails"], (assoc, l)),
            d_keys,
            kernel=wide_blocks,
            after=(written,),
        )
        pins = (d_norm,)
        if l == 0:
            att_next = cut(1, att_pair, ATT_ORDERS[1], block, (d_norm,))
            feed_next = cut(1, later_feed, FEED_ORDERS[1][0], block, (att_next[0],))
            attention_got = with_core(attention_sent, d_mid)
            att_got = arrival(2, att_next, ATT_ORDERS[1])
            feed_got_next = arrival(2, feed_next, FEED_ORDERS[1][0])
            *feed_pair, small_f = feed_gradients(0, s, d_pre, feed_got, feed_rows, (feed_next[0],))
            pins = (feed_pair[0],)
        d_tail, vals_own, vals_other = run(
            functools.partial(tail_back, out_bit=out_bit),
            [((NMEM, D), F32)] + [((NMEM, columns), BF)] * 2,
            written_all,
            *far((assoc, l), (write_rows, l), *s["fetched"]["write"]),
            after=pins,
        )
        assoc_keep, assoc_send = run(
            functools.partial(assoc_second, segs=segs),
            [((D // 4, 2 * key_dim), BF, True), ((D // 4 + NMEM, 2 * key_dim), BF, True)],
            assoc_keep,
            core_swap(assoc_send),
            vals_other,
            kernel=wide_blocks,
        )
        if l == 0:
            mem_later = memory_gradients(1, *waiting["memory"], (d_tail,))
            mem_later_got = arrival(1, mem_later, MEM_ORDERS[1])
        d_x, d_x_low = run(
            layer_end_back,
            [more_f32, own_low],
            *far(d_mid, d_norm),
            d_tail,
            core_swap(d_tail),
            *far(s["x"], (gains, l)),
            after=(assoc_keep,) if l else (assoc_keep, mem_later[0], att_got),
        )
        early[l] = d_x[own_rows:]
        memory = (s, assoc_keep, half_swap(assoc_send), vals_own)
        pins = ()
        if l > 0:
            waiting = dict(
                feed=(s, d_pre, with_core(feed_sent, d_x), feed_rows),
                attention=(s, d_packed, attention_sent, attention_rows),
                memory=memory,
            )
        else:
            feed_next = cut(2, feed_next, FEED_ORDERS[1][0], block, (d_x,), feed_got_next)
            att_next = cut(2, att_next, ATT_ORDERS[1], block, (feed_next[0],), att_got)
            *att_pair, small_g = attention_gradients(
                0, s, d_packed, attention_got, attention_rows, (att_next[0], mem_later_got)
            )
            early[0] = early[0] + small_f + small_g
            fc_got = arrival(1, feed_pair[:2], FEED_ORDERS[0][0])
            proj_got = arrival(1, feed_pair[2:], FEED_ORDERS[0][1])
            later_sums = [end_of(3, feed_next, FEED_ORDERS[1][0], block), end_of(3, att_next, ATT_ORDERS[1], block)]
            fc = cut(1, feed_pair[:2], FEED_ORDERS[0][0], block, (att_pair[0],), fc_got)
            mem_pair = memory_gradients(0, *memory, (fc[0],))
            proj = cut(1, feed_pair[2:], FEED_ORDERS[0][1], block, (mem_pair[0], later_sums[0][1]), proj_got)
        grad, grad_low = d_x, d_x_low

    fc_order, proj_order = FEED_ORDERS[0]
    gates = [mem_pair[0], proj[0]]
    fc = cut(2, fc, fc_order, block, (proj[0], later_sums[1][1]))
    proj = cut(2, proj, proj_order, block, (fc[0],))
    mem_next = cut(1, mem_later, MEM_ORDERS[1], folded, (proj[0],), mem_later_got)
    att_pair = cut(1, att_pair, ATT_ORDERS[0], block, (mem_next[0],))
    gates.append(att_pair[0])
    fc, proj = end_of(3, fc, fc_order, block), end_of(3, proj, proj_order, block)
    mem_pair = cut(1, mem_pair, MEM_ORDERS[0], folded, (att_pair[0],))
    gates.append(mem_pair[0])
    mem_next = cut(2, mem_next, MEM_ORDERS[1], folded, (mem_pair[0],))
    att_pair = cut(2, att_pair, ATT_ORDERS[0], block, (mem_next[0], fc[1]))
    mem_pair = cut(2, mem_pair, MEM_ORDERS[0], folded, (att_pair[0], proj[1]))
    later_sums.append(end_of(3, mem_next, MEM_ORDERS[1], folded))
    last_sums = [fc, proj, end_of(3, att_pair, ATT_ORDERS[0], block), end_of(3, mem_pair, MEM_ORDERS[0], folded)]

    grad = grad[:own_rows]
    mine = pick(grad.reshape(2, block_rows, D), half)
    given = half_swap(pick(grad_low.reshape(2, block_rows, D), 1 - half))
    grad_tokens = both_batches(mine, wide(given))[:, mem_rows:][:, None]

    kept = grad.reshape(2, block_rows, D)[:, :mem_rows]
    mem_full = lax.dynamic_update_slice(jnp.zeros((2, 2, mem_rows, D), F32), kept[:, None], (0, core, 0, 0))
    smalls = sum_over_all(jnp.concatenate(early + [mem_full.reshape(-1, D)]), gates)

    few, many = D // (4 * segs), D // segs
    g_mem, g_gains, g_shifts, g_bias, g_qv, g_bfc = run(
        functools.partial(small_end, few=few),
        [
            ((4 * mem_rows, few), F32),
            ((3, LAYERS, few), F32),
            ((3, LAYERS, few), F32),
            ((LAYERS, 2, few), F32),
            ((LAYERS, 2 * few), F32),
            ((LAYERS, 4 * few), F32),
        ],
        *smalls,
    )
    qkv_columns = 3 * HD * heads
    g_fc, g_proj = run(
        feed_end,
        [((LAYERS, many, units), F32), ((LAYERS, many, units), F32)],
        *last_sums[0],
        *last_sums[1],
        *later_sums[0],
        kernel=wide_blocks,
    )
    g_qkv, g_out = run(
        functools.partial(attention_end, columns=qkv_columns),
        [((LAYERS, many, qkv_columns), F32), ((LAYERS, many, columns), F32)],
        *last_sums[2],
        *later_sums[1],
        kernel=wide_blocks,
    )
    g_assoc, g_write = run(
        memory_end,
        [((LAYERS, few, D), F32), ((LAYERS, many, columns), F32)],
        *last_sums[3],
        *later_sums[2],
        kernel=wide_blocks,
    )
    return (
        out_tokens,
        out_memory,
        grad_tokens,
        g_mem,
        jnp.swapaxes(g_gains, 0, 1),
        jnp.swapaxes(g_shifts, 0, 1),
        jnp.swapaxes(g_assoc, 1, 2),
        g_write,
        g_qkv,
        g_qv,
        jnp.swapaxes(g_out, 1, 2),
        g_bias,
        g_fc,
        g_bfc,
        jnp.swapaxes(g_proj, 1, 2),
    )


def solution(mesh):
    return jax.shard_map(
        local,
        mesh=mesh,
        in_specs=(
            P(None, "seg", "tp", None),
            P("tp", None),
            P(None, "seg"),
            P(),
            P(),
            P(),
            P(None, None, "tp"),
            P(None, None, "tp"),
            P(None, "tp"),
            P(None, "tp", None),
            P(),
            P(None, None, "tp"),
            P(None, "tp"),
            P(None, "tp", None),
            P(None, "seg", "tp", None),
            P(None, "seg", "tp", None),
        ),
        out_specs=(
            P(None, "seg", "tp", None),
            P(None, "seg", "tp", None),
            P(None, "seg", "tp", None),
            P(None, ("seg", "tp")),
            P(None, None, ("seg", "tp")),
            P(None, None, ("seg", "tp")),
            P(None, None, ("seg", "tp")),
            P(None, "seg", "tp"),
            P(None, "seg", "tp"),
            P(None, ("seg", "tp")),
            P(None, "tp", "seg"),
            P(None, None, ("seg", "tp")),
            P(None, "seg", "tp"),
            P(None, ("seg", "tp")),
            P(None, "tp", "seg"),
        ),
        check_vma=False,
    )
```

```python
import functools

import jax
import jax.numpy as jnp
from jax import lax
from jax.experimental import pallas as pl
from jax.experimental.pallas import tpu as pltpu
from jax.sharding import PartitionSpec as P

D = 768
HD = 64
NMEM = 16
LAYERS = 2
BF = jnp.bfloat16
F32 = jnp.float32
VMEM_BYTES = 40 * 1024 * 1024


class Far:
    def __init__(self, item):
        self.item = item


def far(*items):
    return [Far(item) for item in items]


IN_HBM = []


def lives_in_hbm(x):
    IN_HBM.append(x)
    return x


def settled(x):
    if any(x is known for known in IN_HBM):
        return pltpu.with_memory_space_constraint(x, pltpu.HBM)
    return x


def scalars():
    seg, tp = lax.axis_index("seg"), lax.axis_index("tp")
    return [seg & 1, tp // 2, tp % 2, tp] + [(seg >> b) & 1 for b in range(lax.axis_size("seg").bit_length() - 1)]


def value_of(item):
    if isinstance(item, Far):
        item = item.item
    if not isinstance(item, tuple):
        return item
    if len(item) == 3:
        return item[0][item[1] * item[2] : item[1] * (item[2] + 1)]
    return item[0][item[1]]


def phase(body, outs, ids, *items, kernel=True, after=(), scratch=()):
    if not kernel:
        return body(False, ids, *[value_of(item) for item in items])
    arrays, specs = [], []
    for item in items:
        if isinstance(item, Far):
            item = item.item
            where = functools.partial(pltpu.with_memory_space_constraint, memory_space=pltpu.HBM)
            item = (where(item[0]), *item[1:]) if isinstance(item, tuple) else where(item)
        if isinstance(item, tuple) and len(item) == 3:
            array, rows, at = item
            arrays.append(array)
            specs.append(pl.BlockSpec((rows, array.shape[1]), functools.partial(lambda at, i: (at, 0), at)))
        elif isinstance(item, tuple):
            array, layer = item
            rest = array.shape[1:]
            arrays.append(array)
            specs.append(
                pl.BlockSpec((None,) + rest, functools.partial(lambda l, n, i: (l,) + (0,) * n, layer, len(rest)))
            )
        else:
            arrays.append(item)
            specs.append(pl.BlockSpec(item.shape, functools.partial(lambda n, i: (0,) * n, item.ndim)))
    count = len(arrays)
    for array in after:
        arrays.append(settled(array))
        specs.append(pl.BlockSpec(memory_space=pl.ANY))

    def run(*refs):
        spaces = refs[len(arrays) + len(outs) :]
        results = body(True, scalars(), *spaces, *[r[...] for r in refs[:count]])
        for ref, result in zip(refs[len(arrays) :], results):
            ref[...] = result

    results = pl.pallas_call(
        run,
        grid=(1,),
        out_shape=[pltpu.HBM(*out[:2]) if len(out) == 3 else jax.ShapeDtypeStruct(*out) for out in outs],
        in_specs=specs,
        out_specs=[pl.BlockSpec(out[0], functools.partial(lambda n, i: (0,) * n, len(out[0]))) for out in outs],
        scratch_shapes=[pltpu.VMEM(s, t) for s, t in scratch],
        compiler_params=pltpu.CompilerParams(vmem_limit_bytes=VMEM_BYTES),
        name=getattr(body, "func", body).__name__,
    )(*arrays)
    return [lives_in_hbm(r) if len(out) == 3 else r for out, r in zip(outs, results)]


def wide(v):
    return v.astype(F32)


def dot(a, b):
    return lax.dot_general(a, b, (((1,), (0,)), ((), ())), preferred_element_type=F32)


def dot_nt(a, b):
    return lax.dot_general(a, b, (((1,), (1,)), ((), ())), preferred_element_type=F32)


def dot_tn(a, b):
    return lax.dot_general(a, b, (((0,), (0,)), ((), ())), preferred_element_type=F32)


def turn(v, by, native):
    if native:
        return pltpu.roll(v, (-by) % v.shape[1], 1)
    return jnp.roll(v, -by, axis=1)


def rows_of(*pieces):
    return jnp.concatenate(pieces, axis=0)


def columns_of(*pieces):
    return jnp.concatenate(pieces, axis=1)


def ordered(flag, first, second):
    return jnp.where(flag == 1, second, first), jnp.where(flag == 1, first, second)


def split_blocks(total, rows, flag, place=0):
    keep, send = [], []
    step = rows << place
    for at in range(0, total.shape[0], 2 * step):
        mine, others = ordered(flag, total[at : at + step], total[at + step : at + 2 * step])
        keep.append(mine)
        send.append(others)
    return rows_of(*keep), rows_of(*send)


def place_row(row, at, first, count=16):
    index = lax.broadcasted_iota(jnp.int32, (count, row.shape[1]), 0)
    return jnp.where(index == first + at, jnp.broadcast_to(row, (count, row.shape[1])), 0.0)


ODD, HALF, CORE, TP, BIT = 0, 1, 2, 3, 4
FEED_ORDERS = (((0, 1), (1, 0)), ((0, 1),))
ATT_ORDERS = ((0, 1), (1, 0))
MEM_ORDERS = ((1, 0), (1, 0))


def norm_parts(rows):
    centred = rows - jnp.mean(rows, axis=-1, keepdims=True)
    rstd = lax.rsqrt(jnp.mean(centred * centred, axis=-1, keepdims=True) + 1e-05)
    return centred * rstd, rstd


def norm_rows(rows, gain, shift):
    return norm_parts(rows)[0] * wide(gain) + wide(shift)


def norm_back(rows, gain, grad):
    hat, rstd = norm_parts(rows)
    d_hat = grad * wide(gain)
    d_rows = rstd * (
        d_hat
        - jnp.mean(d_hat, axis=-1, keepdims=True)
        - hat * jnp.mean(d_hat * hat, axis=-1, keepdims=True)
    )
    return d_rows, jnp.sum(grad * hat, axis=0, keepdims=True), jnp.sum(grad, axis=0, keepdims=True)


def paired(v):
    rest = jnp.log1p(jnp.exp(-jnp.abs(v)))
    return columns_of(jnp.maximum(v, 0.0) + rest, jnp.maximum(-v, 0.0) + rest)


def features(v, native):
    c = paired(v)
    return columns_of(*[c * turn(c, k, native) for k in (1, 2, 3)])


def features_back(v, grad, native):
    c = paired(v)
    size = c.shape[1]
    d_c = jnp.zeros_like(c)
    for k in (1, 2, 3):
        part = grad[:, (k - 1) * size : k * size]
        d_c = d_c + part * turn(c, k, native) + turn(part * c, -k, native)
    half = v.shape[1]
    up = 1.0 / (1.0 + jnp.exp(-v))
    return d_c[:, :half] * up - d_c[:, half:] * (1.0 - up)


def other_rows(odd, part, rest, first=0, last=None):
    return rows_of(*ordered(odd, part[first:last], rest[first:last]))


def first_rows(native, ids, own, got, gains, shifts, sizes):
    count = own.shape[0]
    x = wide(rows_of(*ordered(ids[HALF], own, got[:count])))
    normed = norm_rows(x, gains[0:1], shifts[0:1]).astype(BF)
    pieces, at = [], count
    for size in sizes:
        pieces.append(got[at : at + size])
        at += size
    return (x, normed, normed[normed.shape[0] - NMEM :], *pieces)


def read_keys_of(normed, assoc):
    return wide(dot_nt(normed, assoc[: assoc.shape[0] // 2]).astype(BF))


def written_keys_of(tails, assoc):
    return dot_nt(tails, assoc[assoc.shape[0] // 2 :])


def write_scores(native, ids, normed, tails, assoc, mask, w_write, part, rest, out_bit):
    feat_q = features(read_keys_of(normed, assoc), native).astype(BF)
    feat_k = features(written_keys_of(tails, assoc), native).astype(BF)
    scores = dot_nt(feat_q, feat_k) * mask
    denom = jnp.sum(scores, axis=1, keepdims=True) + 1.0
    others = other_rows(ids[BIT + out_bit], part, rest)
    values = columns_of(*ordered(ids[HALF], dot_nt(tails, w_write), dot_nt(tails, others)))
    return (scores.astype(BF), jnp.broadcast_to(denom, mask.shape), values.astype(BF))


def read_memory(native, ids, x, scores, values, values_core, denom, gains, shifts):
    left, right = ordered(ids[CORE], values, values_core)
    width = left.shape[1] // 2
    values = columns_of(left[:, :width], right[:, :width], left[:, width:], right[:, width:])
    read = (dot(scores, values) / denom[:, 0:1]).astype(BF)
    mid = x + wide(read)
    return (mid, norm_rows(mid, gains[1:2], shifts[1:2]).astype(BF), values)


def head_parts(packed, head):
    at = 3 * HD * head
    return packed[:, at : at + HD], packed[:, at + HD : at + 2 * HD], packed[:, at + 2 * HD : at + 3 * HD]


def head_probs(queries, keys, hide):
    scores = dot_nt(queries, keys) * 0.125 + hide
    weights = jnp.exp(scores - jnp.max(scores, axis=1, keepdims=True))
    return weights / jnp.sum(weights, axis=1, keepdims=True)


def head_bias(row):
    row = wide(row)
    blank = jnp.zeros((1, HD), F32)
    pieces = []
    for at in range(0, row.shape[1], 2 * HD):
        pieces += [row[:, at : at + HD], blank, row[:, at + HD : at + 2 * HD]]
    return columns_of(*pieces)


def attention_weights(ids, out_bit, w_qkv, w_out, part, rest, out_part, out_rest):
    return (w_qkv, w_out), (other_rows(ids[BIT], part, rest), other_rows(ids[BIT + out_bit], out_part, out_rest))


def put_heads(space, at, packed, parts):
    for column in range(packed.shape[1] // HD):
        space[at + column // parts, column % parts] = packed[:, HD * column : HD * (column + 1)]


def take_heads(space, first, last):
    return columns_of(*[space[head, part] for head in range(first, last) for part in range(space.shape[1])])


def attention(native, ids, heads, mixed_heads, own, other, w_qkv, w_out, part, rest, out_part, out_rest, bias, biases, hide, layer, out_bit):
    rows = rows_of(own, other)
    half = own.shape[0]
    width = bias.shape[1]
    other_bias = biases[LAYERS : LAYERS + 1, layer * width : (layer + 1) * width]
    weights = attention_weights(ids, out_bit, w_qkv, w_out, part, rest, out_part, out_rest)
    count = width // (2 * HD)
    packs = []
    for block, ((w, _), row) in enumerate(zip(weights, (bias, other_bias))):
        packed = (dot_nt(rows, w) + head_bias(row)).astype(BF)
        put_heads(heads, block * count, packed, 3)
        packs.append(packed)

    def one(head, carried):
        probs = head_probs(heads[head, 0], heads[head, 1], hide)
        mixed_heads[head, 0] = dot(probs.astype(BF), heads[head, 2]).astype(BF)
        return carried

    lax.fori_loop(0, 2 * count, one, 0, unroll=2)
    total, mixes = 0.0, []
    for block, (_, o) in enumerate(weights):
        mixed = take_heads(mixed_heads, block * count, (block + 1) * count)
        total = total + dot(mixed, o)
        mixes.append(mixed)
    return (total[:half], total[half:].astype(BF), *packs, *mixes)


def after_attention(native, ids, mid, part, arrived, bias, gains, shifts):
    after = mid + part + wide(arrived) + wide(bias[0:1])
    return (after, norm_rows(after, gains[2:3], shifts[2:3]).astype(BF))


def gelu_both(v):
    inner = 0.7978845608028654 * (v + 0.044715 * v * v * v)
    t = jnp.tanh(inner)
    slope = 0.5 * (1.0 + t) + 0.5 * v * (1.0 - t * t) * 0.7978845608028654 * (1.0 + 3 * 0.044715 * v * v)
    return 0.5 * v * (1.0 + t), slope


def by_halves(flag, rows, part, rest):
    cut = part.shape[0]
    first, second = ordered(flag, rows[:, :cut], rows[:, cut:])
    return dot(first, part) + dot(second, rest)


def back_by_halves(flag, rows, part, rest):
    return columns_of(*ordered(flag, dot_nt(rows, part), dot_nt(rows, rest)))


def feed_forward(
    native, ids, own, other, w_fc, w_proj, part, rest, part_proj, rest_proj, bias, biases, normed1, tail, layer
):
    rows = rows_of(own, other)
    half = own.shape[0]
    other_bias = biases[layer : layer + 1]
    hidden0, slope0 = gelu_both(dot(rows, w_fc) + wide(bias))
    hidden0 = hidden0.astype(BF)
    hidden1, slope1 = gelu_both(by_halves(ids[BIT], rows, part, rest) + wide(other_bias))
    hidden1 = hidden1.astype(BF)
    total = dot(hidden0, w_proj) + by_halves(ids[BIT + 1], hidden1, part_proj, rest_proj)
    return (
        total[:half],
        total[half:].astype(BF),
        hidden0,
        slope0.astype(BF),
        slope1.astype(BF),
        rows_of(hidden1, normed1, own, tail),
    )


def after_feed(native, ids, after, part, arrived, bias, next_gains, next_shifts):
    x = after + part + wide(arrived) + wide(bias[1:2])
    normed = norm_rows(x, next_gains[0:1], next_shifts[0:1]).astype(BF)
    return (x, normed, normed[normed.shape[0] - NMEM :])


def after_last(native, ids, after, part, arrived, bias):
    x = (after + part + wide(arrived) + wide(bias[1:2])).astype(BF)
    half = x.shape[0] // 2
    return ordered(ids[HALF], x[:half], x[half:])


def feed_back(native, ids, own, other, w_fc, w_proj, part, rest, part_proj, rest_proj, slope0, slope1):
    grads = rows_of(own, other)
    half = own.shape[0]
    d_pre0 = (dot_nt(grads, w_proj) * wide(slope0)).astype(BF)
    d_pre1 = (back_by_halves(ids[BIT + 1], grads, part_proj, rest_proj) * wide(slope1)).astype(BF)
    total = dot_nt(d_pre0, w_fc) + back_by_halves(ids[BIT], d_pre1, part, rest)
    return (total[:half], total[half:].astype(BF), d_pre0, rows_of(d_pre1, own))


def after_feed_back(native, ids, grad, part, arrived, after, gains):
    grad = wide(grad[: after.shape[0]])
    d_rows, d_gain, d_shift = norm_back(after, gains[2:3], part + wide(arrived))
    d_after = grad + d_rows
    d_bias = jnp.sum(grad, axis=0, keepdims=True)
    small = place_row(d_gain, 2, 0) + place_row(d_shift, 5, 0) + place_row(d_bias, 7, 0)
    return (rows_of(d_after, small), d_after.astype(BF))


def attention_back(
    native, ids, heads, d_mixed_heads, d_heads, own, other, w_qkv, w_out, part, rest, out_part, out_rest, packed0, packed1, mixed1, hide, out_bit
):
    grads = rows_of(own, other)
    half = own.shape[0]
    count = packed0.shape[1] // (3 * HD)
    weights = attention_weights(ids, out_bit, w_qkv, w_out, part, rest, out_part, out_rest)
    for block, ((_, o), packed) in enumerate(zip(weights, (packed0, packed1))):
        put_heads(heads, block * count, packed, 3)
        put_heads(d_mixed_heads, block * count, dot_nt(grads, o).astype(BF), 1)

    def one(head, carried):
        queries, keys, values = heads[head, 0], heads[head, 1], heads[head, 2]
        dm = d_mixed_heads[head, 0]
        probs = head_probs(queries, keys, hide)
        d_probs = dot_nt(dm, values)
        d_scores = (probs * (d_probs - jnp.sum(d_probs * probs, axis=1, keepdims=True))).astype(BF)
        d_heads[head, 0] = (dot(d_scores, keys) * 0.125).astype(BF)
        d_heads[head, 1] = (dot_tn(d_scores, queries) * 0.125).astype(BF)
        d_heads[head, 2] = dot_tn(probs.astype(BF), dm).astype(BF)
        return carried

    lax.fori_loop(0, 2 * count, one, 0)
    total, saved = 0.0, []
    for block, (w, _) in enumerate(weights):
        d_packed = take_heads(d_heads, block * count, (block + 1) * count)
        total = total + dot(d_packed, w)
        saved.append(d_packed)
    return (total[:half], total[half:].astype(BF), saved[0], rows_of(columns_of(saved[1], mixed1), own))


def after_attention_back(native, ids, d_after, part, arrived, mid, gains, scores, values, denom, mask, normed, tails, assoc):
    d_after, small = d_after[: mid.shape[0]], d_after[mid.shape[0] :]
    d_rows, d_gain, d_shift = norm_back(mid, gains[1:2], part + wide(arrived))
    d_mid = d_after + d_rows
    d_bias = jnp.sum(d_after, axis=0, keepdims=True)
    small = small + place_row(d_gain, 1, 0) + place_row(d_shift, 4, 0) + place_row(d_bias, 6, 0)
    scale = 1.0 / denom[:, 0:1]
    d_numer = (d_mid * scale).astype(BF)
    d_denom = -jnp.sum(d_mid * dot(scores, values), axis=1, keepdims=True) * scale * scale
    d_scores = ((dot_nt(d_numer, values) + d_denom) * mask).astype(BF)
    feat_q = features(read_keys_of(normed, assoc), native).astype(BF)
    d_keys = features_back(written_keys_of(tails, assoc), dot_tn(d_scores, feat_q), native)
    d_values = dot_tn(scores, d_numer)
    cut, width = d_keys.shape[1] // 2, d_values.shape[1] // 4
    mine, others = ordered(
        ids[CORE],
        columns_of(d_keys[:, :cut], d_values[:, :width], d_values[:, 2 * width : 3 * width]),
        columns_of(d_keys[:, cut:], d_values[:, width : 2 * width], d_values[:, 3 * width :]),
    )
    return (rows_of(d_mid, small), d_scores, d_keys.astype(BF), mine, others.astype(BF))


def read_back(native, ids, d_scores, normed, tails, assoc, d_tail_keys, segs):
    feat_k = features(written_keys_of(tails, assoc), native).astype(BF)
    d_keys = features_back(read_keys_of(normed, assoc), dot(d_scores, feat_k), native).astype(BF)
    d_norm = dot(d_keys, assoc[: assoc.shape[0] // 2])
    product = columns_of(dot_tn(normed, d_keys), dot_tn(tails, d_tail_keys))
    keep, send = split_blocks(product, product.shape[0] // (4 * segs), ids[CORE])
    return (d_norm, keep.astype(BF), send.astype(BF))


def assoc_second(native, ids, keep, arrived, values, segs):
    total = wide(keep) + wide(arrived)
    keep, send = split_blocks(total, total.shape[0] // (2 * segs), ids[HALF])
    blank = jnp.zeros((values.shape[0], send.shape[1] - values.shape[1]), BF)
    return (keep.astype(BF), rows_of(send.astype(BF), columns_of(values, blank)))


def tail_back(native, ids, arrived, assoc, w_write, part, rest, out_bit):
    total = wide(arrived[:NMEM])
    for at in range(NMEM, arrived.shape[0], NMEM):
        total = total + wide(arrived[at : at + NMEM])
    cut = total.shape[1] // 3
    low = total.astype(BF)
    own, other = ordered(ids[HALF], low[:, cut : 2 * cut], low[:, 2 * cut :])
    size = assoc.shape[0] // 4
    used, _ = ordered(ids[CORE], assoc[2 * size : 3 * size], assoc[3 * size :])
    others = other_rows(ids[BIT + out_bit], part, rest)
    d_tail = dot(low[:, :cut], used) + dot(own, w_write) + dot(other, others)
    return (d_tail, own, other)


def layer_end_back(native, ids, d_mid, d_norm, d_tail, d_tail_core, x, gains):
    rows = d_norm.shape[0]
    d_mid, small = d_mid[:rows], d_mid[rows:]
    added = jnp.where(ids[CORE] == 1, d_tail + d_tail_core, 0.0)
    d_norm = rows_of(d_norm[: rows - NMEM], d_norm[rows - NMEM :] + added)
    d_rows, d_gain, d_shift = norm_back(x, gains[0:1], d_norm)
    d_x = d_mid + d_rows
    return (rows_of(d_x, small + place_row(d_gain, 0, 0) + place_row(d_shift, 3, 0)), d_x.astype(BF))


def feed_grads(
    native, ids, n_own, n_core, n_got, n_got_core, d_pre, d_pre_got, g_own, g_core, g_got, g_got_core, hidden, hidden_got, segs, orders
):
    fc = dot_tn(rows_of(n_own, n_core), d_pre) + dot_tn(rows_of(n_got, n_got_core), d_pre_got)
    proj = dot_tn(rows_of(g_own, g_core), hidden) + dot_tn(rows_of(g_got, g_got_core), hidden_got)
    sums = jnp.sum(wide(d_pre), axis=0, keepdims=True) + jnp.sum(wide(d_pre_got), axis=0, keepdims=True)
    cuts = []
    for order, product in zip(orders, (fc, proj) if len(orders) == 2 else (columns_of(fc, proj),)):
        for v in split_blocks(product, fc.shape[0] // segs, ids[BIT + order[0]], order[0]):
            cuts.append(v.astype(BF))
    return (*cuts, place_row(sums, ids[TP], 8))


def attention_grads(
    native, ids, n_own, n_core, n_got, n_got_core, d_packed, got, g_own, g_core, g_got, g_got_core, mixed, segs, order
):
    width = d_packed.shape[1]
    qkv = dot_tn(rows_of(n_own, n_core), d_packed) + dot_tn(rows_of(n_got, n_got_core), got[:, :width])
    out = dot_tn(rows_of(g_own, g_core), mixed) + dot_tn(rows_of(g_got, g_got_core), got[:, width:])
    sums = jnp.sum(wide(d_packed), axis=0, keepdims=True) + jnp.sum(wide(got[:, :width]), axis=0, keepdims=True)
    pieces = []
    for at in range(0, sums.shape[1], 3 * HD):
        pieces += [sums[:, at : at + HD], sums[:, at + 2 * HD : at + 3 * HD]]
    sums = columns_of(*pieces)
    blank = jnp.zeros_like(sums)
    row, _ = ordered(ids[CORE], columns_of(sums, blank), columns_of(blank, sums))
    keep, send = split_blocks(columns_of(qkv, out), qkv.shape[0] // segs, ids[BIT + order[0]], order[0])
    return (keep.astype(BF), send.astype(BF), place_row(row, ids[HALF], 12))


def memory_grads(native, ids, keep, arrived, tail, tail_got, d_own, segs, order):
    count = keep.shape[0]
    total = wide(keep) + wide(arrived[:count])
    write = dot_tn(tail, d_own) + dot_tn(tail_got, arrived[count:, : d_own.shape[1]])
    few, many = count // segs, write.shape[0] // segs
    blocks = []
    for s in range(segs):
        part = write[s * many : (s + 1) * many]
        folded = columns_of(*[part[i * few : (i + 1) * few] for i in range(4)])
        blocks.append(rows_of(total[s * few : (s + 1) * few], folded))
    keep, send = split_blocks(rows_of(*blocks), 2 * few, ids[BIT + order[0]], order[0])
    return (keep.astype(BF), send.astype(BF))


def small_end(native, ids, first, second, few):
    total = first + second
    size = total.shape[1]
    at = lax.axis_index("seg") * 4 + lax.axis_index("tp")

    def own(rows, width, count):
        start = at * width
        row = start // size
        chosen = rows[0:1]
        for i in range(1, count):
            chosen = jnp.where(row == i, rows[i : i + 1], chosen)
        return pltpu.roll(jnp.broadcast_to(chosen, (8, size)), size - start % size, 1)[0:1, :width]

    mine = pltpu.roll(total, size - at * few, 1)[:, :few]
    layers = [mine[16 * l : 16 * (l + 1)] for l in range(LAYERS)]
    return (
        mine[16 * LAYERS :],
        jnp.stack([rows_of(*[m[i : i + 1] for m in layers]) for i in range(3)]),
        jnp.stack([rows_of(*[m[3 + i : 4 + i] for m in layers]) for i in range(3)]),
        jnp.stack([m[6:8] for m in layers]),
        rows_of(*[own(total[16 * l + 12 : 16 * l + 14], 2 * few, 2) for l in range(LAYERS)]),
        rows_of(*[own(total[16 * l + 8 : 16 * l + 12], 4 * few, 4) for l in range(LAYERS)]),
    )


def next_cut(native, ids, keep, arrived, bit, place, rows):
    total = wide(keep) + wide(arrived)
    keep, send = split_blocks(total, rows, ids[BIT + bit], place)
    return (keep.astype(BF), send.astype(BF))


def both_layers(first_keep, first_got, second_keep, second_got):
    return jnp.stack([wide(first_keep) + wide(first_got), wide(second_keep) + wide(second_got)])


def feed_end(native, ids, fc_keep, fc_got, proj_keep, proj_got, both_keep, both_got):
    width = fc_keep.shape[1]
    both = wide(both_keep) + wide(both_got)
    fc, proj = wide(fc_keep) + wide(fc_got), wide(proj_keep) + wide(proj_got)
    return (jnp.stack([fc, both[:, :width]]), jnp.stack([proj, both[:, width:]]))


def attention_end(native, ids, *pairs, columns):
    total = both_layers(*pairs)
    return (total[:, :, :columns], total[:, :, columns:])


def memory_end(native, ids, *pairs):
    total = both_layers(*pairs)
    few = total.shape[1] // 2
    width = total.shape[2] // 4
    folded = total[:, few:]
    return (total[:, :few], jnp.concatenate([folded[:, :, i * width : (i + 1) * width] for i in range(4)], axis=1))


def pack_rows(*refs, count):
    weights, packed, at = refs[1 : 1 + count], refs[-1], 0
    for w in weights:
        packed[at : at + w.shape[0]] = w[...]
        at += w.shape[0]


def pack(ids, layer, weights, front=(), after=()):
    halves = [w.shape[1] // 2 for w, _ in weights]
    rows = sum(f.shape[0] for f in front) + sum(halves)
    packed = pl.pallas_call(
        functools.partial(pack_rows, count=len(front) + len(weights)),
        grid_spec=pltpu.PrefetchScalarGridSpec(
            num_scalar_prefetch=1,
            grid=(1,),
            in_specs=[pl.BlockSpec(f.shape, lambda i, ids: (0, 0)) for f in front]
            + [
                pl.BlockSpec((None, n, w.shape[2]), functools.partial(lambda b, i, ids: (layer, ids[BIT + b], 0), bit))
                for n, (w, bit) in zip(halves, weights)
            ]
            + [pl.BlockSpec(memory_space=pl.ANY) for _ in after],
            out_specs=pl.BlockSpec((rows, D), lambda i, ids: (0, 0)),
        ),
        out_shape=pltpu.HBM((rows, D), BF),
        compiler_params=pltpu.CompilerParams(vmem_limit_bytes=VMEM_BYTES),
        name="pack_rows",
    )(ids, *front, *[pltpu.with_memory_space_constraint(w, pltpu.HBM) for w, _ in weights], *map(settled, after))
    return lives_in_hbm(packed)


def relay(x, *after):
    anywhere = pl.BlockSpec(memory_space=pl.ANY)
    result = pl.pallas_call(
        lambda *refs: None,
        in_specs=[anywhere] * (1 + len(after)),
        out_specs=anywhere,
        out_shape=jax.ShapeDtypeStruct(x.shape, x.dtype),
        input_output_aliases={0: 0},
        name="relay",
    )(settled(x), *map(settled, after))
    return lives_in_hbm(result) if any(x is known for known in IN_HBM) else result


def toward(x, axis, bit):
    size = lax.axis_size(axis)
    moved = lax.ppermute(x, axis, [(i, i ^ bit) for i in range(size)])
    return moved if (axis, bit) == ("tp", 1) else lives_in_hbm(moved)


def core_swap(x):
    return toward(x, "tp", 1)


def half_swap(x):
    return toward(x, "tp", 2)


def gather_segments(x):
    size = lax.axis_size("seg")
    spread = jnp.broadcast_to(x, (size,) + x.shape)
    return lax.all_to_all(spread, "seg", 0, 0, tiled=True).reshape(-1, x.shape[1])


def sum_over_all(x, gates):
    steps = [("tp", 1), ("tp", 2)] + [("seg", 1 << b) for b in range(lax.axis_size("seg").bit_length() - 1)]
    for i, (axis, bit) in enumerate(steps):
        arrived = toward(x, axis, bit)
        if i + 1 == len(steps):
            return x, arrived
        x = x + (relay(arrived, gates[i]) if i < len(gates) else arrived)


def local(
    tokens,
    mem_tokens,
    segno,
    gains,
    shifts,
    assoc,
    w_write,
    w_qkv,
    b_query_value,
    w_out,
    out_bias,
    w_fc,
    b_fc,
    w_proj,
    cot_tokens,
    cot_memory,
):
    IN_HBM.clear()
    mem_rows = mem_tokens.shape[0]
    block_rows = mem_rows + tokens.shape[2]
    own_rows = 2 * block_rows
    all_rows = 2 * own_rows
    segs = lax.axis_size("seg")
    levels = segs.bit_length() - 1
    me = lax.axis_index("seg")
    tp = lax.axis_index("tp")
    half, core = tp // 2, tp % 2
    slots = segs * NMEM
    key_dim = assoc.shape[1] // 2
    heads = w_qkv.shape[2] // (3 * HD)
    units = w_fc.shape[2]
    columns = w_write.shape[2]
    phi = 6 * key_dim
    wide_blocks = (D // segs) % 16 == 0 and (D // (4 * segs)) % 8 == 0
    ids = jnp.stack([me & 1, half, core, tp] + [(me >> level) & 1 for level in range(levels)]).astype(jnp.int32)

    def pick(pair, which):
        return lax.dynamic_index_in_dim(pair, which, 0, keepdims=False)

    both = jnp.concatenate([jnp.broadcast_to(mem_tokens, (2,) + mem_tokens.shape), tokens[:, 0]], axis=1)
    cots = jnp.concatenate([cot_memory[:, 0], cot_tokens[:, 0]], axis=1)
    bias_rows = jnp.concatenate([b_fc, b_query_value.reshape(1, -1), jnp.zeros((16 - LAYERS - 1, D), BF)])
    qkv_rows, write_rows = jnp.swapaxes(w_qkv, 1, 2), jnp.swapaxes(w_write, 1, 2)

    attention_weights_of = ((qkv_rows, 0), (write_rows, 1), (w_out, 1))
    few, q_rows = columns // 2, qkv_rows.shape[1] // 2
    first_got = half_swap(jnp.concatenate([pick(both, 1 - half), bias_rows]))
    biases = (first_got, 16, block_rows // 16)

    def run(body, outs, *items, **more):
        return phase(body, outs, ids, *items, **more)

    def fetch(packed, bit):
        part = half_swap(packed)
        return part, toward(part, "seg", 1 << bit)

    def places(core_id):
        within = jnp.arange(block_rows)
        rows = []
        for block in (core_id, core_id + 2):
            rows.append(
                jnp.where(
                    within < mem_rows,
                    block * mem_rows + within,
                    4 * mem_rows + block * (block_rows - mem_rows) + within - mem_rows,
                )
            )
        return jnp.concatenate(rows)

    pos = jnp.concatenate([places(core), places(1 - core)]).astype(jnp.int32)
    hide = jnp.where(pos[:, None] >= pos[None, :], 0.0, -1e30).astype(F32)
    number = lax.dynamic_index_in_dim(segno[:, 0], half, 0, keepdims=False)
    segment_of = jnp.arange(slots) // NMEM
    mask = jnp.broadcast_to(
        ((segment_of < me) & (segment_of >= me - number)).astype(F32)[None, :], (own_rows, slots)
    )
    own_f32, own_low = ((own_rows, D), F32), ((own_rows, D), BF)
    tail_low = ((NMEM, D), BF)
    small_rows = ((16, D), F32)
    more_f32 = ((own_rows + 16, D), F32)

    saved = []
    x, normed, tail = run(
        functools.partial(first_rows, sizes=()),
        [own_f32, own_low, tail_low],
        pick(both, half),
        first_got,
        (gains, 0),
        (shifts, 0),
    )
    packs = pack(ids, 0, attention_weights_of[:1]), pack(ids, 0, attention_weights_of[1:])
    (q_part, q_rest), (o_part, o_rest) = fetch(packs[0], 0), fetch(packs[1], 1)
    fetched = dict(
        qkv=(q_part, q_rest), write=((o_part, few, 0), (o_rest, few, 0)), out=((o_part, few, 1), (o_rest, few, 1))
    )
    feed_packs = pack(ids, 0, ((w_fc, 0),), after=(x,)), pack(ids, 0, ((w_proj, 1),), after=(x,))
    fetched["fc"], fetched["proj"] = fetch(feed_packs[0], 0), fetch(feed_packs[1], 1)
    tail = relay(tail, *packs, *feed_packs)
    for l in range(LAYERS):
        out_bit = 1 - l
        if l:
            tail = relay(tail, fetched["fc"][0])
        tail = jnp.where(core == 1, tail, core_swap(tail))
        tails = gather_segments(tail)
        scores, denom, values = run(
            functools.partial(write_scores, out_bit=out_bit),
            [((own_rows, slots), BF), ((own_rows, slots), F32), ((slots, 2 * columns), BF)],
            normed,
            tails,
            Far((assoc, l)),
            mask,
            Far((write_rows, l)),
            *far(*fetched["write"]),
            after=(fetched["proj"][0],) if l else (q_part,),
        )
        mid, normed1, values = run(
            read_memory,
            [own_f32, own_low, ((slots, D), BF)],
            x,
            scores,
            values,
            core_swap(values),
            denom,
            (gains, l),
            (shifts, l),
        )
        normed1_core = core_swap(normed1)
        if l == 0:
            pack_next = pack(ids, 1, [(w, 0) for w, _ in attention_weights_of], after=(normed1,))
            next_attention = fetch(pack_next, 0)
        part, sent, packed0, packed1, mixed0, mixed1 = run(
            functools.partial(attention, layer=l, out_bit=out_bit),
            [own_f32, own_low]
            + [((all_rows, 3 * HD * heads), BF)] * 2
            + [((all_rows, HD * heads), BF, True)] * 2,
            normed1,
            normed1_core,
            *far((qkv_rows, l), (w_out, l), *fetched["qkv"], *fetched["out"]),
            b_query_value[l : l + 1],
            biases,
            hide,
            scratch=[((2 * heads, 3, all_rows, HD), BF), ((2 * heads, 1, all_rows, HD), BF)],
            after=() if l else (fetched["fc"][0], pack_next),
        )
        after, normed2 = run(
            after_attention,
            [own_f32, own_low],
            mid,
            part,
            core_swap(sent),
            (out_bias, l),
            (gains, l),
            (shifts, l),
        )
        normed2_core = core_swap(normed2)
        if l == 0:
            packs = pack(ids, 1, ((w_fc, 0),), after=(normed2,)), pack(ids, 1, ((w_proj, 1),), after=(normed2,))
            next_fc, next_proj = fetch(packs[0], 0), fetch(packs[1], 1)
        part, sent, hidden, slope0, slope1, acts = run(
            functools.partial(feed_forward, layer=l),
            [own_f32, own_low]
            + [((all_rows, units), BF, True)] * 3
            + [((2 * all_rows + NMEM, D), BF, True)],
            normed2,
            normed2_core,
            *far((w_fc, l), (w_proj, l), *fetched["fc"], *fetched["proj"]),
            b_fc[l : l + 1],
            biases,
            normed1,
            tail,
            after=() if l else packs,
        )
        saved.append(
            dict(
                x=x, normed=normed, tail=tail, tails=tails, scores=scores, denom=denom, values=values, mid=mid,
                normed1=(normed1, normed1_core), packed=(packed0, packed1), mixed=(mixed0, mixed1), after=after,
                normed2=(normed2, normed2_core), hidden=hidden, slope=(slope0, slope1), acts=acts, fetched=fetched,
            )
        )
        if l == 0:
            x, normed, tail = run(
                after_feed,
                [own_f32, own_low, tail_low],
                after,
                part,
                core_swap(sent),
                (out_bias, l),
                (gains, l + 1),
                (shifts, l + 1),
                after=(next_attention[0],),
            )
            place = q_rows // few
            fetched = dict(
                qkv=[(m, q_rows, 0) for m in next_attention],
                write=[(m, few, place) for m in next_attention],
                out=[(m, few, place + 1) for m in next_attention],
                fc=next_fc,
                proj=next_proj,
            )
        else:
            mine, given = run(
                after_last, [((block_rows, D), BF, True)] * 2, after, part, core_swap(sent), (out_bias, l)
            )

    def both_batches(mine, got):
        return jnp.where(half == 0, jnp.stack([mine, got]), jnp.stack([got, mine]))

    result = both_batches(mine, half_swap(given))
    out_memory = result[:, :mem_rows][:, None]
    out_tokens = result[:, mem_rows:][:, None]

    cot_own, cot_got = pick(cots, half), half_swap(pick(cots, 1 - half))
    grad_low = jnp.where(half == 0, jnp.concatenate([cot_own, cot_got]), jnp.concatenate([cot_got, cot_own]))
    grad = grad_low
    cut_rows = D * (segs // 2) // segs
    early = [None] * LAYERS

    block, folded = D // segs, D // (2 * segs)

    def arrival(level, pair, order):
        bits = list(order) + list(range(2, levels))
        return toward(pair[1], "seg", 1 << bits[level - 1])

    def cut(level, pair, order, rows, after=(), got=None):
        bits = list(order) + list(range(2, levels))
        left = [b for b in range(levels) if b not in bits[:level]]
        keep, send = pair
        got = arrival(level, pair, order) if got is None else got
        return run(
            functools.partial(next_cut, bit=bits[level], place=left.index(bits[level]), rows=rows),
            [((keep.shape[0] // 2, keep.shape[1]), BF)] * 2,
            *[Far(v) if any(v is known for known in IN_HBM) else v for v in (keep, got)],
            kernel=wide_blocks,
            after=after,
        )

    def end_of(level, pair, order, rows, after=()):
        while level < levels:
            pair = cut(level, pair, order, rows, after)
            level += 1
        bits = list(order) + list(range(2, levels))
        return pair[0], toward(pair[1], "seg", 1 << bits[-1])

    def feed_gradients(l, s, d_pre, sent_got, rows, after):
        orders = FEED_ORDERS[l]
        shapes = [((cut_rows, D), BF, True)] * 4 if len(orders) == 2 else [((cut_rows, D + units), BF, True)] * 2
        got, got_core = s["acts"]
        return run(
            functools.partial(feed_grads, segs=segs, orders=orders),
            shapes + [small_rows],
            *far(*s["normed2"], (got, own_rows, 3), (got_core, own_rows, 3)),
            *far(d_pre, (sent_got[0], all_rows, 0)),
            *far(*rows, (sent_got[0], own_rows, 2), (sent_got[1], own_rows, 2)),
            *far(s["hidden"], (got, all_rows, 0)),
            kernel=wide_blocks,
            after=after,
        )

    def attention_gradients(l, s, d_packed, sent_got, rows, after):
        got, got_core = s["acts"]
        return run(
            functools.partial(attention_grads, segs=segs, order=ATT_ORDERS[l]),
            [((cut_rows, 3 * HD * heads + HD * heads), BF, True)] * 2 + [small_rows],
            *far(*s["normed1"], (got, own_rows, 2), (got_core, own_rows, 2)),
            *far(d_packed, (sent_got[0], all_rows, 0)),
            *far(*rows, (sent_got[0], own_rows, 2), (sent_got[1], own_rows, 2)),
            Far(s["mixed"][0]),
            kernel=wide_blocks,
            after=after,
        )

    def memory_gradients(l, s, assoc_keep, assoc_got, vals_own, after):
        return run(
            functools.partial(memory_grads, segs=segs, order=MEM_ORDERS[l]),
            [((cut_rows // 2, D), BF, True)] * 2,
            *far(assoc_keep, assoc_got, s["tail"], (s["acts"][0], NMEM, 2 * all_rows // NMEM), vals_own),
            kernel=wide_blocks,
            after=after,
        )

    def with_core(sent, *gate):
        got = relay(half_swap(sent), *gate)
        return got, core_swap(got)

    for s in saved:
        s["acts"] = with_core(s["acts"], s["normed2"][0])

    waiting = None
    pins = (mine, saved[0]["acts"][0])
    for l in reversed(range(LAYERS)):
        s, out_bit = saved[l], 1 - l
        grad_core = core_swap(grad_low)
        feed_rows = (grad_low, grad_core)
        part, sent, d_pre, feed_sent = run(
            feed_back,
            [own_f32, own_low, ((all_rows, units), BF), ((all_rows + own_rows, D), BF, True)],
            grad_low,
            grad_core,
            *far((w_fc, l), (w_proj, l), *s["fetched"]["fc"], *s["fetched"]["proj"], *s["slope"]),
            after=pins,
        )
        pins = ()
        if waiting:
            *feed_pair, small_f = feed_gradients(1, *waiting["feed"], (sent,))
            early[1] = early[1] + small_f
            pins = (feed_pair[0],)
        d_after, d_after_low = run(
            after_feed_back,
            [more_f32, own_low],
            grad,
            part,
            core_swap(sent),
            s["after"],
            (gains, l),
            after=pins,
        )
        d_after_core = core_swap(d_after_low)
        attention_rows = (d_after_low, d_after_core)
        pins = ()
        if waiting:
            later, later_packed, later_sent, later_rows = waiting["attention"]
            later_got = with_core(later_sent, feed_pair[0])
            *att_pair, small_g = attention_gradients(1, later, later_packed, later_got, later_rows, (d_after_low,))
            early[1] = early[1] + small_g
            pins = (att_pair[0],)
            later_feed = feed_pair
        part, sent, d_packed, attention_sent = run(
            functools.partial(attention_back, out_bit=out_bit),
            [own_f32, own_low, ((all_rows, 3 * HD * heads), BF), ((all_rows + own_rows, D), BF, True)],
            d_after_low,
            d_after_core,
            *far((qkv_rows, l), (w_out, l), *s["fetched"]["qkv"], *s["fetched"]["out"]),
            *far(*s["packed"], s["mixed"][1]),
            hide,
            after=pins,
            scratch=[
                ((2 * heads, 3, all_rows, HD), BF),
                ((2 * heads, 1, all_rows, HD), BF),
                ((2 * heads, 3, all_rows, HD), BF),
            ],
        )
        if waiting:
            feed_got = with_core(feed_sent, d_after_low)
            pins = (feed_got[0],)
        else:
            pins = (s["acts"][0],)
        d_mid, d_scores, d_keys, y_mine, y_sent = run(
            after_attention_back,
            [
                more_f32,
                ((own_rows, slots), BF),
                ((slots, key_dim), BF),
                ((slots, key_dim // 2 + 2 * columns), F32),
                ((slots, key_dim // 2 + 2 * columns), BF),
            ],
            d_after,
            part,
            core_swap(sent),
            *far(s["mid"], (gains, l), s["scores"], s["values"], s["denom"], mask, s["normed"], s["tails"], (assoc, l)),
            after=pins,
        )
        written = (y_mine + wide(core_swap(y_sent))).astype(BF)
        written_all = lax.all_to_all(written.reshape(segs, NMEM, -1), "seg", 0, 0, tiled=True).reshape(slots, -1)
        d_norm, assoc_keep, assoc_send = run(
            functools.partial(read_back, segs=segs),
            [own_f32, ((D // 2, 2 * key_dim), BF), ((D // 2, 2 * key_dim), BF)],
            d_scores,
            *far(s["normed"], s["tails"], (assoc, l)),
            d_keys,
            kernel=wide_blocks,
            after=(written,),
        )
        pins = (d_norm,)
        if l == 0:
            att_next = cut(1, att_pair, ATT_ORDERS[1], block, (d_norm,))
            feed_next = cut(1, later_feed, FEED_ORDERS[1][0], block, (att_next[0],))
            attention_got = with_core(attention_sent, d_mid)
            att_got = arrival(2, att_next, ATT_ORDERS[1])
            feed_got_next = arrival(2, feed_next, FEED_ORDERS[1][0])
            *feed_pair, small_f = feed_gradients(0, s, d_pre, feed_got, feed_rows, (feed_next[0],))
            pins = (feed_pair[0],)
        d_tail, vals_own, vals_other = run(
            functools.partial(tail_back, out_bit=out_bit),
            [((NMEM, D), F32)] + [((NMEM, columns), BF)] * 2,
            written_all,
            *far((assoc, l), (write_rows, l), *s["fetched"]["write"]),
            after=pins,
        )
        assoc_keep, assoc_send = run(
            functools.partial(assoc_second, segs=segs),
            [((D // 4, 2 * key_dim), BF, True), ((D // 4 + NMEM, 2 * key_dim), BF, True)],
            assoc_keep,
            core_swap(assoc_send),
            vals_other,
            kernel=wide_blocks,
        )
        if l == 0:
            mem_later = memory_gradients(1, *waiting["memory"], (d_tail,))
            mem_later_got = arrival(1, mem_later, MEM_ORDERS[1])
        d_x, d_x_low = run(
            layer_end_back,
            [more_f32, own_low],
            *far(d_mid, d_norm),
            d_tail,
            core_swap(d_tail),
            *far(s["x"], (gains, l)),
            after=(assoc_keep,) if l else (assoc_keep, mem_later[0], att_got),
        )
        early[l] = d_x[own_rows:]
        memory = (s, assoc_keep, half_swap(assoc_send), vals_own)
        pins = ()
        if l > 0:
            waiting = dict(
                feed=(s, d_pre, with_core(feed_sent, d_x), feed_rows),
                attention=(s, d_packed, attention_sent, attention_rows),
                memory=memory,
            )
        else:
            feed_next = cut(2, feed_next, FEED_ORDERS[1][0], block, (d_x,), feed_got_next)
            att_next = cut(2, att_next, ATT_ORDERS[1], block, (feed_next[0],), att_got)
            *att_pair, small_g = attention_gradients(
                0, s, d_packed, attention_got, attention_rows, (att_next[0], mem_later_got)
            )
            early[0] = early[0] + small_f + small_g
            fc_got = arrival(1, feed_pair[:2], FEED_ORDERS[0][0])
            proj_got = arrival(1, feed_pair[2:], FEED_ORDERS[0][1])
            later_sums = [end_of(3, feed_next, FEED_ORDERS[1][0], block), end_of(3, att_next, ATT_ORDERS[1], block)]
            fc = cut(1, feed_pair[:2], FEED_ORDERS[0][0], block, (att_pair[0],), fc_got)
            mem_pair = memory_gradients(0, *memory, (fc[0],))
            proj = cut(1, feed_pair[2:], FEED_ORDERS[0][1], block, (mem_pair[0], later_sums[0][1]), proj_got)
        grad, grad_low = d_x, d_x_low

    fc_order, proj_order = FEED_ORDERS[0]
    fc = cut(2, fc, fc_order, block, (proj[0], later_sums[1][1]))
    gates = [mem_pair[0], fc[0]]
    proj = cut(2, proj, proj_order, block, (fc[0],))
    mem_next = cut(1, mem_later, MEM_ORDERS[1], folded, (proj[0],), mem_later_got)
    att_pair = cut(1, att_pair, ATT_ORDERS[0], block, (mem_next[0],))
    gates.append(att_pair[0])
    fc, proj = end_of(3, fc, fc_order, block), end_of(3, proj, proj_order, block)
    mem_pair = cut(1, mem_pair, MEM_ORDERS[0], folded, (att_pair[0],))
    gates.append(mem_pair[0])
    mem_next = cut(2, mem_next, MEM_ORDERS[1], folded, (mem_pair[0],))
    att_pair = cut(2, att_pair, ATT_ORDERS[0], block, (mem_next[0], fc[1]))
    mem_pair = cut(2, mem_pair, MEM_ORDERS[0], folded, (att_pair[0],))
    later_sums.append(end_of(3, mem_next, MEM_ORDERS[1], folded))
    last_sums = [fc, proj, end_of(3, att_pair, ATT_ORDERS[0], block), end_of(3, mem_pair, MEM_ORDERS[0], folded)]

    grad = grad[:own_rows]
    mine = pick(grad.reshape(2, block_rows, D), half)
    given = half_swap(pick(grad_low.reshape(2, block_rows, D), 1 - half))
    grad_tokens = both_batches(mine, wide(given))[:, mem_rows:][:, None]

    kept = grad.reshape(2, block_rows, D)[:, :mem_rows]
    mem_full = lax.dynamic_update_slice(jnp.zeros((2, 2, mem_rows, D), F32), kept[:, None], (0, core, 0, 0))
    smalls = sum_over_all(jnp.concatenate(early + [mem_full.reshape(-1, D)]), gates)

    few, many = D // (4 * segs), D // segs
    g_mem, g_gains, g_shifts, g_bias, g_qv, g_bfc = run(
        functools.partial(small_end, few=few),
        [
            ((4 * mem_rows, few), F32),
            ((3, LAYERS, few), F32),
            ((3, LAYERS, few), F32),
            ((LAYERS, 2, few), F32),
            ((LAYERS, 2 * few), F32),
            ((LAYERS, 4 * few), F32),
        ],
        *smalls,
    )
    qkv_columns = 3 * HD * heads
    g_fc, g_proj = run(
        feed_end,
        [((LAYERS, many, units), F32), ((LAYERS, many, units), F32)],
        *last_sums[0],
        *last_sums[1],
        *later_sums[0],
        kernel=wide_blocks,
    )
    g_qkv, g_out = run(
        functools.partial(attention_end, columns=qkv_columns),
        [((LAYERS, many, qkv_columns), F32), ((LAYERS, many, columns), F32)],
        *last_sums[2],
        *later_sums[1],
        kernel=wide_blocks,
    )
    g_assoc, g_write = run(
        memory_end,
        [((LAYERS, few, D), F32), ((LAYERS, many, columns), F32)],
        *last_sums[3],
        *later_sums[2],
        kernel=wide_blocks,
    )
    return (
        out_tokens,
        out_memory,
        grad_tokens,
        g_mem,
        jnp.swapaxes(g_gains, 0, 1),
        jnp.swapaxes(g_shifts, 0, 1),
        jnp.swapaxes(g_assoc, 1, 2),
        g_write,
        g_qkv,
        g_qv,
        jnp.swapaxes(g_out, 1, 2),
        g_bias,
        g_fc,
        g_bfc,
        jnp.swapaxes(g_proj, 1, 2),
    )


def solution(mesh):
    return jax.shard_map(
        local,
        mesh=mesh,
        in_specs=(
            P(None, "seg", "tp", None),
            P("tp", None),
            P(None, "seg"),
            P(),
            P(),
            P(),
            P(None, None, "tp"),
            P(None, None, "tp"),
            P(None, "tp"),
            P(None, "tp", None),
            P(),
            P(None, None, "tp"),
            P(None, "tp"),
            P(None, "tp", None),
            P(None, "seg", "tp", None),
            P(None, "seg", "tp", None),
        ),
        out_specs=(
            P(None, "seg", "tp", None),
            P(None, "seg", "tp", None),
            P(None, "seg", "tp", None),
            P(None, ("seg", "tp")),
            P(None, None, ("seg", "tp")),
            P(None, None, ("seg", "tp")),
            P(None, None, ("seg", "tp")),
            P(None, "seg", "tp"),
            P(None, "seg", "tp"),
            P(None, ("seg", "tp")),
            P(None, "tp", "seg"),
            P(None, None, ("seg", "tp")),
            P(None, "seg", "tp"),
            P(None, ("seg", "tp")),
            P(None, "tp", "seg"),
        ),
        check_vma=False,
    )
```
